256 devices in a mesh: dp: 32 (over z, y), mp: 8 (over x, core).
Axes of the slice: x: 4, y: 4, z: 8, core: 2. Of those that a mesh axis runs over, the one named last changes fastest.
Arguments:
- tokens: bfloat16 [16384, 2304], P('dp'), may hold values from -120 to 120
- grad_out: bfloat16 [16384, 18432], P('dp', 'mp'), may hold values from -120 to 120
- next_tokens: bfloat16 [16384, 2304], P('dp'), may hold values from -6 to 6
- master: float32 [2304, 18432], P('dp', 'mp'), may hold values from -0.125 to 0.125
- momentum: float32 [2304, 18432], P('dp', 'mp'), may hold values from -6 to 6
Outputs:
- new_master: float32 [2304, 18432], P('dp', 'mp')
- new_momentum: float32 [2304, 18432], P('dp', 'mp')
- next_out: bfloat16 [16384, 18432], P('dp', 'mp')
- row_checks: float32 [8, 2304], P('mp', 'dp')
The draws below stay inside these ranges and needn't reach their ends.
All inputs are finite; a program needn't handle non-finite values.
Results may differ from the reference program's by a relative error of at most 0.0049.
Values may be sent and summed in bfloat16 or wider, within the bound.
No kernel may reach another device: no remote copies, remote signals or barrier semaphores. Data moves between devices by JAX's collectives and lax.ppermute only.
A program may use at most 128 MiB of HBM per device.

```python
import jax
import jax.numpy as jnp
from jax import lax

D = 2304
FF = 18432
FD = 2304
TOKENS = 16384
N_MP = 8


def token_signs(key):
    return jax.random.rademacher(jax.random.fold_in(key, 71), (TOKENS,), jnp.float32)


def column_scales(key, columns):
    spread = jax.random.uniform(key, (columns,), jnp.float32)
    position = jnp.arange(columns, dtype=jnp.float32) / columns
    return 10.0 ** spread * 3.0 ** position


def scaled_field(key, rows, columns, signs):
    first = jax.random.fold_in(key, 0)
    second = jax.random.fold_in(key, 1)
    fourth = jax.random.fold_in(key, 3)
    scales = column_scales(first, columns)
    pattern = jax.random.rademacher(fourth, (columns,), jnp.float32)
    base = jnp.clip(jax.random.normal(second, (rows, columns), jnp.float32), -3.7, 3.7)
    base = base + 0.3 * signs[:, None] * pattern[None, :]
    return (base * scales).astype(jnp.bfloat16)


def draw_tokens(key, part):
    signs = token_signs(key)
    key = jax.random.fold_in(key, 11)
    return scaled_field(key, TOKENS, D, signs)


def draw_grad_out(key, part):
    signs = token_signs(key)
    key = jax.random.fold_in(key, 23)
    return scaled_field(key, TOKENS, FF, signs)


def steps_of(own_key, extent, pieces, smallest, top_value):
    level = 1.0
    for dim, shards_of in pieces:
        heights = jax.random.uniform(jax.random.fold_in(jax.random.fold_in(own_key, 6), dim), (shards_of,), jnp.float32, smallest / len(pieces), top_value / len(pieces))
        level = level * jnp.repeat(jnp.exp(heights), extent[dim] // shards_of).reshape((-1,) + (1,) * (len(extent) - 1 - dim))
    return level


def gaussian(key, shape, deviation, most, cuts=(), kind=jnp.bfloat16):
    values = jax.random.normal(key, shape, jnp.float32) * deviation
    if len(cuts) > 0:
        values = steps_of(key, shape, cuts, -0.22, 0.18) * values
    return jnp.clip(values, min=-most, max=most).astype(kind)


def setup_inputs(seed: int = 0) -> dict:
    keys = jax.random.split(jax.random.key(seed), 6)
    return {
        "tokens": draw_tokens(jax.random.fold_in(keys[5], 71), 0),
        "grad_out": draw_grad_out(jax.random.fold_in(keys[5], 71), 0),
        "next_tokens": gaussian(keys[2], (TOKENS, D), 1.0, 6.0, ((0, 32),)),
        "master": gaussian(keys[3], (D, FF), D ** -0.5, 0.125, ((0, 32), (1, 8)), jnp.float32),
        "momentum": gaussian(keys[4], (D, FF), 1.0, 6.0, ((0, 32), (1, 8)), jnp.float32),
    }


def reference(tokens, grad_out, next_tokens, master, momentum):
    grad = jnp.dot(tokens.T, grad_out, preferred_element_type=jnp.float32)
    row_sum = lax.optimization_barrier(jnp.sum(grad.reshape(D, N_MP, FD), axis=2)).T
    mean_square = jnp.sum(grad * grad) / (D * FF)
    clip_factor = jnp.minimum(1.0, 1.0 / jnp.sqrt(mean_square + 1e-06))
    row_checks = clip_factor * row_sum / float(FD) ** 0.5
    new_momentum = 0.9 * momentum + clip_factor * grad
    new_master = master - 0.01 * new_momentum
    weights_low = new_master.astype(jnp.bfloat16)
    next_out = jnp.dot(next_tokens, weights_low, preferred_element_type=jnp.float32).astype(jnp.bfloat16)
    return (new_master, new_momentum, next_out, row_checks)
```

```python
import jax
import jax.numpy as jnp
from jax import lax
from jax.experimental import pallas as pl
from jax.experimental.pallas import tpu as pltpu
from jax.sharding import Mesh, PartitionSpec as P

D = 2304
FF = 18432
NZ, NY, NX, NC = 8, 4, 4, 2
ROWS = D // (NZ * NY)
HALF = D // 2
CUT = 40
F32, BF16 = jnp.float32, jnp.bfloat16


def shift(value, axis, by):
    size = {"z": NZ, "y": NY, "x": NX, "c": NC}[axis]
    return lax.ppermute(value, axis, [(i, (i + by) % size) for i in range(size)])


def grad_kernel(tokens_ref, grad_ref, by_y_ref, by_z_ref, turned):
    step = pl.program_id(0)

    @pl.when(step == 0)
    def _():
        turned[...] = tokens_ref[...].T

    rows = 2 * NY * ROWS
    start = pl.multiple_of(step * rows, rows)
    part = jnp.dot(turned[pl.ds(start, rows), :], grad_ref[...], preferred_element_type=F32)
    part = part.astype(BF16).reshape(2, NY, ROWS, D)
    for i in range(2):
        for j in range(NY):
            by_y_ref[j, i] = part[i, j, :, :HALF]
            by_z_ref[i, j] = part[i, j, :, HALF:]


def partial_grad(tokens, grad_out):
    tokens_count = tokens.shape[0]
    whole = pl.BlockSpec((tokens_count, D), lambda i: (0, 0))
    return pl.pallas_call(
        grad_kernel,
        grid=(NZ // 2,),
        in_specs=[whole, whole],
        out_specs=[
            pl.BlockSpec((NY, 2, ROWS, HALF), lambda i: (0, i, 0, 0)),
            pl.BlockSpec((2, NY, ROWS, HALF), lambda i: (i, 0, 0, 0)),
        ],
        out_shape=[
            jax.ShapeDtypeStruct((NY, NZ, ROWS, HALF), BF16),
            jax.ShapeDtypeStruct((NZ, NY, ROWS, HALF), BF16),
        ],
        scratch_shapes=[pltpu.VMEM((D, tokens_count), BF16)],
        compiler_params=pltpu.CompilerParams(vmem_limit_bytes=48 * 1024 * 1024),
    )(tokens, grad_out)


def scatter_sum(chunks, axis, size, cut):
    me = lax.axis_index(axis)

    def chunk(k):
        return lax.dynamic_index_in_dim(chunks, (me + k) % size, 0, keepdims=False).astype(F32)

    far = chunk(size // 2).astype(BF16)
    up = shift(far[:cut], axis, 1)
    down = shift(far[cut:], axis, -1)
    for k in range(size // 2 - 1, 0, -1):
        if k == size // 2 - 1:
            above, below = chunk(k), chunk(-k)
            up = jnp.concatenate([above[:cut] + up.astype(F32), above[cut:]])
            down = jnp.concatenate([below[:cut], below[cut:] + down.astype(F32)])
        else:
            up = chunk(k) + up.astype(F32)
            down = chunk(-k) + down.astype(F32)
        up = shift(up.astype(BF16), axis, 1)
        down = shift(down.astype(BF16), axis, -1)
    return chunk(0) + up.astype(F32) + down.astype(F32)


def gather_rounds(own, axis, size, cut):
    rounds = [own]
    up = down = own
    for k in range(1, size // 2):
        up, down = shift(up, axis, 1), shift(down, axis, -1)
        rounds += [up, down]
    up, down = shift(up[:cut], axis, 1), shift(down[cut:], axis, -1)
    rounds.append(jnp.concatenate([up, down]))
    return rounds


def offsets(size):
    order = [0]
    for k in range(1, size // 2):
        order += [-k, k]
    return order + [size // 2]


def local(tokens, grad_out, next_tokens, master, momentum):
    z, y = lax.axis_index("z"), lax.axis_index("y")
    by_y, by_z = partial_grad(tokens, grad_out)
    token_sums = jnp.sum(grad_out.astype(F32), axis=1)
    row_total = jnp.dot(token_sums[None, :], tokens.astype(F32), precision=lax.Precision.HIGHEST)
    row_totals = lax.all_gather(row_total, ("z", "y"), axis=0, tiled=True)

    first = scatter_sum(by_y.reshape(NY, NZ * ROWS, HALF), "y", NY, NZ * ROWS // 2)
    second = scatter_sum(by_z.reshape(NZ, NY * ROWS, HALF), "z", NZ, NY * ROWS // 2)
    first = scatter_sum(first.reshape(NZ, ROWS, HALF), "z", NZ, CUT)
    second = scatter_sum(second.reshape(NY, ROWS, HALF), "y", NY, CUT)
    reduced = jnp.concatenate([first, second], axis=1)

    squares = jnp.sum(reduced * reduced)
    for axis in ("c", "x", "y", "z"):
        squares = lax.psum(squares, axis)
    mean_square = squares / (D * FF)
    clip_factor = jnp.minimum(1.0, 1.0 / jnp.sqrt(mean_square + 1e-06))
    new_momentum = 0.9 * momentum + clip_factor * reduced
    new_master = master - 0.01 * new_momentum
    weights_low = new_master.astype(BF16)

    row_sum = lax.dynamic_slice_in_dim(jnp.sum(row_totals, axis=0), (z * NY + y) * ROWS, ROWS)
    row_checks = (clip_factor * row_sum / float(D) ** 0.5)[None, :]

    turned = next_tokens.T.reshape(NZ, NY, ROWS, next_tokens.shape[0])
    z_order = (z + jnp.array(offsets(NZ))) % NZ
    y_order = (y + jnp.array(offsets(NY))) % NY
    turned = jnp.take(jnp.take(turned, z_order, axis=0), y_order, axis=1)

    def product(features, weights):
        return lax.dot_general(
            features.reshape(-1, features.shape[-1]), weights, (((0,), (0,)), ((), ())),
            preferred_element_type=F32,
        )

    one = gather_rounds(weights_low[:, :HALF], "z", NZ, CUT)
    two = gather_rounds(weights_low[:, HALF:], "y", NY, CUT)
    one = gather_rounds(jnp.concatenate(one), "y", NY, NZ * ROWS // 2)
    two = gather_rounds(jnp.concatenate(two), "z", NZ, NY * ROWS // 2)
    by_first = jnp.swapaxes(turned, 0, 1)
    out_one = product(by_first[0], one[0])
    out_one += product(by_first[1:3], jnp.concatenate(one[1:3]))
    out_one += product(by_first[3], one[3])
    out_two = product(turned[0], two[0])
    for k in range(1, NZ - 1, 2):
        out_two += product(turned[k : k + 2], jnp.concatenate(two[k : k + 2]))
    out_two += product(turned[NZ - 1], two[NZ - 1])
    forward = jnp.concatenate([out_one, out_two], axis=1).astype(BF16)
    return new_master, new_momentum, forward, row_checks


def solution(mesh):
    split = Mesh(mesh.devices.reshape(NZ, NY, NX, NC), ("z", "y", "x", "c"))
    dp, mp = ("z", "y"), ("x", "c")
    in_specs = (P(dp, None), P(dp, mp), P(dp, None), P(dp, mp), P(dp, mp))
    out_specs = (P(dp, mp), P(dp, mp), P(dp, mp), P(mp, dp))
    return jax.shard_map(local, mesh=split, in_specs=in_specs, out_specs=out_specs, check_vma=False)
```

```python
import jax
import jax.numpy as jnp
from jax import lax
from jax.experimental import pallas as pl
from jax.experimental.pallas import tpu as pltpu
from jax.sharding import Mesh, PartitionSpec as P

D = 2304
FF = 18432
NZ, NY, NX, NC = 8, 4, 4, 2
ROWS = D // (NZ * NY)
HALF = D // 2
WIDE = 1152
CUT = 40
F32, BF16 = jnp.float32, jnp.bfloat16


def shift(value, axis, by):
    size = {"z": NZ, "y": NY, "x": NX, "c": NC}[axis]
    return lax.ppermute(value, axis, [(i, (i + by) % size) for i in range(size)])


def grad_kernel(tokens_ref, grad_ref, by_y_ref, by_z_ref, turned):
    step = pl.program_id(0)

    @pl.when(step == 0)
    def _():
        turned[...] = tokens_ref[...].T

    rows = 2 * NY * ROWS
    start = pl.multiple_of(step * rows, rows)
    part = jnp.dot(turned[pl.ds(start, rows), :], grad_ref[...], preferred_element_type=F32)
    part = part.astype(BF16).reshape(2, NY, ROWS, D)
    for i in range(2):
        for j in range(NY):
            by_y_ref[j, i] = part[i, j, :, :HALF]
            by_z_ref[i, j] = part[i, j, :, HALF:]


def partial_grad(tokens, grad_out):
    tokens_count = tokens.shape[0]
    whole = pl.BlockSpec((tokens_count, D), lambda i: (0, 0))
    return pl.pallas_call(
        grad_kernel,
        grid=(NZ // 2,),
        in_specs=[whole, whole],
        out_specs=[
            pl.BlockSpec((NY, 2, ROWS, HALF), lambda i: (0, i, 0, 0)),
            pl.BlockSpec((2, NY, ROWS, HALF), lambda i: (i, 0, 0, 0)),
        ],
        out_shape=[
            jax.ShapeDtypeStruct((NY, NZ, ROWS, HALF), BF16),
            jax.ShapeDtypeStruct((NZ, NY, ROWS, HALF), BF16),
        ],
        scratch_shapes=[pltpu.VMEM((D, tokens_count), BF16)],
        compiler_params=pltpu.CompilerParams(vmem_limit_bytes=48 * 1024 * 1024),
    )(tokens, grad_out)


def scatter_sum(chunks, axis, size, cut):
    me = lax.axis_index(axis)

    def chunk(k):
        return lax.dynamic_index_in_dim(chunks, (me + k) % size, 0, keepdims=False).astype(F32)

    far = chunk(size // 2).astype(BF16)
    up, down = shift(far[:cut], axis, 1), shift(far[cut:], axis, -1)
    for k in range(size // 2 - 1, 0, -1):
        up, down = lax.optimization_barrier((up, down))
        above, below = chunk(k), chunk(-k)
        if k == size // 2 - 1:
            up = jnp.concatenate([above[:cut] + up.astype(F32), above[cut:]])
            down = jnp.concatenate([below[:cut], below[cut:] + down.astype(F32)])
        else:
            up, down = above + up.astype(F32), below + down.astype(F32)
        up, down = shift(up.astype(BF16), axis, 1), shift(down.astype(BF16), axis, -1)
    return chunk(0) + up.astype(F32) + down.astype(F32)


def offsets(size):
    order = [0]
    for k in range(1, size // 2):
        order += [-k, k]
    return order + [size // 2]


def local(tokens, grad_out, next_tokens, master, momentum):
    z, y = lax.axis_index("z"), lax.axis_index("y")
    by_y, by_z = partial_grad(tokens, grad_out)
    token_sums = jnp.sum(grad_out.astype(F32), axis=1)
    row_total = jnp.dot(token_sums[None, :], tokens.astype(F32), precision=lax.Precision.HIGHEST)

    first = scatter_sum(by_y.reshape(NY, NZ * ROWS, HALF), "y", NY, NZ * ROWS // 2)
    second = scatter_sum(by_z.reshape(NZ, NY * ROWS, HALF), "z", NZ, NY * ROWS // 2)
    first = scatter_sum(first.reshape(NZ, ROWS, HALF), "z", NZ, CUT)
    second = scatter_sum(second.reshape(NY, ROWS, HALF), "y", NY, CUT)
    reduced = jnp.concatenate([first, second], axis=1)

    kept = (master - 0.01 * (0.9 * momentum)).astype(BF16)
    both = jnp.stack([kept, reduced.astype(BF16)])
    one, two = both[:, :, :WIDE], both[:, :, WIDE:]
    squares = jnp.sum(reduced * reduced)

    up1, down1 = shift(one, "z", 1), shift(one, "z", -1)
    up2, down2 = shift(two, "y", 1), shift(two, "y", -1)
    squares = lax.psum(squares, "c")
    up1, down1, up2, down2, squares = lax.optimization_barrier((up1, down1, up2, down2, squares))
    ones, twos = [one, up1, down1], [two, up2, down2]

    up1, down1 = shift(up1, "z", 1), shift(down1, "z", -1)
    up2, down2 = shift(up2[0], "y", 1), shift(down2[1], "y", -1)
    squares = lax.psum(squares, "x")
    up1, down1, up2, down2, squares = lax.optimization_barrier((up1, down1, up2, down2, squares))
    ones += [up1, down1]
    twos = jnp.stack(twos + [jnp.stack([up2, down2])], axis=1).reshape(2, NY * ROWS, D - WIDE)

    up1, down1 = shift(up1, "z", 1), shift(down1, "z", -1)
    up2, down2 = shift(twos, "z", 1), shift(twos, "z", -1)
    sums = jnp.concatenate([row_total.reshape(-1, 128), jnp.full((1, 128), squares)])
    sums = lax.psum(sums, "y")
    up1, down1, sums = lax.optimization_barrier((up1, down1, sums))
    ones += [up1, down1]

    up1, down1 = shift(up1[0], "z", 1), shift(down1[1], "z", -1)
    sums = lax.psum(sums, "z")
    up1, down1, up2, down2, sums = lax.optimization_barrier((up1, down1, up2, down2, sums))
    ones.append(jnp.stack([up1, down1]))

    mean_square = sums[-1, 0] / (D * FF)
    clip_factor = jnp.minimum(1.0, 1.0 / jnp.sqrt(mean_square + 1e-06))
    new_momentum = 0.9 * momentum + clip_factor * reduced
    new_master = master - 0.01 * new_momentum
    row_sum = lax.dynamic_slice_in_dim(sums[:-1].reshape(-1), (z * NY + y) * ROWS, ROWS)
    row_checks = (clip_factor * row_sum / float(D) ** 0.5)[None, :]

    def weights(pair):
        return (pair[0].astype(F32) - (0.01 * clip_factor) * pair[1].astype(F32)).astype(BF16)

    next_tokens, _ = lax.optimization_barrier((next_tokens, clip_factor))
    turned = next_tokens.T.reshape(NZ, NY, ROWS, next_tokens.shape[0])
    z_order = (z + jnp.array(offsets(NZ))) % NZ
    y_order = (y + jnp.array(offsets(NY))) % NY
    turned = jnp.take(jnp.take(turned, z_order, axis=0), y_order, axis=1)

    def product(features, *blocks):
        return lax.dot_general(
            features.reshape(-1, features.shape[-1]), jnp.concatenate(blocks),
            (((0,), (0,)), ((), ())), preferred_element_type=F32,
        )

    one = jnp.concatenate([weights(pair) for pair in ones])
    two, up2, down2 = weights(twos), weights(up2), weights(down2)
    up1, down1 = shift(one, "y", 1), shift(one, "y", -1)
    by_first = jnp.swapaxes(turned, 0, 1)
    out_one = product(by_first[0], one)
    out_two = product(turned[0], two)
    for k in range(2, NZ // 2):
        out_two += product(turned[2 * k - 3 : 2 * k - 1], up2, down2)
        up2, down2 = lax.optimization_barrier((shift(up2, "z", 1), shift(down2, "z", -1)))
    out_two += product(turned[NZ - 3 : NZ - 1], up2, down2)
    cut = NY * ROWS // 2
    up2, down2 = shift(up2[:cut], "z", 1), shift(down2[cut:], "z", -1)
    up1, down1 = lax.optimization_barrier((up1, down1))
    out_one += product(by_first[1:3], up1, down1)
    cut = NZ * ROWS // 2
    up1, down1 = shift(up1[:cut], "y", 1), shift(down1[cut:], "y", -1)
    out_one += product(by_first[3], up1, down1)
    out_two += product(turned[NZ - 1], up2, down2)
    forward = jnp.concatenate([out_one, out_two], axis=1).astype(BF16)
    return new_master, new_momentum, forward, row_checks


def solution(mesh):
    split = Mesh(mesh.devices.reshape(NZ, NY, NX, NC), ("z", "y", "x", "c"))
    dp, mp = ("z", "y"), ("x", "c")
    in_specs = (P(dp, None), P(dp, mp), P(dp, None), P(dp, mp), P(dp, mp))
    out_specs = (P(dp, mp), P(dp, mp), P(dp, mp), P(mp, dp))
    return jax.shard_map(local, mesh=split, in_specs=in_specs, out_specs=out_specs, check_vma=False)
```

```python
import functools

import jax
import jax.numpy as jnp
from jax import lax
from jax.experimental import pallas as pl
from jax.experimental.pallas import tpu as pltpu
from jax.sharding import Mesh, PartitionSpec as P

D = 2304
FF = 18432
NZ, NY, NX, NC = 8, 4, 4, 2
SIZES = {"z": NZ, "y": NY, "x": NX, "c": NC}
ROWS = D // (NZ * NY)
YROWS, ZROWS = NZ * ROWS, NY * ROWS
HALF = D // 2
WIDE = D // 2
F32, BF16 = jnp.float32, jnp.bfloat16
LIMIT = pltpu.CompilerParams(vmem_limit_bytes=48 * 1024 * 1024)
HBM = pl.BlockSpec(memory_space=pl.ANY)
VMEM = pl.BlockSpec(memory_space=pltpu.VMEM)
SMEM = pl.BlockSpec(memory_space=pltpu.SMEM)


def shift(value, axis, by):
    size = SIZES[axis]
    return lax.ppermute(value, axis, [(i, (i + by) % size) for i in range(size)])


def far_kernel(tokens_hbm, grad_hbm, up_y, down_y, up_z, down_z, turned, tokens, grad, sems):
    first = pltpu.make_async_copy(tokens_hbm, tokens, sems.at[0])
    second = pltpu.make_async_copy(grad_hbm, grad, sems.at[1])
    first.start()
    second.start()
    first.wait()
    turned[...] = tokens[...].T
    second.wait()
    z = (lax.axis_index("z") + NZ // 2) % NZ
    y = (lax.axis_index("y") + NY // 2) % NY
    rows = turned[pl.ds(pl.multiple_of(z * ZROWS, ZROWS), ZROWS), :]
    part = jnp.dot(rows, grad[:, HALF:], preferred_element_type=F32).astype(BF16)
    up_z[...] = part[: ZROWS // 2]
    down_z[...] = part[ZROWS // 2 :]
    for j in range(NY):

        @pl.when(y == j)
        def _():
            starts = [i * ZROWS + j * ROWS for i in range(NZ)]
            rows = jnp.concatenate([turned[s : s + ROWS, :] for s in starts])
            part = jnp.dot(rows, grad[:, :HALF], preferred_element_type=F32).astype(BF16)
            up_y[...] = part[: YROWS // 2]
            down_y[...] = part[YROWS // 2 :]


def far_chunks(tokens, grad_out):
    count = tokens.shape[0]
    shapes = [(YROWS // 2, HALF)] * 2 + [(ZROWS // 2, D - HALF)] * 2 + [(D, count)]
    return pl.pallas_call(
        far_kernel,
        in_specs=[HBM, HBM],
        out_specs=[VMEM] * 5,
        out_shape=[jax.ShapeDtypeStruct(s, BF16) for s in shapes],
        scratch_shapes=[
            pltpu.VMEM(tokens.shape, BF16),
            pltpu.VMEM(grad_out.shape, BF16),
            pltpu.SemaphoreType.DMA((2,)),
        ],
        compiler_params=LIMIT,
    )(tokens, grad_out)


def grad_kernel(turned_ref, grad_ref, by_y_ref, by_z_ref):
    part = jnp.dot(turned_ref[...], grad_ref[...], preferred_element_type=F32)
    part = part.astype(BF16).reshape(2, NY, ROWS, D)
    for i in range(2):
        for j in range(NY):
            by_y_ref[j, i] = part[i, j, :, :HALF]
            by_z_ref[i, j] = part[i, j, :, HALF:]


def all_chunks(turned, grad_out):
    count = turned.shape[1]
    return pl.pallas_call(
        grad_kernel,
        grid=(NZ // 2,),
        in_specs=[
            pl.BlockSpec((2 * ZROWS, count), lambda i: (i, 0)),
            pl.BlockSpec((count, D), lambda i: (0, 0)),
        ],
        out_specs=[
            pl.BlockSpec((NY, 2, ROWS, HALF), lambda i: (0, i, 0, 0)),
            pl.BlockSpec((2, NY, ROWS, D - HALF), lambda i: (i, 0, 0, 0)),
        ],
        out_shape=[
            jax.ShapeDtypeStruct((NY, NZ, ROWS, HALF), BF16),
            jax.ShapeDtypeStruct((NZ, NY, ROWS, D - HALF), BF16),
        ],
        compiler_params=LIMIT,
    )(turned, grad_out)


def combine_kernel(groups, scale_ref, *refs):
    pairs, outs = list(refs[: sum(groups)]), refs[sum(groups) :]
    for count, out in zip(groups, outs):
        rows = out.shape[0] // count
        for i in range(count):
            pair = pairs.pop(0)
            weights = pair[0].astype(F32) - scale_ref[0] * pair[1].astype(F32)
            out[i * rows : (i + 1) * rows, :] = weights.astype(BF16)


def combine(scale, *groups):
    pairs = [pair for group in groups for pair in group]
    return pl.pallas_call(
        functools.partial(combine_kernel, [len(group) for group in groups]),
        in_specs=[SMEM] + [VMEM] * len(pairs),
        out_specs=[VMEM] * len(groups),
        out_shape=[
            jax.ShapeDtypeStruct((sum(pair.shape[1] for pair in group), group[0].shape[2]), BF16)
            for group in groups
        ],
        compiler_params=LIMIT,
    )(scale, *pairs)


def chunk_of(chunks, axis):
    size = SIZES[axis]
    me = lax.axis_index(axis)
    return lambda k: lax.dynamic_index_in_dim(chunks, (me + k) % size, 0, keepdims=False).astype(F32)


def grow(value, before, after):
    return jnp.pad(value.astype(F32), ((before, after), (0, 0)))


def scatter_rounds(chunks, axis, up, down, between):
    chunk, size = chunk_of(chunks, axis), SIZES[axis]
    rows = chunks.shape[1]
    up, down = grow(up, 0, rows - up.shape[0]), grow(down, rows - down.shape[0], 0)
    for k in range(size // 2 - 1, 0, -1):
        up, down = (chunk(k) + up).astype(BF16), (chunk(-k) + down).astype(BF16)
        up, down = between(k, shift(up, axis, 1), shift(down, axis, -1))
        up, down = up.astype(F32), down.astype(F32)
    return chunk(0) + up + down


def scatter_small(chunks, axis):
    chunk, size = chunk_of(chunks, axis), SIZES[axis]
    up, down = chunk(size // 2), chunk(1 - size // 2)
    for k in range(size // 2 - 1, 0, -1):
        up, down = shift(up.astype(BF16), axis, 1), shift(down.astype(BF16), axis, -1)
        up, down = lax.optimization_barrier((up, down))
        up = chunk(k) + up.astype(F32)
        down = down.astype(F32)
        if k > 1:
            down = chunk(1 - k) + down
    return chunk(0) + down + shift(up.astype(BF16), axis, 1).astype(F32)


def offsets(size):
    order = [0]
    for k in range(1, size // 2):
        order += [-k, k]
    return order + [size // 2]


def feature_rows(next_tokens):
    turned = next_tokens.T.reshape(NZ, NY, ROWS, next_tokens.shape[0])
    z_order = (lax.axis_index("z") + jnp.array(offsets(NZ))) % NZ
    y_order = (lax.axis_index("y") + jnp.array(offsets(NY))) % NY
    return jnp.take(jnp.take(turned, z_order, axis=0), y_order, axis=1)


def product(features, *blocks):
    return lax.dot_general(
        features.reshape(-1, features.shape[-1]), jnp.concatenate(blocks),
        (((0,), (0,)), ((), ())), preferred_element_type=F32,
    )


def local(tokens, grad_out, next_tokens, master, momentum):
    z, y = lax.axis_index("z"), lax.axis_index("y")
    up1, down1, up2, down2, turned = far_chunks(tokens, grad_out)
    up1, down1 = shift(up1, "y", 1), shift(down1, "y", -1)
    up2, down2 = shift(up2, "z", 1), shift(down2, "z", -1)
    by_y, by_z = all_chunks(turned, grad_out)
    token_sums = jnp.sum(grad_out.astype(F32), axis=1)
    row_total = jnp.dot(token_sums[None, :], tokens.astype(F32), precision=lax.Precision.HIGHEST)
    kept = (master - 0.01 * (0.9 * momentum)).astype(BF16)

    features = []

    def between(k, up, down):
        if k == 3:
            up, down, late = lax.optimization_barrier((up, down, next_tokens))
            features.append(feature_rows(late))
        elif k == 2:
            up, down, features[0] = lax.optimization_barrier((up, down, features[0]))
        else:
            up, down = lax.optimization_barrier((up, down))
        return up, down

    first = scatter_rounds(
        by_y.reshape(NY, YROWS, HALF), "y", up1, down1, lambda k, *sent: lax.optimization_barrier(sent)
    )
    second = scatter_rounds(by_z.reshape(NZ, ZROWS, D - HALF), "z", up2, down2, between)
    first = scatter_small(first.reshape(NZ, ROWS, HALF), "z")
    second = scatter_small(second.reshape(NY, ROWS, D - HALF), "y")
    reduced = jnp.concatenate([first, second], axis=1)

    both = jnp.stack([kept, reduced.astype(BF16)])
    one, two = both[:, :, :WIDE], both[:, :, WIDE:]
    squares = jnp.sum(reduced * reduced)

    up1, down1 = shift(one, "z", 1), shift(one, "z", -1)
    up2, down2 = shift(two, "y", 1), shift(two, "y", -1)
    sums = jnp.concatenate([row_total.reshape(-1, 128), jnp.full((1, 128), squares)])
    sums = lax.psum(sums, "z")
    up1, down1, up2, down2, sums = lax.optimization_barrier((up1, down1, up2, down2, sums))
    ones, twos = [one, up1, down1], [two, up2, down2]

    up1, down1 = shift(up1, "z", 1), shift(down1, "z", -1)
    up2 = shift(up2, "y", 1)
    sums = lax.psum(sums, "y")
    squares = sums[-1, 0]
    up1, down1, up2, squares = lax.optimization_barrier((up1, down1, up2, squares))
    ones += [up1, down1]
    twos = jnp.stack(twos + [up2], axis=1).reshape(2, ZROWS, D - WIDE)

    up1, down1 = shift(up1, "z", 1), shift(down1, "z", -1)
    up2, down2 = shift(twos, "z", 1), shift(twos, "z", -1)
    squares = lax.psum(squares, "x")
    up1, down1, squares = lax.optimization_barrier((up1, down1, squares))
    ones += [up1, down1]

    up1 = shift(up1, "z", 1)
    squares = lax.psum(squares, "c")
    up1, up2, down2, squares = lax.optimization_barrier((up1, up2, down2, squares))
    ones.append(up1)

    mean_square = squares / (D * FF)
    clip_factor = jnp.minimum(1.0, 1.0 / jnp.sqrt(mean_square + 1e-06))
    scale = (0.01 * clip_factor).reshape(1)
    (one,) = combine(scale, ones)
    two, up2, down2 = combine(scale, [twos], [up2], [down2])
    up1, down1 = shift(one, "y", 1), shift(one, "y", -1)

    new_momentum = 0.9 * momentum + clip_factor * reduced
    new_master = master - 0.01 * new_momentum
    row_sum = lax.dynamic_slice_in_dim(sums[:-1].reshape(-1), (z * NY + y) * ROWS, ROWS)
    row_checks = (clip_factor * row_sum / float(D) ** 0.5)[None, :]

    by_second = features[0]
    by_first = jnp.swapaxes(by_second, 0, 1)
    out_one = product(by_first[0], one)
    out_two = product(by_second[0], two)
    for k in range(2, NZ // 2):
        out_two += product(by_second[2 * k - 3 : 2 * k - 1], up2, down2)
        up2, down2 = lax.optimization_barrier((shift(up2, "z", 1), shift(down2, "z", -1)))
    out_two += product(by_second[NZ - 3 : NZ - 1], up2, down2)
    cut = ZROWS // 2
    up2, down2 = shift(up2[:cut], "z", 1), shift(down2[cut:], "z", -1)
    up1, down1 = lax.optimization_barrier((up1, down1))
    out_one += product(by_first[1:3], up1, down1)
    cut = YROWS // 2
    up1, down1 = shift(up1[:cut], "y", 1), shift(down1[cut:], "y", -1)
    out_one += product(by_first[3], up1, down1)
    out_two += product(by_second[NZ - 1], up2, down2)
    forward = jnp.concatenate([out_one, out_two], axis=1).astype(BF16)
    return new_master, new_momentum, forward, row_checks


def solution(mesh):
    split = Mesh(mesh.devices.reshape(NZ, NY, NX, NC), ("z", "y", "x", "c"))
    dp, mp = ("z", "y"), ("x", "c")
    in_specs = (P(dp, None), P(dp, mp), P(dp, None), P(dp, mp), P(dp, mp))
    out_specs = (P(dp, mp), P(dp, mp), P(dp, mp), P(mp, dp))
    return jax.shard_map(local, mesh=split, in_specs=in_specs, out_specs=out_specs, check_vma=False)
```

```python
import jax
import jax.numpy as jnp
from jax import lax
from jax.experimental import pallas as pl
from jax.experimental.pallas import tpu as pltpu
from jax.sharding import Mesh, PartitionSpec as P

D = 2304
FF = 18432
NZ, NY, NX, NC = 8, 4, 4, 2
SIZES = {"z": NZ, "y": NY, "x": NX, "c": NC}
ROWS = D // (NZ * NY)
YROWS, ZROWS = NZ * ROWS, NY * ROWS
HALF = D // 2
WIDE = D // 2
F32, BF16 = jnp.float32, jnp.bfloat16
LIMIT = pltpu.CompilerParams(vmem_limit_bytes=48 * 1024 * 1024)
HBM = pl.BlockSpec(memory_space=pl.ANY)
VMEM = pl.BlockSpec(memory_space=pltpu.VMEM)


def shift(value, axis, by):
    size = SIZES[axis]
    return lax.ppermute(value, axis, [(i, (i + by) % size) for i in range(size)])


def far_kernel(tokens_hbm, grad_hbm, up_y, down_y, up_z, down_z, turned, tokens, grad, sems):
    first = pltpu.make_async_copy(tokens_hbm, tokens, sems.at[0])
    second = pltpu.make_async_copy(grad_hbm, grad, sems.at[1])
    first.start()
    second.start()
    first.wait()
    turned[...] = tokens[...].T
    second.wait()
    z = (lax.axis_index("z") + NZ // 2) % NZ
    y = (lax.axis_index("y") + NY // 2) % NY
    rows = turned[pl.ds(pl.multiple_of(z * ZROWS, ZROWS), ZROWS), :]
    part = jnp.dot(rows, grad[:, HALF:], preferred_element_type=F32).astype(BF16)
    up_z[...] = part[: ZROWS // 2]
    down_z[...] = part[ZROWS // 2 :]
    for j in range(NY):

        @pl.when(y == j)
        def _():
            starts = [i * ZROWS + j * ROWS for i in range(NZ)]
            rows = jnp.concatenate([turned[s : s + ROWS, :] for s in starts])
            part = jnp.dot(rows, grad[:, :HALF], preferred_element_type=F32).astype(BF16)
            up_y[...] = part[: YROWS // 2]
            down_y[...] = part[YROWS // 2 :]


def far_chunks(tokens, grad_out):
    count = tokens.shape[0]
    shapes = [(YROWS // 2, HALF)] * 2 + [(ZROWS // 2, D - HALF)] * 2 + [(D, count)]
    return pl.pallas_call(
        far_kernel,
        in_specs=[HBM, HBM],
        out_specs=[VMEM] * 5,
        out_shape=[jax.ShapeDtypeStruct(s, BF16) for s in shapes],
        scratch_shapes=[
            pltpu.VMEM(tokens.shape, BF16),
            pltpu.VMEM(grad_out.shape, BF16),
            pltpu.SemaphoreType.DMA((2,)),
        ],
        compiler_params=LIMIT,
    )(tokens, grad_out)


def grad_kernel(turned_hbm, grad_hbm, by_y_hbm, by_z_hbm, turned, grad, by_y, by_z, sems_in, sems_out):
    step = 2 * ZROWS
    whole = pltpu.make_async_copy(grad_hbm, grad, sems_in.at[NZ // 2])
    whole.start()
    reads = []
    for i in range(NZ // 2):
        rows = pl.ds(i * step, step)
        reads.append(pltpu.make_async_copy(turned_hbm.at[rows], turned.at[rows], sems_in.at[i]))
        reads[-1].start()
    whole.wait()
    writes = []
    for i in range(NZ // 2):
        reads[i].wait()
        part = jnp.dot(turned[i * step : (i + 1) * step, :], grad[...], preferred_element_type=F32)
        part = part.astype(BF16).reshape(2, NY, ROWS, D)
        for k in range(2):
            for j in range(NY):
                by_y[j, 2 * i + k] = part[k, j, :, :HALF]
                by_z[2 * i + k, j] = part[k, j, :, HALF:]
        pair = pl.ds(2 * i, 2)
        writes.append(pltpu.make_async_copy(by_z.at[pair], by_z_hbm.at[pair], sems_out.at[0, i]))
        writes[-1].start()
        writes.append(pltpu.make_async_copy(by_y.at[:, pair], by_y_hbm.at[:, pair], sems_out.at[1, i]))
        writes[-1].start()
    for write in writes:
        write.wait()


def all_chunks(turned, grad_out):
    shapes = (NY, NZ, ROWS, HALF), (NZ, NY, ROWS, D - HALF)
    return pl.pallas_call(
        grad_kernel,
        in_specs=[HBM, HBM],
        out_specs=[HBM, HBM],
        out_shape=[jax.ShapeDtypeStruct(s, BF16) for s in shapes],
        scratch_shapes=[pltpu.VMEM(s, BF16) for s in (turned.shape, grad_out.shape, *shapes)]
        + [pltpu.SemaphoreType.DMA((NZ // 2 + 1,)), pltpu.SemaphoreType.DMA((2, NZ // 2))],
        compiler_params=LIMIT,
    )(turned, grad_out)


def offsets(size):
    order = [0]
    for k in range(1, size // 2):
        order += [-k, k]
    return order + [size // 2]


def order_kernel(tokens, by_y, by_z, turned):
    turned[...] = tokens[...].T
    z, y = lax.axis_index("z"), lax.axis_index("y")
    for j in range(NY):

        @pl.when(y == j)
        def _():
            for i, far in enumerate(offsets(NZ)):
                start = pl.multiple_of((z + far + NZ) % NZ * ZROWS, ZROWS)
                block = turned[pl.ds(start, ZROWS), :]
                for k, off in enumerate(offsets(NY)):
                    at = (j + off) % NY * ROWS
                    by_z[i, k] = block[at : at + ROWS]
                    by_y[k, i] = block[at : at + ROWS]


def feature_rows(next_tokens):
    count = next_tokens.shape[0]
    shapes = (NY, NZ, ROWS, count), (NZ, NY, ROWS, count)
    return pl.pallas_call(
        order_kernel,
        in_specs=[VMEM],
        out_specs=[VMEM, VMEM],
        out_shape=[jax.ShapeDtypeStruct(s, BF16) for s in shapes],
        scratch_shapes=[pltpu.VMEM((D, count), BF16)],
        compiler_params=LIMIT,
    )(next_tokens)


def stack_kernel(*refs):
    out, rows = refs[-1], refs[0].shape[0]
    for i, ref in enumerate(refs[:-1]):
        out[i * rows : (i + 1) * rows, :] = ref[...]


def stack(blocks):
    rows, columns = blocks[0].shape
    return pl.pallas_call(
        stack_kernel,
        in_specs=[VMEM] * len(blocks),
        out_specs=VMEM,
        out_shape=jax.ShapeDtypeStruct((rows * len(blocks), columns), BF16),
        compiler_params=LIMIT,
    )(*blocks)


def chunk_of(chunks, axis):
    size = SIZES[axis]
    me = lax.axis_index(axis)
    return lambda k: lax.dynamic_index_in_dim(chunks, (me + k) % size, 0, keepdims=False).astype(F32)


def grow(value, before, after):
    return jnp.pad(value.astype(F32), ((before, after), (0, 0)))


def scatter_rounds(chunks, axis, up, down, ready, come):
    chunk, size = chunk_of(chunks, axis), SIZES[axis]
    rows = chunks.shape[1]
    up, down = lax.optimization_barrier((up, down))
    up, down = grow(up, 0, rows - up.shape[0]), grow(down, rows - down.shape[0], 0)
    for k in range(size // 2 - 1, 0, -1):
        up, down = ready(k, (chunk(k) + up).astype(BF16), (chunk(-k) + down).astype(BF16))
        up, down = come(k, shift(up, axis, 1), shift(down, axis, -1))
        up, down = up.astype(F32), down.astype(F32)
    return chunk(0) + up + down


def scatter_small(chunks, axis):
    chunk, size = chunk_of(chunks, axis), SIZES[axis]
    up, down = chunk(size // 2), chunk(1 - size // 2)
    for k in range(size // 2 - 1, 0, -1):
        up, down = shift(up.astype(BF16), axis, 1), shift(down.astype(BF16), axis, -1)
        up, down = lax.optimization_barrier((up, down))
        up = chunk(k) + up.astype(F32)
        down = down.astype(F32)
        if k > 1:
            down = chunk(1 - k) + down
    return chunk(0) + down + shift(up.astype(BF16), axis, 1).astype(F32)


def product(features, *blocks):
    return lax.dot_general(
        features.reshape(-1, features.shape[-1]), jnp.concatenate(blocks),
        (((0,), (0,)), ((), ())), preferred_element_type=F32,
    )


def together(k, *values):
    return lax.optimization_barrier(values)


def local(tokens, grad_out, next_tokens, master, momentum):
    z, y = lax.axis_index("z"), lax.axis_index("y")
    up1, down1, up2, down2, turned = far_chunks(tokens, grad_out)
    up2, down2 = shift(up2, "z", 1), shift(down2, "z", -1)
    up1, down1 = shift(up1, "y", 1), shift(down1, "y", -1)
    by_y, by_z = all_chunks(turned, grad_out)

    aside = []

    def ready(k, up, down):
        up, down, late, late_tokens, late_grad = together(k, up, down, next_tokens, tokens, grad_out)
        aside.extend(feature_rows(late))
        token_sums = jnp.sum(late_grad.astype(F32), axis=1)
        row_total = jnp.dot(
            token_sums[None, :], late_tokens.astype(F32), precision=lax.Precision.HIGHEST
        )
        aside.append(row_total)
        return up, down

    def come(k, up, down):
        if k == NZ // 2 - 1:
            up, down, *aside[:] = together(k, up, down, *aside)
            return up, down
        return together(k, up, down)

    first = scatter_rounds(by_y.reshape(NY, YROWS, HALF), "y", up1, down1, ready, together)
    second = scatter_rounds(by_z.reshape(NZ, ZROWS, D - HALF), "z", up2, down2, together, come)
    first = scatter_small(first.reshape(NZ, ROWS, HALF), "z")
    second = scatter_small(second.reshape(NY, ROWS, D - HALF), "y")
    reduced = jnp.concatenate([first, second], axis=1)
    by_first, by_second, row_total = aside

    squares = jnp.sum(first * first) + jnp.sum(second * second)
    squares = lax.psum(lax.psum(squares, "c"), "x")
    sums = jnp.concatenate([row_total, jnp.full((1, 128), squares)], axis=1)
    sums = lax.psum(lax.psum(sums, "y"), "z")
    mean_square = sums[0, D] / (D * FF)
    clip_factor = jnp.minimum(1.0, 1.0 / jnp.sqrt(mean_square + 1e-06))
    new_momentum = 0.9 * momentum + clip_factor * reduced
    new_master = master - 0.01 * new_momentum
    one, two = new_master[:, :WIDE].astype(BF16), new_master[:, WIDE:].astype(BF16)
    row_sum = lax.dynamic_slice_in_dim(sums, (z * NY + y) * ROWS, ROWS, axis=1)
    row_checks = clip_factor * row_sum / float(D) ** 0.5

    ones, twos = [one], [two]
    up1 = down1 = one
    up2 = down2 = two
    for k in range(1, NZ // 2):
        up1, down1 = together(k, shift(up1, "z", 1), shift(down1, "z", -1))
        ones += [up1, down1]
    for k in range(1, NY // 2):
        up2, down2 = together(k, shift(up2, "y", 1), shift(down2, "y", -1))
        twos += [up2, down2]
    one = stack(ones + [shift(up1, "z", 1)])
    two = stack(twos + [shift(up2, "y", 1)])

    up2 = down2 = two
    arrived = []
    for k in range(1, NZ // 2 - 1):
        up2, down2 = together(k, shift(up2, "z", 1), shift(down2, "z", -1))
        arrived.append((up2, down2))
    up1, down1 = shift(one, "y", 1), shift(one, "y", -1)
    up2, down2 = shift(up2, "z", 1), shift(down2, "z", -1)
    up1, down1, up2, down2 = together(0, up1, down1, up2, down2)
    arrived.append((up2, down2))
    cut = ZROWS // 2
    far2 = shift(up2[:cut], "z", 1), shift(down2[cut:], "z", -1)
    cut = YROWS // 2
    far1 = shift(up1[:cut], "y", 1), shift(down1[cut:], "y", -1)
    out_two = product(by_second[0], two)
    for k, blocks in enumerate(arrived):
        out_two += product(by_second[2 * k + 1 : 2 * k + 3], *blocks)
    out_two += product(by_second[NZ - 1], *far2)
    out_one = product(by_first[0], one)
    out_one += product(by_first[1:3], up1, down1)
    out_one += product(by_first[3], *far1)
    forward = jnp.concatenate([out_one, out_two], axis=1).astype(BF16)
    return new_master, new_momentum, forward, row_checks


def solution(mesh):
    split = Mesh(mesh.devices.reshape(NZ, NY, NX, NC), ("z", "y", "x", "c"))
    dp, mp = ("z", "y"), ("x", "c")
    in_specs = (P(dp, None), P(dp, mp), P(dp, None), P(dp, mp), P(dp, mp))
    out_specs = (P(dp, mp), P(dp, mp), P(dp, mp), P(mp, dp))
    return jax.shard_map(local, mesh=split, in_specs=in_specs, out_specs=out_specs, check_vma=False)
```

```python
import jax
import jax.numpy as jnp
from jax import lax
from jax.experimental import pallas as pl
from jax.experimental.pallas import tpu as pltpu
from jax.sharding import Mesh, PartitionSpec as P

D = 2304
FF = 18432
NZ, NY, NX, NC = 8, 4, 4, 2
SIZES = {"z": NZ, "y": NY, "x": NX, "c": NC}
ROWS = D // (NZ * NY)
YROWS, ZROWS = NZ * ROWS, NY * ROWS
HALF = D // 2
WIDE = 1408
NEAR = 5
F32, BF16 = jnp.float32, jnp.bfloat16
HBM = pl.BlockSpec(memory_space=pltpu.HBM)
VMEM = pl.BlockSpec(memory_space=pltpu.VMEM)


def vmem_limit(mib):
    return pltpu.CompilerParams(vmem_limit_bytes=mib * 1024 * 1024)


def shift(value, axis, by):
    size = SIZES[axis]
    return lax.ppermute(value, axis, [(i, (i + by) % size) for i in range(size)])


def far_kernel(tokens_hbm, grad_hbm, up_y, down_y, up_z, down_z, turned, tokens, grad, sems):
    first = pltpu.make_async_copy(tokens_hbm, tokens, sems.at[0])
    second = pltpu.make_async_copy(grad_hbm, grad, sems.at[1])
    first.start()
    second.start()
    first.wait()
    turned[...] = tokens[...].T
    second.wait()
    z = (lax.axis_index("z") + NZ // 2) % NZ
    y = (lax.axis_index("y") + NY // 2) % NY
    rows = turned[pl.ds(pl.multiple_of(z * ZROWS, ZROWS), ZROWS), :]
    part = jnp.dot(rows, grad[:, HALF:], preferred_element_type=F32).astype(BF16)
    up_z[...] = part[: ZROWS // 2]
    down_z[...] = part[ZROWS // 2 :]
    for j in range(NY):

        @pl.when(y == j)
        def _():
            starts = [i * ZROWS + j * ROWS for i in range(NZ)]
            rows = jnp.concatenate([turned[s : s + ROWS, :] for s in starts])
            part = jnp.dot(rows, grad[:, :HALF], preferred_element_type=F32).astype(BF16)
            up_y[...] = part[: YROWS // 2]
            down_y[...] = part[YROWS // 2 :]


def far_chunks(tokens, grad_out):
    count = tokens.shape[0]
    shapes = [(YROWS // 2, HALF)] * 2 + [(ZROWS // 2, D - HALF)] * 2 + [(D, count)]
    return pl.pallas_call(
        far_kernel,
        in_specs=[HBM, HBM],
        out_specs=[VMEM] * 5,
        out_shape=[jax.ShapeDtypeStruct(s, BF16) for s in shapes],
        scratch_shapes=[
            pltpu.VMEM(tokens.shape, BF16),
            pltpu.VMEM(grad_out.shape, BF16),
            pltpu.SemaphoreType.DMA((2,)),
        ],
        compiler_params=vmem_limit(24),
    )(tokens, grad_out)


def grad_kernel(turned, grad_hbm, by_y, by_z, grad, sem):
    whole = pltpu.make_async_copy(grad_hbm, grad, sem)
    whole.start()
    whole.wait()
    step = 2 * ZROWS
    for i in range(NZ // 2):
        part = jnp.dot(turned[i * step : (i + 1) * step, :], grad[...], preferred_element_type=F32)
        part = part.astype(BF16).reshape(2, NY, ROWS, D)
        for k in range(2):
            for j in range(NY):
                by_y[j, 2 * i + k] = part[k, j, :, :HALF]
                by_z[2 * i + k, j] = part[k, j, :, HALF:]


def all_chunks(turned, grad_out):
    shapes = (NY, NZ, ROWS, HALF), (NZ, NY, ROWS, D - HALF)
    return pl.pallas_call(
        grad_kernel,
        in_specs=[VMEM, HBM],
        out_specs=[VMEM, VMEM],
        out_shape=[jax.ShapeDtypeStruct(s, BF16) for s in shapes],
        scratch_shapes=[pltpu.VMEM(grad_out.shape, BF16), pltpu.SemaphoreType.DMA],
        compiler_params=vmem_limit(32),
    )(turned, grad_out)


def offsets(size):
    order = [0]
    for k in range(1, size // 2):
        order += [-k, k]
    return order + [size // 2]


def order_kernel(tokens, near, rest, by_z, turned):
    turned[...] = tokens[...].T
    z, y = lax.axis_index("z"), lax.axis_index("y")
    for j in range(NY):

        @pl.when(y == j)
        def _():
            for i, far in enumerate(offsets(NZ)):
                start = pl.multiple_of((z + far + NZ) % NZ * ZROWS, ZROWS)
                block = turned[pl.ds(start, ZROWS), :]
                for k, off in enumerate(offsets(NY)):
                    at = (j + off) % NY * ROWS
                    by_z[i, k] = block[at : at + ROWS]
                    if i < NEAR:
                        near[k, i] = block[at : at + ROWS]
                    else:
                        rest[k, i - NEAR] = block[at : at + ROWS]


def feature_rows(next_tokens):
    count = next_tokens.shape[0]
    shapes = (NY, NEAR, ROWS, count), (NY, NZ - NEAR, ROWS, count), (NZ, NY, ROWS, count)
    return pl.pallas_call(
        order_kernel,
        in_specs=[VMEM],
        out_specs=[VMEM] * 3,
        out_shape=[jax.ShapeDtypeStruct(s, BF16) for s in shapes],
        scratch_shapes=[pltpu.VMEM((D, count), BF16)],
        compiler_params=vmem_limit(20),
    )(next_tokens)


def stack_kernel(*refs):
    out, rows = refs[-1], refs[0].shape[0]
    for i, ref in enumerate(refs[:-1]):
        out[i * rows : (i + 1) * rows, :] = ref[...]


def stack(blocks):
    rows, columns = blocks[0].shape
    return pl.pallas_call(
        stack_kernel,
        in_specs=[VMEM] * len(blocks),
        out_specs=VMEM,
        out_shape=jax.ShapeDtypeStruct((rows * len(blocks), columns), BF16),
        compiler_params=vmem_limit(12),
    )(*blocks)


def chunk_of(chunks, axis):
    size = SIZES[axis]
    me = lax.axis_index(axis)
    return lambda k: lax.dynamic_index_in_dim(chunks, (me + k) % size, 0, keepdims=False).astype(F32)


def grow(value, before, after):
    return jnp.pad(value.astype(F32), ((before, after), (0, 0)))


def scatter_rounds(chunks, axis, up, down, ready, come):
    chunk, size = chunk_of(chunks, axis), SIZES[axis]
    rows = chunks.shape[1]
    up, down = lax.optimization_barrier((up, down))
    up, down = grow(up, 0, rows - up.shape[0]), grow(down, rows - down.shape[0], 0)
    for k in range(size // 2 - 1, 0, -1):
        up, down = ready(k, (chunk(k) + up).astype(BF16), (chunk(-k) + down).astype(BF16))
        up, down = come(k, shift(up, axis, 1), shift(down, axis, -1))
        up, down = up.astype(F32), down.astype(F32)
    return chunk(0) + up + down


def scatter_ring(chunks, axis):
    chunk, size = chunk_of(chunks, axis), SIZES[axis]
    up, down = chunk(size // 2), chunk(1 - size // 2)
    for k in range(size // 2 - 1, 0, -1):
        up, down = shift(up.astype(BF16), axis, 1), shift(down.astype(BF16), axis, -1)
        up, down = lax.optimization_barrier((up, down))
        up = chunk(k) + up.astype(F32)
        down = down.astype(F32)
        if k > 1:
            down = chunk(1 - k) + down
    return chunk(0) + down + shift(up.astype(BF16), axis, 1).astype(F32)


def scatter_direct(chunks, axis):
    chunk = chunk_of(chunks, axis)
    sent = [shift(chunk(k).astype(BF16), axis, k) for k in (1, -1, 2)]
    sent = lax.optimization_barrier(tuple(sent))
    return chunk(0) + sent[0].astype(F32) + sent[1].astype(F32) + sent[2].astype(F32)


def product(features, *blocks):
    return lax.dot_general(
        features.reshape(-1, features.shape[-1]), jnp.concatenate(blocks),
        (((0,), (0,)), ((), ())), preferred_element_type=F32,
    )


def together(k, *values):
    return lax.optimization_barrier(values)


def total_slots(tokens, grad_out):
    token_sums = jnp.sum(grad_out.astype(F32), axis=1)
    row_total = jnp.dot(token_sums[None, :], tokens.astype(F32), precision=lax.Precision.HIGHEST)
    slots = jnp.pad(row_total.reshape(NZ * NY, ROWS), ((0, 0), (0, 128 - ROWS)))
    return jnp.repeat(slots, NX * NC, axis=0)


def local(tokens, grad_out, next_tokens, master, momentum):
    far_tokens = pltpu.with_memory_space_constraint(tokens, pltpu.HBM)
    far_grad = pltpu.with_memory_space_constraint(grad_out, pltpu.HBM)
    up1, down1, up2, down2, turned = far_chunks(far_tokens, far_grad)
    up2, down2 = shift(up2, "z", 1), shift(down2, "z", -1)
    up1, down1 = shift(up1, "y", 1), shift(down1, "y", -1)
    by_y, by_z = all_chunks(turned, far_grad)

    aside = []

    def ready_first(k, up, down):
        up, down, late, late_tokens, late_grad = together(k, up, down, next_tokens, tokens, grad_out)
        aside.extend(feature_rows(late))
        aside.append(total_slots(late_tokens, late_grad))
        return up, down

    first = scatter_rounds(by_y.reshape(NY, YROWS, HALF), "y", up1, down1, ready_first, together)
    held = [first]

    def ready_second(k, up, down):
        if k == 1:
            up, down, *held[:] = together(k, up, down, *held)
        return up, down

    def come_second(k, up, down):
        if k == NZ // 2 - 1:
            up, down, *aside[:] = together(k, up, down, *aside)
            return up, down
        return together(k, up, down)

    second = scatter_rounds(by_z.reshape(NZ, ZROWS, D - HALF), "z", up2, down2, ready_second, come_second)
    first = scatter_ring(held[0].reshape(NZ, ROWS, HALF), "z")
    second = scatter_direct(second.reshape(NY, ROWS, D - HALF), "y")
    reduced = jnp.concatenate([first, second], axis=1)
    near, rest, by_z, slots = aside

    squares = jnp.sum(first * first) + jnp.sum(second * second)
    slots = jnp.where(lax.broadcasted_iota(jnp.int32, slots.shape, 1) < ROWS, slots, squares)
    slots = lax.all_to_all(slots, ("z", "y", "x", "c"), split_axis=0, concat_axis=0, tiled=True)
    mean_square = jnp.sum(slots[:, ROWS]) / (D * FF)
    clip_factor = jnp.minimum(1.0, 1.0 / jnp.sqrt(mean_square + 1e-06))
    new_momentum = 0.9 * momentum + clip_factor * reduced
    new_master = master - 0.01 * new_momentum
    one, two = new_master[:, :WIDE].astype(BF16), new_master[:, WIDE:].astype(BF16)
    place = lax.axis_index("x") * NC + lax.axis_index("c")
    same = lax.dynamic_index_in_dim(slots.reshape(NZ * NY, NX * NC, 128), place, 1, keepdims=False)
    row_sum = jnp.sum(same[:, :ROWS], axis=0, keepdims=True)
    row_checks = clip_factor * row_sum / float(D) ** 0.5

    up1, down1 = shift(one, "z", 1), shift(one, "z", -1)
    twos = together(0, shift(two, "y", 1), shift(two, "y", -1), shift(two, "y", 2))
    up1, down1 = together(1, up1, down1)
    ones = [one, up1, down1]
    up1, down1 = together(2, shift(up1, "z", 1), shift(down1, "z", -1))
    ones += [up1, down1]
    two = stack([two, *twos])
    up2, down2 = shift(two, "z", 1), shift(two, "z", -1)
    up1, down1 = together(3, shift(up1, "z", 1), shift(down1, "z", -1))
    one_near = stack(ones)
    up3, down3 = shift(one_near, "y", 1), shift(one_near, "y", -1)
    one_rest = stack([up1, down1, shift(up1, "z", 1)])

    up2, down2 = together(1, up2, down2)
    arrived = [(up2, down2)]
    up4, down4 = shift(one_rest, "y", 1), shift(one_rest, "y", -1)
    up2, down2 = together(2, shift(up2, "z", 1), shift(down2, "z", -1))
    arrived.append((up2, down2))
    up3, down3 = together(1, up3, down3)
    cut = NEAR * ROWS // 16 * 8
    far3 = shift(up3[:cut], "y", 1), shift(down3[cut:], "y", -1)
    up2, down2 = shift(up2, "z", 1), shift(down2, "z", -1)
    up2, down2, up4, down4 = together(3, up2, down2, up4, down4)
    arrived.append((up2, down2))
    cut = ZROWS // 2
    far2 = shift(up2[:cut], "z", 1), shift(down2[cut:], "z", -1)
    cut = (NZ - NEAR) * ROWS // 16 * 8
    far4 = shift(up4[:cut], "y", 1), shift(down4[cut:], "y", -1)
    out_two = product(by_z[0], two)
    for k, blocks in enumerate(arrived):
        out_two += product(by_z[2 * k + 1 : 2 * k + 3], *blocks)
    out_two += product(by_z[NZ - 1], *far2)
    out_one = product(near[0], one_near) + product(rest[0], one_rest)
    out_one += product(near[1:3], up3, down3)
    out_one += product(rest[1:3], up4, down4)
    out_one += product(near[3], *far3)
    out_one += product(rest[3], *far4)
    forward = jnp.concatenate([out_one, out_two], axis=1).astype(BF16)
    return new_master, new_momentum, forward, row_checks


def solution(mesh):
    split = Mesh(mesh.devices.reshape(NZ, NY, NX, NC), ("z", "y", "x", "c"))
    dp, mp = ("z", "y"), ("x", "c")
    in_specs = (P(dp, None), P(dp, mp), P(dp, None), P(dp, mp), P(dp, mp))
    out_specs = (P(dp, mp), P(dp, mp), P(dp, mp), P(mp, dp))
    return jax.shard_map(local, mesh=split, in_specs=in_specs, out_specs=out_specs, check_vma=False)
```

```python
import functools

import jax
import jax.numpy as jnp
from jax import lax
from jax.experimental import pallas as pl
from jax.experimental.pallas import tpu as pltpu
from jax.sharding import Mesh, PartitionSpec as P

D = 2304
FF = 18432
NZ, NY, NX, NC = 8, 4, 4, 2
SIZES = {"z": NZ, "y": NY, "x": NX, "c": NC}
ROWS = D // (NZ * NY)
YROWS, ZROWS = NZ * ROWS, NY * ROWS
HALF = 1024
WIDE = 1408
NEAR = 5
REST = (4, -3, 3)
F32, BF16 = jnp.float32, jnp.bfloat16
HBM = pl.BlockSpec(memory_space=pltpu.HBM)
VMEM = pl.BlockSpec(memory_space=pltpu.VMEM)


def vmem_limit(mib):
    return pltpu.CompilerParams(vmem_limit_bytes=mib * 1024 * 1024)


def shift(value, axis, by):
    size = SIZES[axis]
    return lax.ppermute(value, axis, [(i, (i + by) % size) for i in range(size)])


def far_kernel(tokens_hbm, grad_hbm, up_y, down_y, up_z, down_z, turned, tokens, grad, sems):
    first = pltpu.make_async_copy(tokens_hbm, tokens, sems.at[0])
    second = pltpu.make_async_copy(grad_hbm, grad, sems.at[1])
    first.start()
    second.start()
    first.wait()
    turned[...] = tokens[...].T
    second.wait()
    z = (lax.axis_index("z") + NZ // 2) % NZ
    y = (lax.axis_index("y") + NY // 2) % NY
    rows = turned[pl.ds(pl.multiple_of(z * ZROWS, ZROWS), ZROWS), :]
    part = jnp.dot(rows, grad[:, HALF:], preferred_element_type=F32).astype(BF16)
    up_z[...] = part[: ZROWS // 2]
    down_z[...] = part[ZROWS // 2 :]
    for j in range(NY):

        @pl.when(y == j)
        def _():
            starts = [i * ZROWS + j * ROWS for i in range(NZ)]
            rows = jnp.concatenate([turned[s : s + ROWS, :] for s in starts])
            part = jnp.dot(rows, grad[:, :HALF], preferred_element_type=F32).astype(BF16)
            up_y[...] = part[: YROWS // 2]
            down_y[...] = part[YROWS // 2 :]


def far_chunks(tokens, grad_out):
    count = tokens.shape[0]
    shapes = [(YROWS // 2, HALF)] * 2 + [(ZROWS // 2, D - HALF)] * 2 + [(D, count)]
    return pl.pallas_call(
        far_kernel,
        in_specs=[HBM, HBM],
        out_specs=[VMEM] * 5,
        out_shape=[jax.ShapeDtypeStruct(s, BF16) for s in shapes],
        scratch_shapes=[
            pltpu.VMEM(tokens.shape, BF16),
            pltpu.VMEM(grad_out.shape, BF16),
            pltpu.SemaphoreType.DMA((2,)),
        ],
        compiler_params=vmem_limit(24),
    )(tokens, grad_out)


def grad_kernel(turned, grad_hbm, by_y_hbm, by_z_hbm, grad, by_y, by_z, sem, sems):
    whole = pltpu.make_async_copy(grad_hbm, grad, sem)
    whole.start()
    whole.wait()
    step = 2 * ZROWS
    writes = []
    for i in range(NZ // 2):
        part = jnp.dot(turned[i * step : (i + 1) * step, :], grad[...], preferred_element_type=F32)
        part = part.astype(BF16).reshape(2, NY, ROWS, D)
        for k in range(2):
            for j in range(NY):
                by_y[j, 2 * i + k] = part[k, j, :, :HALF]
                by_z[2 * i + k, j] = part[k, j, :, HALF:]
        pair = pl.ds(2 * i, 2)
        writes.append(pltpu.make_async_copy(by_z.at[pair], by_z_hbm.at[pair], sems.at[0, i]))
        writes[-1].start()
        writes.append(pltpu.make_async_copy(by_y.at[:, pair], by_y_hbm.at[:, pair], sems.at[1, i]))
        writes[-1].start()
    for write in writes:
        write.wait()


def all_chunks(turned, grad_out):
    shapes = (NY, NZ, ROWS, HALF), (NZ, NY, ROWS, D - HALF)
    return pl.pallas_call(
        grad_kernel,
        in_specs=[VMEM, HBM],
        out_specs=[HBM, HBM],
        out_shape=[pltpu.HBM(s, BF16) for s in shapes],
        scratch_shapes=[pltpu.VMEM(s, BF16) for s in (grad_out.shape, *shapes)]
        + [pltpu.SemaphoreType.DMA, pltpu.SemaphoreType.DMA((2, NZ // 2))],
        compiler_params=vmem_limit(40),
    )(turned, grad_out)


def add_kernel(axis, k, chunks, up, down, up_out, down_out, above, below, sems):
    size, me = SIZES[axis], lax.axis_index(axis)
    first = pltpu.make_async_copy(chunks.at[(me + k) % size], above, sems.at[0])
    second = pltpu.make_async_copy(chunks.at[(me - k + size) % size], below, sems.at[1])
    first.start()
    second.start()
    rows, half = above.shape[0], up.shape[0]
    first.wait()
    up_out[:half] = (above[:half].astype(F32) + up[...].astype(F32)).astype(BF16)
    if half < rows:
        up_out[half:] = above[half:]
    second.wait()
    rest = rows - down.shape[0]
    if rest:
        down_out[:rest] = below[:rest]
    down_out[rest:] = (below[rest:].astype(F32) + down[...].astype(F32)).astype(BF16)


def ring_add(chunks, axis, k, up, down):
    shape = chunks.shape[1:]
    return pl.pallas_call(
        functools.partial(add_kernel, axis, k),
        in_specs=[HBM, VMEM, VMEM],
        out_specs=[VMEM, VMEM],
        out_shape=[jax.ShapeDtypeStruct(shape, BF16)] * 2,
        scratch_shapes=[pltpu.VMEM(shape, BF16)] * 2 + [pltpu.SemaphoreType.DMA((2,))],
        compiler_params=vmem_limit(16),
    )(chunks, up, down)


def total_kernel(axis, chunks, up, down, out, own, sem):
    copy = pltpu.make_async_copy(chunks.at[lax.axis_index(axis)], own, sem)
    copy.start()
    copy.wait()
    out[...] = own[...].astype(F32) + up[...].astype(F32) + down[...].astype(F32)


def ring_total(chunks, axis, up, down):
    shape = chunks.shape[1:]
    return pl.pallas_call(
        functools.partial(total_kernel, axis),
        in_specs=[HBM, VMEM, VMEM],
        out_specs=VMEM,
        out_shape=jax.ShapeDtypeStruct(shape, F32),
        scratch_shapes=[pltpu.VMEM(shape, BF16), pltpu.SemaphoreType.DMA],
        compiler_params=vmem_limit(16),
    )(chunks, up, down)


def offsets(size):
    order = [0]
    for k in range(1, size // 2):
        order += [-k, k]
    return order + [size // 2]


def side_kernel(tokens_hbm, grad_hbm, next_hbm, near, rest, by_z, totals, tokens, grad, late, turned, sems):
    pairs = (next_hbm, late), (grad_hbm, grad), (tokens_hbm, tokens)
    copies = [pltpu.make_async_copy(a, b, sems.at[i]) for i, (a, b) in enumerate(pairs)]
    for copy in copies:
        copy.start()
    copies[0].wait()
    turned[...] = late[...].T
    z, y = lax.axis_index("z"), lax.axis_index("y")
    for j in range(NY):

        @pl.when(y == j)
        def _():
            for i, far in enumerate(offsets(NZ)):
                start = pl.multiple_of((z + far + NZ) % NZ * ZROWS, ZROWS)
                block = turned[pl.ds(start, ZROWS), :]
                for k, off in enumerate(offsets(NY)):
                    at = (j + off) % NY * ROWS
                    by_z[i, k] = block[at : at + ROWS]
                    if i < NEAR:
                        near[k, i] = block[at : at + ROWS]
                    else:
                        rest[k, REST.index(far)] = block[at : at + ROWS]

    copies[1].wait()
    copies[2].wait()
    total = jnp.zeros((1, D), F32)
    for i in range(0, tokens.shape[0], 64):
        sums = jnp.sum(grad[i : i + 64, :].astype(F32), axis=1, keepdims=True)
        total += jnp.sum(tokens[i : i + 64, :].astype(F32) * sums, axis=0, keepdims=True)
    totals[...] = total


def side_work(tokens, grad_out, next_tokens):
    count = tokens.shape[0]
    shapes = (NY, NEAR, ROWS, count), (NY, NZ - NEAR, ROWS, count), (NZ, NY, ROWS, count)
    *features, totals = pl.pallas_call(
        side_kernel,
        in_specs=[HBM] * 3,
        out_specs=[VMEM] * 4,
        out_shape=[jax.ShapeDtypeStruct(s, BF16) for s in shapes] + [jax.ShapeDtypeStruct((1, D), F32)],
        scratch_shapes=[pltpu.VMEM((count, D), BF16)] * 3
        + [pltpu.VMEM((D, count), BF16), pltpu.SemaphoreType.DMA((3,))],
        compiler_params=vmem_limit(32),
    )(tokens, grad_out, next_tokens)
    slots = jnp.pad(totals.reshape(NZ * NY, ROWS), ((0, 0), (0, 128 - ROWS)))
    return [*features, jnp.repeat(slots, NX * NC, axis=0)]


def update_kernel(slots, first, second, master, momentum, new_master, new_momentum, one, two, checks):
    lane = lax.broadcasted_iota(jnp.int32, slots.shape, 1)
    row = lax.broadcasted_iota(jnp.int32, slots.shape, 0)
    place = lax.axis_index("x") * NC + lax.axis_index("c")
    values = slots[...]
    squares = jnp.sum(jnp.where(lane == ROWS, values, 0.0), axis=(0, 1), keepdims=True)
    clip_factor = jnp.minimum(1.0, 1.0 / jnp.sqrt(squares / (D * FF) + 1e-06))
    row_sum = jnp.sum(jnp.where(row % (NX * NC) == place, values, 0.0), axis=0, keepdims=True)
    checks[...] = (clip_factor * row_sum / float(D) ** 0.5)[:, :ROWS]
    for grad, start in ((first, 0), (second, HALF)):
        at = pl.ds(start, grad.shape[1])
        fresh = 0.9 * momentum[:, at] + clip_factor * grad[...]
        new_momentum[:, at] = fresh
        new_master[:, at] = master[:, at] - 0.01 * fresh
    one[...] = new_master[:, :WIDE].astype(BF16)
    two[...] = new_master[:, WIDE:].astype(BF16)


def update(slots, first, second, master, momentum):
    shapes = [(master.shape, F32)] * 2 + [((ROWS, WIDE), BF16), ((ROWS, D - WIDE), BF16), ((1, ROWS), F32)]
    return pl.pallas_call(
        update_kernel,
        in_specs=[VMEM] * 5,
        out_specs=[VMEM] * 5,
        out_shape=[jax.ShapeDtypeStruct(*s) for s in shapes],
        compiler_params=vmem_limit(16),
    )(slots, first, second, master, momentum)


def stack_kernel(*refs):
    out, at = refs[-1], 0
    for ref in refs[:-1]:
        out[at : at + ref.shape[0], :] = ref[...]
        at += ref.shape[0]


def stack(blocks):
    rows, columns = sum(block.shape[0] for block in blocks), blocks[0].shape[1]
    return pl.pallas_call(
        stack_kernel,
        in_specs=[VMEM] * len(blocks),
        out_specs=VMEM,
        out_shape=jax.ShapeDtypeStruct((rows, columns), BF16),
        compiler_params=vmem_limit(12),
    )(*blocks)


def chunk_of(chunks, axis):
    size = SIZES[axis]
    me = lax.axis_index(axis)
    return lambda k: lax.dynamic_index_in_dim(chunks, (me + k) % size, 0, keepdims=False).astype(F32)


def scatter_rounds(chunks, axis, up, down, ready, come):
    chunks = pltpu.with_memory_space_constraint(chunks, pltpu.HBM)
    up, down = lax.optimization_barrier((up, down))
    for k in range(SIZES[axis] // 2 - 1, 0, -1):
        up, down = ready(k, *ring_add(chunks, axis, k, up, down))
        up, down = come(k, shift(up, axis, 1), shift(down, axis, -1))
    return ring_total(chunks, axis, up, down)


def scatter_ring(chunks):
    chunk = chunk_of(chunks, "z")
    far, up, down = (chunk(k).astype(BF16) for k in (4, 3, -3))
    far, up, down = lax.optimization_barrier((shift(far, "z", 2), shift(up, "z", 1), shift(down, "z", -1)))
    up = chunk(2) + far.astype(F32) + up.astype(F32)
    for k in (2, 1):
        down = chunk(-k) + down.astype(F32)
        up, down = shift(up.astype(BF16), "z", 1), shift(down.astype(BF16), "z", -1)
        up, down = lax.optimization_barrier((up, down))
        up = chunk(k - 1) + up.astype(F32)
    return up + down.astype(F32)


def scatter_direct(chunks, axis):
    chunk = chunk_of(chunks, axis)
    sent = [shift(chunk(k).astype(BF16), axis, k) for k in (1, -1, 2)]
    sent = lax.optimization_barrier(tuple(sent))
    return chunk(0) + sent[0].astype(F32) + sent[1].astype(F32) + sent[2].astype(F32)


def product(features, *blocks):
    return lax.dot_general(
        features.reshape(-1, features.shape[-1]), jnp.concatenate(blocks),
        (((0,), (0,)), ((), ())), preferred_element_type=F32,
    )


def together(k, *values):
    return lax.optimization_barrier(values)


def local(tokens, grad_out, next_tokens, master, momentum):
    far_tokens = pltpu.with_memory_space_constraint(tokens, pltpu.HBM)
    far_grad = pltpu.with_memory_space_constraint(grad_out, pltpu.HBM)
    up1, down1, up2, down2, turned = far_chunks(far_tokens, far_grad)
    up2, down2 = shift(up2, "z", 1), shift(down2, "z", -1)
    up1, down1 = shift(up1, "y", 1), shift(down1, "y", -1)
    by_y, by_z = all_chunks(turned, far_grad)

    aside, held = [], []

    def ready_second(k, up, down):
        if k == 2:
            up, down, *late = together(k, up, down, tokens, grad_out, next_tokens)
            aside.extend(side_work(*(pltpu.with_memory_space_constraint(a, pltpu.HBM) for a in late)))
        elif k == 1:
            up, down, *held[:] = together(k, up, down, *held)
        return up, down

    def come_second(k, up, down):
        if k == 2:
            up, down, *aside[:] = together(k, up, down, *aside)
            return up, down
        return together(k, up, down)

    def ready_first(k, up, down):
        return up, down

    held.append(scatter_rounds(by_y.reshape(NY, YROWS, HALF), "y", up1, down1, ready_first, together))
    second = scatter_rounds(by_z.reshape(NZ, ZROWS, D - HALF), "z", up2, down2, ready_second, come_second)
    first = scatter_ring(held[0].reshape(NZ, ROWS, HALF))
    second = scatter_direct(second.reshape(NY, ROWS, D - HALF), "y")
    near, rest, by_z, slots = aside

    squares = jnp.sum(first * first) + jnp.sum(second * second)
    slots = jnp.where(lax.broadcasted_iota(jnp.int32, slots.shape, 1) < ROWS, slots, squares)
    slots = lax.all_to_all(slots, ("z", "y", "x", "c"), split_axis=0, concat_axis=0, tiled=True)
    new_master, new_momentum, one, two, row_checks = update(slots, first, second, master, momentum)

    up1, down1 = shift(one, "z", 1), shift(one, "z", -1)
    twos = together(0, shift(two, "y", 1), shift(two, "y", -1), shift(two, "y", 2))
    up1, down1 = together(1, up1, down1)
    ones = [one, up1, down1]
    up1, down1 = together(2, shift(up1, "z", 1), shift(down1, "z", -1))
    two = stack([two, *twos])
    up2, down2 = shift(two, "z", 1), shift(two, "z", -1)
    one_near = stack([*ones, up1, down1])
    pair = stack([up1, ones[1]])
    up3, down3 = shift(one_near, "y", 1), shift(one_near, "y", -1)
    one_rest = stack([shift(pair, "z", 2), shift(down1, "z", -1)])

    up2, down2 = together(1, up2, down2)
    arrived = [(up2, down2)]
    up4, down4 = shift(one_rest, "y", 1), shift(one_rest, "y", -1)
    up2, down2 = together(2, shift(up2, "z", 1), shift(down2, "z", -1))
    arrived.append((up2, down2))
    up3, down3 = together(1, up3, down3)
    cut = NEAR * ROWS // 16 * 8
    far3 = shift(up3[:cut], "y", 1), shift(down3[cut:], "y", -1)
    up2, down2 = shift(up2, "z", 1), shift(down2, "z", -1)
    up2, down2, up4, down4 = together(3, up2, down2, up4, down4)
    arrived.append((up2, down2))
    cut = ZROWS // 2
    far2 = shift(up2[:cut], "z", 1), shift(down2[cut:], "z", -1)
    cut = (NZ - NEAR) * ROWS // 16 * 8
    far4 = shift(up4[:cut], "y", 1), shift(down4[cut:], "y", -1)
    out_two = product(by_z[0], two)
    for k, blocks in enumerate(arrived):
        out_two += product(by_z[2 * k + 1 : 2 * k + 3], *blocks)
    out_two += product(by_z[NZ - 1], *far2)
    out_one = product(near[0], one_near) + product(rest[0], one_rest)
    out_one += product(near[1:3], up3, down3)
    out_one += product(rest[1:3], up4, down4)
    out_one += product(near[3], *far3)
    out_one += product(rest[3], *far4)
    forward = jnp.concatenate([out_one, out_two], axis=1).astype(BF16)
    return new_master, new_momentum, forward, row_checks


def solution(mesh):
    split = Mesh(mesh.devices.reshape(NZ, NY, NX, NC), ("z", "y", "x", "c"))
    dp, mp = ("z", "y"), ("x", "c")
    in_specs = (P(dp, None), P(dp, mp), P(dp, None), P(dp, mp), P(dp, mp))
    out_specs = (P(dp, mp), P(dp, mp), P(dp, mp), P(mp, dp))
    return jax.shard_map(local, mesh=split, in_specs=in_specs, out_specs=out_specs, check_vma=False)
```

```python
import functools

import jax
import jax.numpy as jnp
from jax import lax
from jax.experimental import pallas as pl
from jax.experimental.pallas import tpu as pltpu
from jax.sharding import Mesh, PartitionSpec as P

D = 2304
FF = 18432
NZ, NY, NX, NC = 8, 4, 4, 2
SIZES = {"z": NZ, "y": NY, "x": NX, "c": NC}
ROWS = D // (NZ * NY)
YROWS, ZROWS = NZ * ROWS, NY * ROWS
HALF = 1152
WIDE = 1280
NEAR = 5
CUT = 192
F32, BF16 = jnp.float32, jnp.bfloat16
HBM = pl.BlockSpec(memory_space=pltpu.HBM)
VMEM = pl.BlockSpec(memory_space=pltpu.VMEM)


def vmem_limit(mib):
    return pltpu.CompilerParams(vmem_limit_bytes=mib * 1024 * 1024)


def shift(value, axis, by):
    size = SIZES[axis]
    return lax.ppermute(value, axis, [(i, (i + by) % size) for i in range(size)])


def far_kernel(tokens_hbm, grad_hbm, up_y, down_y, up_z, down_z, turned, tokens, grad, sems):
    first = pltpu.make_async_copy(tokens_hbm, tokens, sems.at[0])
    second = pltpu.make_async_copy(grad_hbm, grad, sems.at[1])
    first.start()
    second.start()
    first.wait()
    turned[...] = tokens[...].T
    second.wait()
    z = (lax.axis_index("z") + NZ // 2) % NZ
    y = (lax.axis_index("y") + NY // 2) % NY
    rows = turned[pl.ds(pl.multiple_of(z * ZROWS, ZROWS), ZROWS), :]
    part = jnp.dot(rows, grad[:, HALF:], preferred_element_type=F32).astype(BF16)
    up_z[...] = part[: ZROWS // 2]
    down_z[...] = part[ZROWS // 2 :]
    for j in range(NY):

        @pl.when(y == j)
        def _():
            starts = [i * ZROWS + j * ROWS for i in range(NZ)]
            rows = jnp.concatenate([turned[s : s + ROWS, :] for s in starts])
            part = jnp.dot(rows, grad[:, :HALF], preferred_element_type=F32).astype(BF16)
            up_y[...] = part[: YROWS // 2]
            down_y[...] = part[YROWS // 2 :]


def far_chunks(tokens, grad_out):
    count = tokens.shape[0]
    shapes = [(YROWS // 2, HALF)] * 2 + [(ZROWS // 2, D - HALF)] * 2 + [(D, count)]
    return pl.pallas_call(
        far_kernel,
        in_specs=[HBM, HBM],
        out_specs=[VMEM] * 5,
        out_shape=[jax.ShapeDtypeStruct(s, BF16) for s in shapes],
        scratch_shapes=[
            pltpu.VMEM(tokens.shape, BF16),
            pltpu.VMEM(grad_out.shape, BF16),
            pltpu.SemaphoreType.DMA((2,)),
        ],
        compiler_params=vmem_limit(24),
    )(tokens, grad_out)


def grad_kernel(turned, grad_hbm, by_y_hbm, by_z_hbm, grad, by_y, by_z, sem, sems):
    whole = pltpu.make_async_copy(grad_hbm, grad, sem)
    whole.start()
    whole.wait()
    step = 2 * ZROWS
    writes = []
    for i in range(NZ // 2):
        part = jnp.dot(turned[i * step : (i + 1) * step, :], grad[...], preferred_element_type=F32)
        part = part.astype(BF16).reshape(2, NY, ROWS, D)
        for k in range(2):
            for j in range(NY):
                by_y[j, 2 * i + k] = part[k, j, :, :HALF]
                by_z[2 * i + k, j] = part[k, j, :, HALF:]
        pair = pl.ds(2 * i, 2)
        writes.append(pltpu.make_async_copy(by_z.at[pair], by_z_hbm.at[pair], sems.at[0, i]))
        writes[-1].start()
        writes.append(pltpu.make_async_copy(by_y.at[:, pair], by_y_hbm.at[:, pair], sems.at[1, i]))
        writes[-1].start()
    for write in writes:
        write.wait()


def all_chunks(turned, grad_out):
    shapes = (NY, NZ, ROWS, HALF), (NZ, NY, ROWS, D - HALF)
    return pl.pallas_call(
        grad_kernel,
        in_specs=[VMEM, HBM],
        out_specs=[HBM, HBM],
        out_shape=[pltpu.HBM(s, BF16) for s in shapes],
        scratch_shapes=[pltpu.VMEM(s, BF16) for s in (grad_out.shape, *shapes)]
        + [pltpu.SemaphoreType.DMA, pltpu.SemaphoreType.DMA((2, NZ // 2))],
        compiler_params=vmem_limit(40),
    )(turned, grad_out)


def add_kernel(axis, k, chunks, up, down, up_out, down_out, above, below, sems):
    size, me = SIZES[axis], lax.axis_index(axis)
    first = pltpu.make_async_copy(chunks.at[(me + k) % size], above, sems.at[0])
    second = pltpu.make_async_copy(chunks.at[(me - k + size) % size], below, sems.at[1])
    first.start()
    second.start()
    rows, half = above.shape[0], up.shape[0]
    first.wait()
    up_out[:half] = (above[:half].astype(F32) + up[...].astype(F32)).astype(BF16)
    if half < rows:
        up_out[half:] = above[half:]
    second.wait()
    rest = rows - down.shape[0]
    if rest:
        down_out[:rest] = below[:rest]
    down_out[rest:] = (below[rest:].astype(F32) + down[...].astype(F32)).astype(BF16)


def ring_add(chunks, axis, k, up, down):
    shape = chunks.shape[1:]
    return pl.pallas_call(
        functools.partial(add_kernel, axis, k),
        in_specs=[HBM, VMEM, VMEM],
        out_specs=[VMEM, VMEM],
        out_shape=[jax.ShapeDtypeStruct(shape, BF16)] * 2,
        scratch_shapes=[pltpu.VMEM(shape, BF16)] * 2 + [pltpu.SemaphoreType.DMA((2,))],
        compiler_params=vmem_limit(16),
    )(chunks, up, down)


def total_kernel(axis, chunks, up, down, out, own, total, sem):
    copy = pltpu.make_async_copy(chunks.at[lax.axis_index(axis)], own, sem)
    copy.start()
    copy.wait()
    total[...] = own[...].astype(F32) + up[...].astype(F32) + down[...].astype(F32)
    copy = pltpu.make_async_copy(total, out, sem)
    copy.start()
    copy.wait()


def ring_total(chunks, axis, up, down):
    shape = chunks.shape[1:]
    return pl.pallas_call(
        functools.partial(total_kernel, axis),
        in_specs=[HBM, VMEM, VMEM],
        out_specs=HBM,
        out_shape=pltpu.HBM(shape, F32),
        scratch_shapes=[pltpu.VMEM(shape, BF16), pltpu.VMEM(shape, F32), pltpu.SemaphoreType.DMA],
        compiler_params=vmem_limit(16),
    )(chunks, up, down)


def offsets(size):
    order = [0]
    for k in range(1, size // 2):
        order += [-k, k]
    return order + [size // 2]


def side_kernel(tokens_hbm, grad_hbm, next_hbm, near_hbm, rest_hbm, by_z_hbm, totals, *scratch):
    near, rest, by_z, tokens, grad, late, turned, sems = scratch
    pairs = (next_hbm, late), (grad_hbm, grad), (tokens_hbm, tokens)
    copies = [pltpu.make_async_copy(a, b, sems.at[i]) for i, (a, b) in enumerate(pairs)]
    for copy in copies:
        copy.start()
    copies[0].wait()
    turned[...] = late[...].T
    z, y = lax.axis_index("z"), lax.axis_index("y")
    for j in range(NY):

        @pl.when(y == j)
        def _():
            for i, far in enumerate(offsets(NZ)):
                start = pl.multiple_of((z + far + NZ) % NZ * ZROWS, ZROWS)
                block = turned[pl.ds(start, ZROWS), :]
                for k, off in enumerate(offsets(NY)):
                    at = (j + off) % NY * ROWS
                    by_z[i, k] = block[at : at + ROWS]
                    if i < NEAR:
                        near[k, i] = block[at : at + ROWS]
                    else:
                        rest[k, i - NEAR] = block[at : at + ROWS]

    pairs = (near, near_hbm), (rest, rest_hbm), (by_z, by_z_hbm)
    writes = [pltpu.make_async_copy(a, b, sems.at[i + 3]) for i, (a, b) in enumerate(pairs)]
    for write in writes:
        write.start()
    copies[1].wait()
    copies[2].wait()
    total = jnp.zeros((1, D), F32)
    for i in range(0, tokens.shape[0], 64):
        sums = jnp.sum(grad[i : i + 64, :].astype(F32), axis=1, keepdims=True)
        total += jnp.sum(tokens[i : i + 64, :].astype(F32) * sums, axis=0, keepdims=True)
    totals[...] = total
    for write in writes:
        write.wait()


def side_work(tokens, grad_out, next_tokens):
    count = tokens.shape[0]
    shapes = (NY, NEAR, ROWS, count), (NY, NZ - NEAR, ROWS, count), (NZ, NY, ROWS, count)
    *features, totals = pl.pallas_call(
        side_kernel,
        in_specs=[HBM] * 3,
        out_specs=[HBM] * 3 + [VMEM],
        out_shape=[pltpu.HBM(s, BF16) for s in shapes] + [jax.ShapeDtypeStruct((1, D), F32)],
        scratch_shapes=[pltpu.VMEM(s, BF16) for s in shapes]
        + [pltpu.VMEM((count, D), BF16)] * 3
        + [pltpu.VMEM((D, count), BF16), pltpu.SemaphoreType.DMA((6,))],
        compiler_params=vmem_limit(32),
    )(tokens, grad_out, next_tokens)
    slots = jnp.pad(totals.reshape(NZ * NY, ROWS), ((0, 0), (0, 128 - ROWS)))
    return [*features, jnp.repeat(slots, NX * NC, axis=0)]


def update_kernel(slots, first, second, master_hbm, momentum_hbm, *refs):
    new_master, new_momentum, one, two, checks, master, momentum, sems = refs
    copies = [
        pltpu.make_async_copy(master_hbm, master, sems.at[0]),
        pltpu.make_async_copy(momentum_hbm, momentum, sems.at[1]),
    ]
    for copy in copies:
        copy.start()
    lane = lax.broadcasted_iota(jnp.int32, slots.shape, 1)
    row = lax.broadcasted_iota(jnp.int32, slots.shape, 0)
    place = lax.axis_index("x") * NC + lax.axis_index("c")
    values = slots[...]
    squares = jnp.sum(jnp.where(lane == ROWS, values, 0.0), axis=(0, 1), keepdims=True)
    clip_factor = jnp.minimum(1.0, 1.0 / jnp.sqrt(squares / (D * FF) + 1e-06))
    row_sum = jnp.sum(jnp.where(row % (NX * NC) == place, values, 0.0), axis=0, keepdims=True)
    checks[...] = (clip_factor * row_sum / float(D) ** 0.5)[:, :ROWS]
    for copy in copies:
        copy.wait()
    for grad, start in ((first, 0), (second, HALF)):
        at = pl.ds(start, grad.shape[1])
        fresh = 0.9 * momentum[:, at] + clip_factor * grad[...]
        new_momentum[:, at] = fresh
        new_master[:, at] = master[:, at] - 0.01 * fresh
    one[...] = new_master[:, :WIDE].astype(BF16)
    two[...] = new_master[:, WIDE:].astype(BF16)


def update(slots, first, second, master, momentum):
    shapes = [(master.shape, F32)] * 2 + [((ROWS, WIDE), BF16), ((ROWS, D - WIDE), BF16), ((1, ROWS), F32)]
    return pl.pallas_call(
        update_kernel,
        in_specs=[VMEM] * 3 + [HBM] * 2,
        out_specs=[VMEM] * 5,
        out_shape=[jax.ShapeDtypeStruct(*s) for s in shapes],
        scratch_shapes=[pltpu.VMEM(master.shape, F32)] * 2 + [pltpu.SemaphoreType.DMA((2,))],
        compiler_params=vmem_limit(16),
    )(slots, first, second, *(pltpu.with_memory_space_constraint(a, pltpu.HBM) for a in (master, momentum)))


def stack_kernel(groups, *refs):
    refs = list(refs)
    outs = refs[len(refs) - len(groups) :]
    for group, out in zip(groups, outs):
        at = 0
        for start, stop in group:
            out[at : at + stop - start, :] = refs.pop(0)[start:stop, :]
            at += stop - start


def stack(*groups):
    ranges = [[(start, stop) for _, start, stop in group] for group in groups]
    blocks = [block for group in groups for block, _, _ in group]
    rows = [sum(stop - start for start, stop in group) for group in ranges]
    return pl.pallas_call(
        functools.partial(stack_kernel, ranges),
        in_specs=[VMEM] * len(blocks),
        out_specs=[VMEM] * len(groups),
        out_shape=[
            jax.ShapeDtypeStruct((count, group[0][0].shape[1]), BF16) for count, group in zip(rows, groups)
        ],
        compiler_params=vmem_limit(16),
    )(*blocks)


def whole(*blocks):
    return [(block, 0, block.shape[0]) for block in blocks]


def chunk_of(chunks, axis):
    size = SIZES[axis]
    me = lax.axis_index(axis)
    return lambda k: lax.dynamic_index_in_dim(chunks, (me + k) % size, 0, keepdims=False).astype(F32)


def scatter_rounds(chunks, axis, up, down, ready, come):
    up, down = lax.optimization_barrier((up, down))
    for k in range(SIZES[axis] // 2 - 1, 0, -1):
        up, down = ready(k, *ring_add(chunks, axis, k, up, down))
        up, down = come(k, shift(up, axis, 1), shift(down, axis, -1))
    return up, down


def short_first(chunk):
    far, up, down = (chunk(k).astype(BF16) for k in (4, 3, -3))
    return shift(far, "z", 2), shift(up, "z", 1), shift(down, "z", -1)


def short_last(chunk, far, up, down):
    up = chunk(2) + far.astype(F32) + up.astype(F32)
    for k in (2, 1):
        down = chunk(-k) + down.astype(F32)
        up, down = shift(up.astype(BF16), "z", 1), shift(down.astype(BF16), "z", -1)
        up, down = lax.optimization_barrier((up, down))
        up = chunk(k - 1) + up.astype(F32)
    return up + down.astype(F32)


def scatter_direct(chunks, axis):
    chunk = chunk_of(chunks, axis)
    sent = [shift(chunk(k).astype(BF16), axis, k) for k in (1, -1, 2)]
    sent = lax.optimization_barrier(tuple(sent))
    return chunk(0) + sent[0].astype(F32) + sent[1].astype(F32) + sent[2].astype(F32)


def product(features, *blocks):
    return lax.dot_general(
        features.reshape(-1, features.shape[-1]), jnp.concatenate(blocks),
        (((0,), (0,)), ((), ())), preferred_element_type=F32,
    )


def together(k, *values):
    return lax.optimization_barrier(values)


def local(tokens, grad_out, next_tokens, master, momentum):
    far_tokens = pltpu.with_memory_space_constraint(tokens, pltpu.HBM)
    far_grad = pltpu.with_memory_space_constraint(grad_out, pltpu.HBM)
    up1, down1, up2, down2, turned = far_chunks(far_tokens, far_grad)
    up2, down2 = shift(up2, "z", 1), shift(down2, "z", -1)
    up1, down1 = shift(up1, "y", 1), shift(down1, "y", -1)
    by_y, by_z = all_chunks(turned, far_grad)

    by_y = pltpu.with_memory_space_constraint(by_y.reshape(NY, YROWS, HALF), pltpu.HBM)
    by_z = pltpu.with_memory_space_constraint(by_z.reshape(NZ, ZROWS, D - HALF), pltpu.HBM)

    aside, held = [], []

    def ready_first(k, up, down):
        return up, down

    def ready_second(k, up, down):
        if k == 2:
            up, down, *late = together(k, up, down, tokens, grad_out, next_tokens)
            late = [pltpu.with_memory_space_constraint(a, pltpu.HBM) for a in late]
            aside.extend(side_work(*late))
        elif k == 1:
            held[:] = together(k, *held, up, down)[:1]
        return up, down

    def come_second(k, up, down):
        if k == 2:
            up, down, *aside[:] = together(k, up, down, *aside)
            return up, down
        if k == 1:
            up, down, *held[:] = together(k, up, down, *short_first(chunk_of(held[0], "z")))
            return up, down
        return together(k, up, down)

    first = ring_total(by_y, "y", *scatter_rounds(by_y, "y", up1, down1, ready_first, together))
    first = first.reshape(NZ, ROWS, HALF)
    held.append(first)
    second = scatter_rounds(by_z, "z", up2, down2, ready_second, come_second)
    second = ring_total(by_z, "z", *second)
    first = short_last(chunk_of(first, "z"), *held)
    second = scatter_direct(second.reshape(NY, ROWS, D - HALF), "y")
    near, rest, by_z, slots = aside

    squares = jnp.sum(first * first) + jnp.sum(second * second)
    slots = jnp.where(lax.broadcasted_iota(jnp.int32, slots.shape, 1) < ROWS, slots, squares)
    slots = lax.all_to_all(slots, ("z", "y", "x", "c"), split_axis=0, concat_axis=0, tiled=True)
    new_master, new_momentum, one, two, row_checks = update(slots, first, second, master, momentum)

    up1, down1, *twos = together(
        1, shift(one, "z", 1), shift(one, "z", -1), shift(two, "y", 1), shift(two, "y", -1), shift(two, "y", 2)
    )
    ones = [one, up1, down1]
    up1, down1 = together(2, shift(up1, "z", 1), shift(down1, "z", -1))
    (two,) = stack(whole(two, *twos))
    up2, down2 = shift(two, "z", 1), shift(two, "z", -1)
    (one_near,) = stack(whole(*ones, up1, down1))
    up3, down3 = shift(one_near, "y", 1), shift(one_near, "y", -1)
    up1, down1, one_near = together(3, up1, down1, one_near)

    up1 = shift(up1, "z", 1)
    up2, down2, down1 = together(1, up2, down2, down1)
    arrived = [(up2, down2)]
    ones = [up1, shift(down1, "z", -1), shift(up1, "z", 1)]
    up2, down2 = together(2, shift(up2, "z", 1), shift(down2, "z", -1))
    arrived.append((up2, down2))
    up3, down3 = together(1, up3, down3)
    count = NEAR * ROWS
    one_rest, up4, down4 = stack(
        whole(*ones), [*whole(*ones), (up3, 0, CUT)], [*whole(*ones), (down3, CUT, count)]
    )
    up4, down4 = shift(up4, "y", 1), shift(down4, "y", -1)
    up2, down2 = shift(up2, "z", 1), shift(down2, "z", -1)
    up2, down2, up4, down4 = together(3, up2, down2, up4, down4)
    arrived.append((up2, down2))
    count = (NZ - NEAR) * ROWS
    cut = count // 16 * 8
    sends = stack(
        [(up4, 0, cut)], [(down4, cut, count)], [(up2, 0, ZROWS // 2)], [(down2, ZROWS // 2, ZROWS)]
    )
    far4 = shift(sends[0], "y", 1), shift(sends[1], "y", -1)
    far2 = shift(sends[2], "z", 1), shift(sends[3], "z", -1)
    sides4, far3 = stack(
        [(up4, 0, count), (down4, 0, count)],
        [(up4, count, up4.shape[0]), (down4, count, down4.shape[0])],
    )
    out_two = product(by_z[0], two)
    for k, blocks in enumerate(arrived):
        out_two += product(by_z[2 * k + 1 : 2 * k + 3], *blocks)
    out_two += product(by_z[NZ - 1], *far2)
    out_one = product(near[0], one_near) + product(rest[0], one_rest)
    out_one += product(near[1:3], up3, down3)
    out_one += product(near[3], far3)
    out_one += product(rest[1:3], sides4)
    out_one += product(rest[3], *far4)
    forward = jnp.concatenate([out_one, out_two], axis=1).astype(BF16)
    return new_master, new_momentum, forward, row_checks


def solution(mesh):
    split = Mesh(mesh.devices.reshape(NZ, NY, NX, NC), ("z", "y", "x", "c"))
    dp, mp = ("z", "y"), ("x", "c")
    in_specs = (P(dp, None), P(dp, mp), P(dp, None), P(dp, mp), P(dp, mp))
    out_specs = (P(dp, mp), P(dp, mp), P(dp, mp), P(mp, dp))
    return jax.shard_map(local, mesh=split, in_specs=in_specs, out_specs=out_specs, check_vma=False)
```

```python
import functools

import jax
import jax.numpy as jnp
from jax import lax
from jax.experimental import pallas as pl
from jax.experimental.pallas import tpu as pltpu
from jax.sharding import Mesh, PartitionSpec as P

D = 2304
FF = 18432
NZ, NY, NX, NC = 8, 4, 4, 2
SIZES = {"z": NZ, "y": NY, "x": NX, "c": NC}
ROWS = D // (NZ * NY)
YROWS, ZROWS = NZ * ROWS, NY * ROWS
HALF = 1152
WIDE = 1280
NEAR = 5
CUT = 192
F32, BF16 = jnp.float32, jnp.bfloat16
HBM = pl.BlockSpec(memory_space=pltpu.HBM)
VMEM = pl.BlockSpec(memory_space=pltpu.VMEM)


def vmem_limit(mib):
    return pltpu.CompilerParams(vmem_limit_bytes=mib * 1024 * 1024)


def shift(value, axis, by):
    size = SIZES[axis]
    return lax.ppermute(value, axis, [(i, (i + by) % size) for i in range(size)])


def far_kernel(tokens_hbm, grad_hbm, up_y, down_y, up_z, down_z, turned, tokens, grad, sems):
    first = pltpu.make_async_copy(tokens_hbm, tokens, sems.at[0])
    second = pltpu.make_async_copy(grad_hbm, grad, sems.at[1])
    first.start()
    second.start()
    first.wait()
    turned[...] = tokens[...].T
    second.wait()
    z = (lax.axis_index("z") + NZ // 2) % NZ
    y = (lax.axis_index("y") + NY // 2) % NY
    rows = turned[pl.ds(pl.multiple_of(z * ZROWS, ZROWS), ZROWS), :]
    part = jnp.dot(rows, grad[:, HALF:], preferred_element_type=F32).astype(BF16)
    up_z[...] = part[: ZROWS // 2]
    down_z[...] = part[ZROWS // 2 :]
    for j in range(NY):

        @pl.when(y == j)
        def _():
            starts = [i * ZROWS + j * ROWS for i in range(NZ)]
            rows = jnp.concatenate([turned[s : s + ROWS, :] for s in starts])
            part = jnp.dot(rows, grad[:, :HALF], preferred_element_type=F32).astype(BF16)
            up_y[...] = part[: YROWS // 2]
            down_y[...] = part[YROWS // 2 :]


def far_chunks(tokens, grad_out):
    count = tokens.shape[0]
    shapes = [(YROWS // 2, HALF)] * 2 + [(ZROWS // 2, D - HALF)] * 2 + [(D, count)]
    return pl.pallas_call(
        far_kernel,
        in_specs=[HBM, HBM],
        out_specs=[VMEM] * 5,
        out_shape=[jax.ShapeDtypeStruct(s, BF16) for s in shapes],
        scratch_shapes=[
            pltpu.VMEM(tokens.shape, BF16),
            pltpu.VMEM(grad_out.shape, BF16),
            pltpu.SemaphoreType.DMA((2,)),
        ],
        compiler_params=vmem_limit(24),
    )(tokens, grad_out)


def grad_kernel(turned, grad_hbm, by_y_hbm, by_z_hbm, grad, by_y, by_z, sem, sems):
    whole = pltpu.make_async_copy(grad_hbm, grad, sem)
    whole.start()
    whole.wait()
    step = 2 * ZROWS
    writes = []
    for i in range(NZ // 2):
        part = jnp.dot(turned[i * step : (i + 1) * step, :], grad[...], preferred_element_type=F32)
        part = part.astype(BF16).reshape(2, NY, ROWS, D)
        for k in range(2):
            for j in range(NY):
                by_y[j, 2 * i + k] = part[k, j, :, :HALF]
                by_z[2 * i + k, j] = part[k, j, :, HALF:]
        pair = pl.ds(2 * i, 2)
        writes.append(pltpu.make_async_copy(by_z.at[pair], by_z_hbm.at[pair], sems.at[0, i]))
        writes[-1].start()
        writes.append(pltpu.make_async_copy(by_y.at[:, pair], by_y_hbm.at[:, pair], sems.at[1, i]))
        writes[-1].start()
    for write in writes:
        write.wait()


def all_chunks(turned, grad_out):
    shapes = (NY, NZ, ROWS, HALF), (NZ, NY, ROWS, D - HALF)
    return pl.pallas_call(
        grad_kernel,
        in_specs=[VMEM, HBM],
        out_specs=[HBM, HBM],
        out_shape=[pltpu.HBM(s, BF16) for s in shapes],
        scratch_shapes=[pltpu.VMEM(s, BF16) for s in (grad_out.shape, *shapes)]
        + [pltpu.SemaphoreType.DMA, pltpu.SemaphoreType.DMA((2, NZ // 2))],
        compiler_params=vmem_limit(40),
    )(turned, grad_out)


def add_kernel(axis, k, chunks, up, down, up_out, down_out, above, below, sems):
    size, me = SIZES[axis], lax.axis_index(axis)
    first = pltpu.make_async_copy(chunks.at[(me + k) % size], above, sems.at[0])
    second = pltpu.make_async_copy(chunks.at[(me - k + size) % size], below, sems.at[1])
    first.start()
    second.start()
    rows, half = above.shape[0], up.shape[0]
    first.wait()
    up_out[:half] = above[:half] + up[...]
    if half < rows:
        up_out[half:] = above[half:]
    second.wait()
    rest = rows - down.shape[0]
    if rest:
        down_out[:rest] = below[:rest]
    down_out[rest:] = below[rest:] + down[...]


def ring_add(chunks, axis, k, up, down):
    shape = chunks.shape[1:]
    return pl.pallas_call(
        functools.partial(add_kernel, axis, k),
        in_specs=[HBM, VMEM, VMEM],
        out_specs=[VMEM, VMEM],
        out_shape=[jax.ShapeDtypeStruct(shape, BF16)] * 2,
        scratch_shapes=[pltpu.VMEM(shape, BF16)] * 2 + [pltpu.SemaphoreType.DMA((2,))],
        compiler_params=vmem_limit(16),
    )(chunks, up, down)


def total_kernel(axis, other, places, chunks, up, down, out, *refs):
    sends, (own, total, sem) = refs[: len(places)], refs[len(places) :]
    copy = pltpu.make_async_copy(chunks.at[lax.axis_index(axis)], own, sem)
    copy.start()
    copy.wait()
    total[...] = own[...].astype(F32) + up[...].astype(F32) + down[...].astype(F32)
    copy = pltpu.make_async_copy(total, out, sem)
    copy.start()
    for send, k in zip(sends, places):
        start = (lax.axis_index(other) + k + SIZES[other]) % SIZES[other] * ROWS
        send[...] = total[pl.ds(pl.multiple_of(start, ROWS), ROWS), :].astype(BF16)
    copy.wait()


def ring_total(chunks, axis, up, down, other, places):
    shape = chunks.shape[1:]
    total, *sends = pl.pallas_call(
        functools.partial(total_kernel, axis, other, places),
        in_specs=[HBM, VMEM, VMEM],
        out_specs=[HBM] + [VMEM] * len(places),
        out_shape=[pltpu.HBM(shape, F32)] + [jax.ShapeDtypeStruct((ROWS, shape[1]), BF16)] * len(places),
        scratch_shapes=[pltpu.VMEM(shape, BF16), pltpu.VMEM(shape, F32), pltpu.SemaphoreType.DMA],
        compiler_params=vmem_limit(16),
    )(chunks, up, down)
    return total.reshape(SIZES[other], ROWS, shape[1]), sends


def offsets(size):
    order = [0]
    for k in range(1, size // 2):
        order += [-k, k]
    return order + [size // 2]


def side_kernel(tokens_hbm, grad_hbm, next_hbm, near_hbm, rest_hbm, by_z_hbm, totals, *scratch):
    near, rest, by_z, tokens, grad, late, turned, sems = scratch
    pairs = (next_hbm, late), (grad_hbm, grad), (tokens_hbm, tokens)
    copies = [pltpu.make_async_copy(a, b, sems.at[i]) for i, (a, b) in enumerate(pairs)]
    for copy in copies:
        copy.start()
    copies[0].wait()
    turned[...] = late[...].T
    z, y = lax.axis_index("z"), lax.axis_index("y")
    for j in range(NY):

        @pl.when(y == j)
        def _():
            for i, far in enumerate(offsets(NZ)):
                start = pl.multiple_of((z + far + NZ) % NZ * ZROWS, ZROWS)
                block = turned[pl.ds(start, ZROWS), :]
                for k, off in enumerate(offsets(NY)):
                    at = (j + off) % NY * ROWS
                    by_z[i, k] = block[at : at + ROWS]
                    if i < NEAR:
                        near[k, i] = block[at : at + ROWS]
                    else:
                        rest[k, i - NEAR] = block[at : at + ROWS]

    pairs = (near, near_hbm), (rest, rest_hbm), (by_z, by_z_hbm)
    writes = [pltpu.make_async_copy(a, b, sems.at[i + 3]) for i, (a, b) in enumerate(pairs)]
    for write in writes:
        write.start()
    copies[1].wait()
    copies[2].wait()
    total = jnp.zeros((1, D), F32)
    for i in range(0, tokens.shape[0], 64):
        sums = jnp.sum(grad[i : i + 64, :].astype(F32), axis=1, keepdims=True)
        total += jnp.sum(tokens[i : i + 64, :].astype(F32) * sums, axis=0, keepdims=True)
    totals[...] = total
    for write in writes:
        write.wait()


def side_work(tokens, grad_out, next_tokens):
    count = tokens.shape[0]
    shapes = (NY, NEAR, ROWS, count), (NY, NZ - NEAR, ROWS, count), (NZ, NY, ROWS, count)
    *features, totals = pl.pallas_call(
        side_kernel,
        in_specs=[HBM] * 3,
        out_specs=[HBM] * 3 + [VMEM],
        out_shape=[pltpu.HBM(s, BF16) for s in shapes] + [jax.ShapeDtypeStruct((1, D), F32)],
        scratch_shapes=[pltpu.VMEM(s, BF16) for s in shapes]
        + [pltpu.VMEM((count, D), BF16)] * 3
        + [pltpu.VMEM((D, count), BF16), pltpu.SemaphoreType.DMA((6,))],
        compiler_params=vmem_limit(32),
    )(tokens, grad_out, next_tokens)
    slots = jnp.pad(totals.reshape(NZ * NY, ROWS), ((0, 0), (0, 128 - ROWS)))
    return [*features, jnp.repeat(slots, NX * NC, axis=0)]


def update_kernel(slots, first, second, master_hbm, momentum_hbm, *refs):
    new_master, new_momentum, one, two, checks, master, momentum, sems = refs
    copies = [
        pltpu.make_async_copy(master_hbm, master, sems.at[0]),
        pltpu.make_async_copy(momentum_hbm, momentum, sems.at[1]),
    ]
    for copy in copies:
        copy.start()
    lane = lax.broadcasted_iota(jnp.int32, slots.shape, 1)
    row = lax.broadcasted_iota(jnp.int32, slots.shape, 0)
    place = lax.axis_index("x") * NC + lax.axis_index("c")
    values = slots[...]
    squares = jnp.sum(jnp.where(lane == ROWS, values, 0.0), axis=(0, 1), keepdims=True)
    clip_factor = jnp.minimum(1.0, 1.0 / jnp.sqrt(squares / (D * FF) + 1e-06))
    row_sum = jnp.sum(jnp.where(row % (NX * NC) == place, values, 0.0), axis=0, keepdims=True)
    checks[...] = (clip_factor * row_sum / float(D) ** 0.5)[:, :ROWS]
    for copy in copies:
        copy.wait()
    for grad, start in ((first, 0), (second, HALF)):
        at = pl.ds(start, grad.shape[1])
        fresh = 0.9 * momentum[:, at] + clip_factor * grad[...]
        new_momentum[:, at] = fresh
        new_master[:, at] = master[:, at] - 0.01 * fresh
    one[...] = new_master[:, :WIDE].astype(BF16)
    two[...] = new_master[:, WIDE:].astype(BF16)


def update(slots, first, second, master, momentum):
    shapes = [(master.shape, F32)] * 2 + [((ROWS, WIDE), BF16), ((ROWS, D - WIDE), BF16), ((1, ROWS), F32)]
    return pl.pallas_call(
        update_kernel,
        in_specs=[VMEM] * 3 + [HBM] * 2,
        out_specs=[VMEM] * 5,
        out_shape=[jax.ShapeDtypeStruct(*s) for s in shapes],
        scratch_shapes=[pltpu.VMEM(master.shape, F32)] * 2 + [pltpu.SemaphoreType.DMA((2,))],
        compiler_params=vmem_limit(16),
    )(slots, first, second, *(pltpu.with_memory_space_constraint(a, pltpu.HBM) for a in (master, momentum)))


def stack_kernel(groups, *refs):
    refs = list(refs)
    outs = refs[len(refs) - len(groups) :]
    for group, out in zip(groups, outs):
        at = 0
        for start, stop in group:
            out[at : at + stop - start, :] = refs.pop(0)[start:stop, :]
            at += stop - start


def stack(*groups):
    ranges = [[(start, stop) for _, start, stop in group] for group in groups]
    blocks = [block for group in groups for block, _, _ in group]
    rows = [sum(stop - start for start, stop in group) for group in ranges]
    return pl.pallas_call(
        functools.partial(stack_kernel, ranges),
        in_specs=[VMEM] * len(blocks),
        out_specs=[VMEM] * len(groups),
        out_shape=[
            jax.ShapeDtypeStruct((count, group[0][0].shape[1]), BF16) for count, group in zip(rows, groups)
        ],
        compiler_params=vmem_limit(16),
    )(*blocks)


def whole(*blocks):
    return [(block, 0, block.shape[0]) for block in blocks]


def chunk_of(chunks, axis):
    size = SIZES[axis]
    me = lax.axis_index(axis)
    return lambda k: lax.dynamic_index_in_dim(chunks, (me + k) % size, 0, keepdims=False).astype(F32)


def scatter_rounds(chunks, axis, up, down, ready, come):
    up, down = lax.optimization_barrier((up, down))
    for k in range(SIZES[axis] // 2 - 1, 0, -1):
        up, down = ready(k, *ring_add(chunks, axis, k, up, down))
        up, down = come(k, shift(up, axis, 1), shift(down, axis, -1))
    return up, down


def short_last(chunk, far, up, down):
    up = chunk(2) + far.astype(F32) + up.astype(F32)
    for k in (2, 1):
        down = chunk(-k) + down.astype(F32)
        up, down = shift(up.astype(BF16), "z", 1), shift(down.astype(BF16), "z", -1)
        up, down = lax.optimization_barrier((up, down))
        up = chunk(k - 1) + up.astype(F32)
    return up + down.astype(F32)


def product(features, *blocks):
    return lax.dot_general(
        features.reshape(-1, features.shape[-1]), jnp.concatenate(blocks),
        (((0,), (0,)), ((), ())), preferred_element_type=F32,
    )


def together(k, *values):
    return lax.optimization_barrier(values)


def local(tokens, grad_out, next_tokens, master, momentum):
    far_tokens = pltpu.with_memory_space_constraint(tokens, pltpu.HBM)
    far_grad = pltpu.with_memory_space_constraint(grad_out, pltpu.HBM)
    up1, down1, up2, down2, turned = far_chunks(far_tokens, far_grad)
    up2, down2 = shift(up2, "z", 1), shift(down2, "z", -1)
    up1, down1 = shift(up1, "y", 1), shift(down1, "y", -1)
    by_y, by_z = all_chunks(turned, far_grad)

    by_y = pltpu.with_memory_space_constraint(by_y.reshape(NY, YROWS, HALF), pltpu.HBM)
    by_z = pltpu.with_memory_space_constraint(by_z.reshape(NZ, ZROWS, D - HALF), pltpu.HBM)

    aside, held = [], []

    def ready_first(k, up, down):
        return up, down

    def ready_second(k, up, down):
        if k == 2:
            up, down, *late = together(k, up, down, tokens, grad_out, next_tokens)
            late = [pltpu.with_memory_space_constraint(a, pltpu.HBM) for a in late]
            aside.extend(side_work(*late))
        elif k == 1:
            held[:] = together(k, *held, up, down)[:3]
        return up, down

    def come_second(k, up, down):
        if k == 2:
            up, down, *aside[:] = together(k, up, down, *aside)
            return up, down
        return together(k, up, down)

    first = scatter_rounds(by_y, "y", up1, down1, ready_first, together)
    first, held[:] = ring_total(by_y, "y", *first, "z", (4, 3, -3))
    second = scatter_rounds(by_z, "z", up2, down2, ready_second, come_second)
    second, sends = ring_total(by_z, "z", *second, "y", (1, -1, 2))
    held = [shift(send, "z", k) for send, k in zip(held, (2, 1, -1))]
    *held, _ = together(0, *held, sends[0])
    first = short_last(chunk_of(first, "z"), *held)
    sends = together(0, *(shift(send, "y", k) for send, k in zip(sends, (1, -1, 2))))
    second = chunk_of(second, "y")(0) + sum(send.astype(F32) for send in sends)
    near, rest, by_z, slots = aside

    squares = jnp.sum(first * first) + jnp.sum(second * second)
    slots = jnp.where(lax.broadcasted_iota(jnp.int32, slots.shape, 1) < ROWS, slots, squares)
    slots = lax.all_to_all(slots, ("z", "y", "x", "c"), split_axis=0, concat_axis=0, tiled=True)
    new_master, new_momentum, one, two, row_checks = update(slots, first, second, master, momentum)

    up1, down1, *twos = together(
        1, shift(one, "z", 1), shift(one, "z", -1), shift(two, "y", 1), shift(two, "y", -1), shift(two, "y", 2)
    )
    ones = [one, up1, down1]
    (two,) = stack(whole(two, *twos))
    up1, down1, two = together(2, shift(up1, "z", 1), shift(down1, "z", -1), two)
    (one_near,) = stack(whole(*ones, up1, down1))

    up1 = shift(up1, "z", 1)
    up3, down3 = shift(one_near, "y", 1), shift(one_near, "y", -1)
    up2, down2 = shift(two, "z", 1), shift(two, "z", -1)
    up2, down2, down1 = together(1, up2, down2, down1)
    arrived = [(up2, down2)]
    ones = [up1, shift(down1, "z", -1), shift(up1, "z", 1)]
    up2, down2 = together(2, shift(up2, "z", 1), shift(down2, "z", -1))
    arrived.append((up2, down2))
    up3, down3 = together(1, up3, down3)
    count = NEAR * ROWS
    one_rest, up4, down4 = stack(
        whole(*ones), [*whole(*ones), (up3, 0, CUT)], [*whole(*ones), (down3, CUT, count)]
    )
    up4, down4 = shift(up4, "y", 1), shift(down4, "y", -1)
    up2, down2 = shift(up2, "z", 1), shift(down2, "z", -1)
    up2, down2, up4, down4 = together(3, up2, down2, up4, down4)
    arrived.append((up2, down2))
    count = (NZ - NEAR) * ROWS
    cut = count // 16 * 8
    sends = stack(
        [(up4, 0, cut)], [(down4, cut, count)], [(up2, 0, ZROWS // 2)], [(down2, ZROWS // 2, ZROWS)]
    )
    far4 = shift(sends[0], "y", 1), shift(sends[1], "y", -1)
    far2 = shift(sends[2], "z", 1), shift(sends[3], "z", -1)
    sides4, far3 = stack(
        [(up4, 0, count), (down4, 0, count)],
        [(up4, count, up4.shape[0]), (down4, count, down4.shape[0])],
    )
    out_two = product(by_z[0], two)
    for k, blocks in enumerate(arrived):
        out_two += product(by_z[2 * k + 1 : 2 * k + 3], *blocks)
    out_two += product(by_z[NZ - 1], *far2)
    out_one = product(near[0], one_near) + product(rest[0], one_rest)
    out_one += product(near[1:3], up3, down3)
    out_one += product(near[3], far3)
    out_one += product(rest[1:3], sides4)
    out_one += product(rest[3], *far4)
    forward = jnp.concatenate([out_one, out_two], axis=1).astype(BF16)
    return new_master, new_momentum, forward, row_checks


def solution(mesh):
    split = Mesh(mesh.devices.reshape(NZ, NY, NX, NC), ("z", "y", "x", "c"))
    dp, mp = ("z", "y"), ("x", "c")
    in_specs = (P(dp, None), P(dp, mp), P(dp, None), P(dp, mp), P(dp, mp))
    out_specs = (P(dp, mp), P(dp, mp), P(dp, mp), P(mp, dp))
    return jax.shard_map(local, mesh=split, in_specs=in_specs, out_specs=out_specs, check_vma=False)
```

```python
import functools

import jax
import jax.numpy as jnp
from jax import lax
from jax.experimental import pallas as pl
from jax.experimental.pallas import tpu as pltpu
from jax.sharding import Mesh, PartitionSpec as P

D = 2304
FF = 18432
NZ, NY, NX, NC = 8, 4, 4, 2
SIZES = {"z": NZ, "y": NY, "x": NX, "c": NC}
ROWS = D // (NZ * NY)
YROWS, ZROWS = NZ * ROWS, NY * ROWS
HALF = 1152
WIDE = 1280
NEAR = 5
CUT = 192
F32, BF16 = jnp.float32, jnp.bfloat16
HBM = pl.BlockSpec(memory_space=pltpu.HBM)
VMEM = pl.BlockSpec(memory_space=pltpu.VMEM)


def vmem_limit(mib):
    return pltpu.CompilerParams(vmem_limit_bytes=mib * 1024 * 1024)


def in_hbm(value):
    return pltpu.with_memory_space_constraint(value, pltpu.HBM)


def shift(value, axis, by):
    size = SIZES[axis]
    return lax.ppermute(value, axis, [(i, (i + by) % size) for i in range(size)])


def far_kernel(tokens_hbm, grad_hbm, up_y, down_y, up_z, down_z, turned, tokens, grad, sems):
    first = pltpu.make_async_copy(tokens_hbm, tokens, sems.at[0])
    second = pltpu.make_async_copy(grad_hbm, grad, sems.at[1])
    first.start()
    second.start()
    first.wait()
    turned[...] = tokens[...].T
    second.wait()
    z = (lax.axis_index("z") + NZ // 2) % NZ
    y = (lax.axis_index("y") + NY // 2) % NY
    rows = turned[pl.ds(pl.multiple_of(z * ZROWS, ZROWS), ZROWS), :]
    part = jnp.dot(rows, grad[:, HALF:], preferred_element_type=F32).astype(BF16)
    up_z[...] = part[: ZROWS // 2]
    down_z[...] = part[ZROWS // 2 :]
    for j in range(NY):

        @pl.when(y == j)
        def _():
            starts = [i * ZROWS + j * ROWS for i in range(NZ)]
            rows = jnp.concatenate([turned[s : s + ROWS, :] for s in starts])
            part = jnp.dot(rows, grad[:, :HALF], preferred_element_type=F32).astype(BF16)
            up_y[...] = part[: YROWS // 2]
            down_y[...] = part[YROWS // 2 :]


def far_chunks(tokens, grad_out):
    count = tokens.shape[0]
    shapes = [(YROWS // 2, HALF)] * 2 + [(ZROWS // 2, D - HALF)] * 2 + [(D, count)]
    return pl.pallas_call(
        far_kernel,
        in_specs=[HBM, HBM],
        out_specs=[VMEM] * 5,
        out_shape=[jax.ShapeDtypeStruct(s, BF16) for s in shapes],
        scratch_shapes=[
            pltpu.VMEM(tokens.shape, BF16),
            pltpu.VMEM(grad_out.shape, BF16),
            pltpu.SemaphoreType.DMA((2,)),
        ],
        compiler_params=vmem_limit(24),
    )(tokens, grad_out)


def grad_kernel(turned, grad_hbm, by_y_hbm, by_z_hbm, grad, by_y, by_z, sem, sems):
    whole = pltpu.make_async_copy(grad_hbm, grad, sem)
    whole.start()
    whole.wait()
    step = 2 * ZROWS
    writes = []
    for i in range(NZ // 2):
        part = jnp.dot(turned[i * step : (i + 1) * step, :], grad[...], preferred_element_type=F32)
        part = part.astype(BF16).reshape(2, NY, ROWS, D)
        for k in range(2):
            for j in range(NY):
                by_y[j, 2 * i + k] = part[k, j, :, :HALF]
                by_z[2 * i + k, j] = part[k, j, :, HALF:]
        pair = pl.ds(2 * i, 2)
        writes.append(pltpu.make_async_copy(by_z.at[pair], by_z_hbm.at[pair], sems.at[0, i]))
        writes[-1].start()
        writes.append(pltpu.make_async_copy(by_y.at[:, pair], by_y_hbm.at[:, pair], sems.at[1, i]))
        writes[-1].start()
    for write in writes:
        write.wait()


def all_chunks(turned, grad_out):
    shapes = (NY, NZ, ROWS, HALF), (NZ, NY, ROWS, D - HALF)
    return pl.pallas_call(
        grad_kernel,
        in_specs=[VMEM, HBM],
        out_specs=[HBM, HBM],
        out_shape=[pltpu.HBM(s, BF16) for s in shapes],
        scratch_shapes=[pltpu.VMEM(s, BF16) for s in (grad_out.shape, *shapes)]
        + [pltpu.SemaphoreType.DMA, pltpu.SemaphoreType.DMA((2, NZ // 2))],
        compiler_params=vmem_limit(32),
    )(turned, grad_out)


def add_kernel(axis, k, chunks, up, down, up_out, down_out, above, below, sems):
    size, me = SIZES[axis], lax.axis_index(axis)
    first = pltpu.make_async_copy(chunks.at[(me + k) % size], above, sems.at[0])
    second = pltpu.make_async_copy(chunks.at[(me - k + size) % size], below, sems.at[1])
    first.start()
    second.start()
    rows, half = above.shape[0], up.shape[0]
    first.wait()
    up_out[:half] = above[:half] + up[...]
    if half < rows:
        up_out[half:] = above[half:]
    second.wait()
    rest = rows - down.shape[0]
    if rest:
        down_out[:rest] = below[:rest]
    down_out[rest:] = below[rest:] + down[...]


def ring_add(chunks, axis, k, up, down):
    shape = chunks.shape[1:]
    return pl.pallas_call(
        functools.partial(add_kernel, axis, k),
        in_specs=[HBM, VMEM, VMEM],
        out_specs=[VMEM, VMEM],
        out_shape=[jax.ShapeDtypeStruct(shape, BF16)] * 2,
        scratch_shapes=[pltpu.VMEM(shape, BF16)] * 2 + [pltpu.SemaphoreType.DMA((2,))],
        compiler_params=vmem_limit(16),
    )(chunks, up, down)


def total_kernel(axis, other, places, chunks, up, down, out, *refs):
    sends, (own, total, sem) = refs[: len(places)], refs[len(places) :]
    copy = pltpu.make_async_copy(chunks.at[lax.axis_index(axis)], own, sem)
    copy.start()
    copy.wait()
    total[...] = own[...].astype(F32) + up[...].astype(F32) + down[...].astype(F32)
    copy = pltpu.make_async_copy(total, out, sem)
    copy.start()
    for send, k in zip(sends, places):
        start = (lax.axis_index(other) + k + SIZES[other]) % SIZES[other] * ROWS
        send[...] = total[pl.ds(pl.multiple_of(start, ROWS), ROWS), :].astype(BF16)
    copy.wait()


def ring_total(chunks, axis, up, down, other, places):
    shape = chunks.shape[1:]
    total, *sends = pl.pallas_call(
        functools.partial(total_kernel, axis, other, places),
        in_specs=[HBM, VMEM, VMEM],
        out_specs=[HBM] + [VMEM] * len(places),
        out_shape=[pltpu.HBM(shape, F32)] + [jax.ShapeDtypeStruct((ROWS, shape[1]), BF16)] * len(places),
        scratch_shapes=[pltpu.VMEM(shape, BF16), pltpu.VMEM(shape, F32), pltpu.SemaphoreType.DMA],
        compiler_params=vmem_limit(16),
    )(chunks, up, down)
    return total.reshape(SIZES[other], ROWS, shape[1]), sends


def offsets(size):
    order = [0]
    for k in range(1, size // 2):
        order += [-k, k]
    return order + [size // 2]


def side_kernel(tokens_hbm, grad_hbm, next_hbm, near_hbm, rest_hbm, by_z_hbm, slots, *scratch):
    near, rest, by_z, tokens, grad, late, turned, sems = scratch
    pairs = (next_hbm, late), (grad_hbm, grad), (tokens_hbm, tokens)
    copies = [pltpu.make_async_copy(a, b, sems.at[i]) for i, (a, b) in enumerate(pairs)]
    for copy in copies:
        copy.start()
    copies[0].wait()
    turned[...] = late[...].T
    z, y = lax.axis_index("z"), lax.axis_index("y")
    for j in range(NY):

        @pl.when(y == j)
        def _():
            for i, far in enumerate(offsets(NZ)):
                start = pl.multiple_of((z + far + NZ) % NZ * ZROWS, ZROWS)
                block = turned[pl.ds(start, ZROWS), :]
                for k, off in enumerate(offsets(NY)):
                    at = (j + off) % NY * ROWS
                    by_z[i, k] = block[at : at + ROWS]
                    if i < NEAR:
                        near[k, i] = block[at : at + ROWS]
                    else:
                        rest[k, i - NEAR] = block[at : at + ROWS]

    pairs = (near, near_hbm), (rest, rest_hbm), (by_z, by_z_hbm)
    writes = [pltpu.make_async_copy(a, b, sems.at[i + 3]) for i, (a, b) in enumerate(pairs)]
    for write in writes:
        write.start()
    copies[1].wait()
    copies[2].wait()
    total = jnp.zeros((1, D), F32)
    for i in range(0, tokens.shape[0], 64):
        sums = jnp.sum(grad[i : i + 64, :].astype(F32), axis=1, keepdims=True)
        total += jnp.sum(tokens[i : i + 64, :].astype(F32) * sums, axis=0, keepdims=True)
    slots[...] = jnp.zeros_like(slots)
    for i in range(NZ * NY):
        row = jnp.broadcast_to(total[:, i * ROWS : (i + 1) * ROWS], (NX * NC, ROWS))
        slots[i * NX * NC : (i + 1) * NX * NC, :ROWS] = row
    for write in writes:
        write.wait()


def side_work(tokens, grad_out, next_tokens):
    count = tokens.shape[0]
    shapes = (NY, NEAR, ROWS, count), (NY, NZ - NEAR, ROWS, count), (NZ, NY, ROWS, count)
    return pl.pallas_call(
        side_kernel,
        in_specs=[HBM] * 3,
        out_specs=[HBM] * 3 + [VMEM],
        out_shape=[pltpu.HBM(s, BF16) for s in shapes] + [jax.ShapeDtypeStruct((FF // D * NZ * NY, 128), F32)],
        scratch_shapes=[pltpu.VMEM(s, BF16) for s in shapes]
        + [pltpu.VMEM((count, D), BF16)] * 3
        + [pltpu.VMEM((D, count), BF16), pltpu.SemaphoreType.DMA((6,))],
        compiler_params=vmem_limit(24),
    )(tokens, grad_out, next_tokens)


def finish_kernel(first_hbm, up, down, second_hbm, near, past, far, slots_in, first, second, slots, *scratch):
    own, other, sems = scratch
    copies = [
        pltpu.make_async_copy(first_hbm.at[lax.axis_index("z")], own, sems.at[0]),
        pltpu.make_async_copy(second_hbm.at[lax.axis_index("y")], other, sems.at[1]),
    ]
    for copy in copies:
        copy.start()
    for copy in copies:
        copy.wait()
    first[...] = own[...] + up[...].astype(F32) + down[...].astype(F32)
    sent = near[...].astype(F32) + past[...].astype(F32) + far[...].astype(F32)
    second[...] = other[...] + sent
    squares = jnp.sum(first[...] * first[...], axis=(0, 1), keepdims=True)
    squares += jnp.sum(second[...] * second[...], axis=(0, 1), keepdims=True)
    lane = lax.broadcasted_iota(jnp.int32, slots.shape, 1)
    slots[...] = jnp.where(lane < ROWS, slots_in[...], squares)


def finish(first, up, down, second, sends, slots):
    shapes = first.shape[1:], second.shape[1:], slots.shape
    return pl.pallas_call(
        finish_kernel,
        in_specs=[HBM, VMEM, VMEM, HBM] + [VMEM] * 4,
        out_specs=[VMEM] * 3,
        out_shape=[jax.ShapeDtypeStruct(s, F32) for s in shapes],
        scratch_shapes=[pltpu.VMEM(s, F32) for s in shapes[:2]] + [pltpu.SemaphoreType.DMA((2,))],
        compiler_params=vmem_limit(12),
    )(in_hbm(first), up, down, in_hbm(second), *sends, slots)


def update_kernel(slots, first, second, master_hbm, momentum_hbm, *refs):
    new_master, new_momentum, one, two, checks, master, momentum, sems = refs
    copies = [
        pltpu.make_async_copy(master_hbm, master, sems.at[0]),
        pltpu.make_async_copy(momentum_hbm, momentum, sems.at[1]),
    ]
    for copy in copies:
        copy.start()
    lane = lax.broadcasted_iota(jnp.int32, slots.shape, 1)
    row = lax.broadcasted_iota(jnp.int32, slots.shape, 0)
    place = lax.axis_index("x") * NC + lax.axis_index("c")
    values = slots[...]
    squares = jnp.sum(jnp.where(lane == ROWS, values, 0.0), axis=(0, 1), keepdims=True)
    clip_factor = jnp.minimum(1.0, 1.0 / jnp.sqrt(squares / (D * FF) + 1e-06))
    row_sum = jnp.sum(jnp.where(row % (NX * NC) == place, values, 0.0), axis=0, keepdims=True)
    checks[...] = (clip_factor * row_sum / float(D) ** 0.5)[:, :ROWS]
    for copy in copies:
        copy.wait()
    for grad, start in ((first, 0), (second, HALF)):
        at = pl.ds(start, grad.shape[1])
        fresh = 0.9 * momentum[:, at] + clip_factor * grad[...]
        new_momentum[:, at] = fresh
        new_master[:, at] = master[:, at] - 0.01 * fresh
    one[...] = new_master[:, :WIDE].astype(BF16)
    two[...] = new_master[:, WIDE:].astype(BF16)


def update(slots, first, second, master, momentum):
    shapes = [(master.shape, F32)] * 2 + [((ROWS, WIDE), BF16), ((ROWS, D - WIDE), BF16), ((1, ROWS), F32)]
    return pl.pallas_call(
        update_kernel,
        in_specs=[VMEM] * 3 + [HBM] * 2,
        out_specs=[VMEM] * 5,
        out_shape=[jax.ShapeDtypeStruct(*s) for s in shapes],
        scratch_shapes=[pltpu.VMEM(master.shape, F32)] * 2 + [pltpu.SemaphoreType.DMA((2,))],
        compiler_params=vmem_limit(16),
    )(slots, first, second, in_hbm(master), in_hbm(momentum))


def stack_kernel(groups, *refs):
    refs = list(refs)
    outs = refs[len(refs) - len(groups) :]
    for group, out in zip(groups, outs):
        at = 0
        for start, stop in group:
            out[at : at + stop - start, :] = refs.pop(0)[start:stop, :]
            at += stop - start


def stack(*groups):
    ranges = [[(start, stop) for _, start, stop in group] for group in groups]
    blocks = [block for group in groups for block, _, _ in group]
    rows = [sum(stop - start for start, stop in group) for group in ranges]
    return pl.pallas_call(
        functools.partial(stack_kernel, ranges),
        in_specs=[VMEM] * len(blocks),
        out_specs=[VMEM] * len(groups),
        out_shape=[
            jax.ShapeDtypeStruct((count, group[0][0].shape[1]), BF16) for count, group in zip(rows, groups)
        ],
        compiler_params=vmem_limit(16),
    )(*blocks)


def whole(*blocks):
    return [(block, 0, block.shape[0]) for block in blocks]


def chunk_of(chunks, axis):
    size = SIZES[axis]
    me = lax.axis_index(axis)
    return lambda k: lax.dynamic_index_in_dim(chunks, (me + k) % size, 0, keepdims=False).astype(F32)


def scatter_rounds(chunks, axis, up, down, ready, come):
    up, down = lax.optimization_barrier((up, down))
    for k in range(SIZES[axis] // 2 - 1, 0, -1):
        up, down = ready(k, *ring_add(chunks, axis, k, up, down))
        up, down = come(k, shift(up, axis, 1), shift(down, axis, -1))
    return up, down


def jump(value):
    return lax.ppermute(value, "z", [(i, (i + 2 - i % 2 * 4) % NZ) for i in range(NZ)])


def short_ring(chunk, far, up, down):
    far, even = far.astype(F32), lax.axis_index("z") % 2 == 0
    up = chunk(2) + up.astype(F32) + jnp.where(even, far, 0.0)
    down = chunk(-2) + down.astype(F32) + jnp.where(even, 0.0, far)
    up, down = shift(up.astype(BF16), "z", 1), shift(down.astype(BF16), "z", -1)
    up, down = lax.optimization_barrier((up, down))
    up, down = chunk(1) + up.astype(F32), chunk(-1) + down.astype(F32)
    up, down = shift(up.astype(BF16), "z", 1), shift(down.astype(BF16), "z", -1)
    return lax.optimization_barrier((up, down))


def product(features, *blocks):
    return lax.dot_general(
        features.reshape(-1, features.shape[-1]), jnp.concatenate(blocks),
        (((0,), (0,)), ((), ())), preferred_element_type=F32,
    )


def together(k, *values):
    return lax.optimization_barrier(values)


def local(tokens, grad_out, next_tokens, master, momentum):
    far_tokens = in_hbm(tokens)
    far_grad = in_hbm(grad_out)
    up1, down1, up2, down2, turned = far_chunks(far_tokens, far_grad)
    up2, down2 = shift(up2, "z", 1), shift(down2, "z", -1)
    up1, down1 = shift(up1, "y", 1), shift(down1, "y", -1)
    by_y, by_z = all_chunks(turned, far_grad)

    by_y = in_hbm(by_y.reshape(NY, YROWS, HALF))
    by_z = in_hbm(by_z.reshape(NZ, ZROWS, D - HALF))

    aside, held = [], []

    def ready_first(k, up, down):
        return up, down

    def ready_second(k, up, down):
        if k == 2:
            up, down, *late = together(k, up, down, tokens, grad_out, next_tokens)
            aside.extend(side_work(*map(in_hbm, late)))
        elif k == 1:
            held[:] = together(k, *held, up, down)[:3]
        return up, down

    def come_second(k, up, down):
        if k == 2:
            up, down, *aside[:] = together(k, up, down, *aside)
            return up, down
        return together(k, up, down)

    first = scatter_rounds(by_y, "y", up1, down1, ready_first, together)
    first, held[:] = ring_total(by_y, "y", *first, "z", (4, 3, -3))
    second = scatter_rounds(by_z, "z", up2, down2, ready_second, come_second)
    second, sends = ring_total(by_z, "z", *second, "y", (1, -1, 2))
    held = [jump(held[0]), shift(held[1], "z", 1), shift(held[2], "z", -1)]
    *held, _ = together(0, *held, sends[0])
    up, down = short_ring(chunk_of(first, "z"), *held)
    sends = together(0, *(shift(send, "y", k) for send, k in zip(sends, (1, -1, 2))))
    near, rest, by_z, slots = aside

    first, second, slots = finish(first, up, down, second, sends, slots)
    slots = lax.all_to_all(slots, ("z", "y", "x", "c"), split_axis=0, concat_axis=0, tiled=True)
    new_master, new_momentum, one, two, row_checks = update(slots, first, second, master, momentum)

    up1, down1, *twos = together(
        1, shift(one, "z", 1), shift(one, "z", -1), shift(two, "y", 1), shift(two, "y", -1), shift(two, "y", 2)
    )
    ones = [one, up1, down1]
    (two,) = stack(whole(two, *twos))
    up1, down1, two = together(2, shift(up1, "z", 1), shift(down1, "z", -1), two)
    (one_near,) = stack(whole(*ones, up1, down1))

    up1 = shift(up1, "z", 1)
    up3, down3 = shift(one_near, "y", 1), shift(one_near, "y", -1)
    up2, down2 = shift(two, "z", 1), shift(two, "z", -1)
    up2, down2, down1 = together(1, up2, down2, down1)
    arrived = [(up2, down2)]
    ones = [up1, shift(down1, "z", -1), shift(up1, "z", 1)]
    up2, down2 = together(2, shift(up2, "z", 1), shift(down2, "z", -1))
    arrived.append((up2, down2))
    up3, down3 = together(1, up3, down3)
    count = NEAR * ROWS
    one_rest, up4, down4 = stack(
        whole(*ones), [*whole(*ones), (up3, 0, CUT)], [*whole(*ones), (down3, CUT, count)]
    )
    up4, down4 = shift(up4, "y", 1), shift(down4, "y", -1)
    up2, down2 = shift(up2, "z", 1), shift(down2, "z", -1)
    up2, down2, up4, down4 = together(3, up2, down2, up4, down4)
    arrived.append((up2, down2))
    count = (NZ - NEAR) * ROWS
    cut = count // 16 * 8
    ends2 = stack([(up2, 0, ZROWS // 2)], [(down2, ZROWS // 2, ZROWS)])
    up4, down4, *ends2 = together(4, up4, down4, *ends2)
    ends4 = stack([(up4, 0, cut)], [(down4, cut, count)])
    far2 = shift(ends2[0], "z", 1), shift(ends2[1], "z", -1)
    far4 = shift(ends4[0], "y", 1), shift(ends4[1], "y", -1)
    sides4, far3 = stack(
        [(up4, 0, count), (down4, 0, count)],
        [(up4, count, up4.shape[0]), (down4, count, down4.shape[0])],
    )
    out_two = product(by_z[0], two)
    for k, blocks in enumerate(arrived):
        out_two += product(by_z[2 * k + 1 : 2 * k + 3], *blocks)
    out_two += product(by_z[NZ - 1], *far2)
    out_one = product(near[0], one_near) + product(rest[0], one_rest)
    out_one += product(near[1:3], up3, down3)
    out_one += product(near[3], far3)
    out_one += product(rest[1:3], sides4)
    out_one += product(rest[3], *far4)
    forward = jnp.concatenate([out_one, out_two], axis=1).astype(BF16)
    return new_master, new_momentum, forward, row_checks


def solution(mesh):
    split = Mesh(mesh.devices.reshape(NZ, NY, NX, NC), ("z", "y", "x", "c"))
    dp, mp = ("z", "y"), ("x", "c")
    in_specs = (P(dp, None), P(dp, mp), P(dp, None), P(dp, mp), P(dp, mp))
    out_specs = (P(dp, mp), P(dp, mp), P(dp, mp), P(mp, dp))
    return jax.shard_map(local, mesh=split, in_specs=in_specs, out_specs=out_specs, check_vma=False)
```

```python
import functools

import jax
import jax.numpy as jnp
from jax import lax
from jax.experimental import pallas as pl
from jax.experimental.pallas import tpu as pltpu
from jax.sharding import Mesh, PartitionSpec as P

D = 2304
FF = 18432
NZ, NY, NX, NC = 8, 4, 4, 2
SIZES = {"z": NZ, "y": NY, "x": NX, "c": NC}
ROWS = D // (NZ * NY)
YROWS, ZROWS = NZ * ROWS, NY * ROWS
HALF = 1152
WIDE = 1280
GROUPS = (0, -1, 1), (-2, 2), (-3, 3, 4)
CUTS = 112, 72, 112
F32, BF16 = jnp.float32, jnp.bfloat16
HBM = pl.BlockSpec(memory_space=pltpu.HBM)
VMEM = pl.BlockSpec(memory_space=pltpu.VMEM)


def vmem_limit(mib):
    return pltpu.CompilerParams(vmem_limit_bytes=mib * 1024 * 1024)


def in_hbm(value):
    return pltpu.with_memory_space_constraint(value, pltpu.HBM)


def shift(value, axis, by):
    size = SIZES[axis]
    return lax.ppermute(value, axis, [(i, (i + by) % size) for i in range(size)])


def far_kernel(tokens_hbm, grad_hbm, up_y, down_y, up_z, down_z, turned, tokens, grad, sems):
    first = pltpu.make_async_copy(tokens_hbm, tokens, sems.at[0])
    second = pltpu.make_async_copy(grad_hbm, grad, sems.at[1])
    first.start()
    second.start()
    first.wait()
    turned[...] = tokens[...].T
    second.wait()
    z = (lax.axis_index("z") + NZ // 2) % NZ
    y = (lax.axis_index("y") + NY // 2) % NY
    rows = turned[pl.ds(pl.multiple_of(z * ZROWS, ZROWS), ZROWS), :]
    part = jnp.dot(rows, grad[:, HALF:], preferred_element_type=F32).astype(BF16)
    up_z[...] = part[: ZROWS // 2]
    down_z[...] = part[ZROWS // 2 :]
    for j in range(NY):

        @pl.when(y == j)
        def _():
            starts = [i * ZROWS + j * ROWS for i in range(NZ)]
            rows = jnp.concatenate([turned[s : s + ROWS, :] for s in starts])
            part = jnp.dot(rows, grad[:, :HALF], preferred_element_type=F32).astype(BF16)
            up_y[...] = part[: YROWS // 2]
            down_y[...] = part[YROWS // 2 :]


def far_chunks(tokens, grad_out):
    count = tokens.shape[0]
    shapes = [(YROWS // 2, HALF)] * 2 + [(ZROWS // 2, D - HALF)] * 2 + [(D, count)]
    return pl.pallas_call(
        far_kernel,
        in_specs=[HBM, HBM],
        out_specs=[VMEM] * 5,
        out_shape=[jax.ShapeDtypeStruct(s, BF16) for s in shapes],
        scratch_shapes=[
            pltpu.VMEM(tokens.shape, BF16),
            pltpu.VMEM(grad_out.shape, BF16),
            pltpu.SemaphoreType.DMA((2,)),
        ],
        compiler_params=vmem_limit(24),
    )(tokens, grad_out)


def grad_kernel(turned, grad_hbm, by_y_hbm, by_z_hbm, grad, by_y, by_z, sem, sems):
    whole = pltpu.make_async_copy(grad_hbm, grad, sem)
    whole.start()
    whole.wait()
    step = 2 * ZROWS
    writes = []
    for i in range(NZ // 2):
        part = jnp.dot(turned[i * step : (i + 1) * step, :], grad[...], preferred_element_type=F32)
        part = part.astype(BF16).reshape(2, NY, ROWS, D)
        for k in range(2):
            for j in range(NY):
                by_y[j, 2 * i + k] = part[k, j, :, :HALF]
                by_z[2 * i + k, j] = part[k, j, :, HALF:]
        pair = pl.ds(2 * i, 2)
        writes.append(pltpu.make_async_copy(by_z.at[pair], by_z_hbm.at[pair], sems.at[0, i]))
        writes[-1].start()
        writes.append(pltpu.make_async_copy(by_y.at[:, pair], by_y_hbm.at[:, pair], sems.at[1, i]))
        writes[-1].start()
    for write in writes:
        write.wait()


def all_chunks(turned, grad_out):
    shapes = (NY, NZ, ROWS, HALF), (NZ, NY, ROWS, D - HALF)
    return pl.pallas_call(
        grad_kernel,
        in_specs=[VMEM, HBM],
        out_specs=[HBM, HBM],
        out_shape=[pltpu.HBM(s, BF16) for s in shapes],
        scratch_shapes=[pltpu.VMEM(s, BF16) for s in (grad_out.shape, *shapes)]
        + [pltpu.SemaphoreType.DMA, pltpu.SemaphoreType.DMA((2, NZ // 2))],
        compiler_params=vmem_limit(32),
    )(turned, grad_out)


def add_kernel(axis, k, chunks, up, down, up_out, down_out, above, below, sems):
    size, me = SIZES[axis], lax.axis_index(axis)
    first = pltpu.make_async_copy(chunks.at[(me + k) % size], above, sems.at[0])
    second = pltpu.make_async_copy(chunks.at[(me - k + size) % size], below, sems.at[1])
    first.start()
    second.start()
    rows, half = above.shape[0], up.shape[0]
    first.wait()
    up_out[:half] = above[:half] + up[...]
    if half < rows:
        up_out[half:] = above[half:]
    second.wait()
    rest = rows - down.shape[0]
    if rest:
        down_out[:rest] = below[:rest]
    down_out[rest:] = below[rest:] + down[...]


def ring_add(chunks, axis, k, up, down):
    shape = chunks.shape[1:]
    return pl.pallas_call(
        functools.partial(add_kernel, axis, k),
        in_specs=[HBM, VMEM, VMEM],
        out_specs=[VMEM, VMEM],
        out_shape=[jax.ShapeDtypeStruct(shape, BF16)] * 2,
        scratch_shapes=[pltpu.VMEM(shape, BF16)] * 2 + [pltpu.SemaphoreType.DMA((2,))],
        compiler_params=vmem_limit(16),
    )(chunks, up, down)


def total_kernel(axis, other, places, chunks, up, down, out, *refs):
    sends, (own, total, sem) = refs[: len(places)], refs[len(places) :]
    copy = pltpu.make_async_copy(chunks.at[lax.axis_index(axis)], own, sem)
    copy.start()
    copy.wait()
    total[...] = own[...].astype(F32) + up[...].astype(F32) + down[...].astype(F32)
    copy = pltpu.make_async_copy(total, out, sem)
    copy.start()
    for send, k in zip(sends, places):
        start = (lax.axis_index(other) + k + SIZES[other]) % SIZES[other] * ROWS
        send[...] = total[pl.ds(pl.multiple_of(start, ROWS), ROWS), :].astype(BF16)
    copy.wait()


def ring_total(chunks, axis, up, down, other, places):
    shape = chunks.shape[1:]
    total, *sends = pl.pallas_call(
        functools.partial(total_kernel, axis, other, places),
        in_specs=[HBM, VMEM, VMEM],
        out_specs=[HBM] + [VMEM] * len(places),
        out_shape=[pltpu.HBM(shape, F32)] + [jax.ShapeDtypeStruct((ROWS, shape[1]), BF16)] * len(places),
        scratch_shapes=[pltpu.VMEM(shape, BF16), pltpu.VMEM(shape, F32), pltpu.SemaphoreType.DMA],
        compiler_params=vmem_limit(16),
    )(chunks, up, down)
    return total.reshape(SIZES[other], ROWS, shape[1]), sends


def offsets(size):
    order = [0]
    for k in range(1, size // 2):
        order += [-k, k]
    return order + [size // 2]


def side_kernel(tokens_hbm, grad_hbm, next_hbm, *refs):
    count = len(GROUPS) + 1
    by_group_hbm, (slots, *refs) = refs[:count], refs[count:]
    by_group, (tokens, grad, late, turned, sems) = refs[:count], refs[count:]
    *by_group, by_z = by_group
    pairs = (next_hbm, late), (grad_hbm, grad), (tokens_hbm, tokens)
    copies = [pltpu.make_async_copy(a, b, sems.at[i]) for i, (a, b) in enumerate(pairs)]
    for copy in copies:
        copy.start()
    copies[0].wait()
    turned[...] = late[...].T
    z, y = lax.axis_index("z"), lax.axis_index("y")
    for j in range(NY):

        @pl.when(y == j)
        def _():
            for i, far in enumerate(offsets(NZ)):
                start = pl.multiple_of((z + far + NZ) % NZ * ZROWS, ZROWS)
                block = turned[pl.ds(start, ZROWS), :]
                for k, off in enumerate(offsets(NY)):
                    at = (j + off) % NY * ROWS
                    by_z[i, k] = block[at : at + ROWS]
                    for group, ref in zip(GROUPS, by_group):
                        if far in group:
                            ref[k, group.index(far)] = block[at : at + ROWS]

    pairs = zip((*by_group, by_z), by_group_hbm)
    writes = [pltpu.make_async_copy(a, b, sems.at[i + 3]) for i, (a, b) in enumerate(pairs)]
    for write in writes:
        write.start()
    copies[1].wait()
    copies[2].wait()
    total = jnp.zeros((1, D), F32)
    for i in range(0, tokens.shape[0], 64):
        sums = jnp.sum(grad[i : i + 64, :].astype(F32), axis=1, keepdims=True)
        total += jnp.sum(tokens[i : i + 64, :].astype(F32) * sums, axis=0, keepdims=True)
    slots[...] = jnp.zeros_like(slots)
    for i in range(NZ * NY):
        row = jnp.broadcast_to(total[:, i * ROWS : (i + 1) * ROWS], (NX * NC, ROWS))
        slots[i * NX * NC : (i + 1) * NX * NC, :ROWS] = row
    for write in writes:
        write.wait()


def side_work(tokens, grad_out, next_tokens):
    count = tokens.shape[0]
    shapes = [(NY, len(group), ROWS, count) for group in GROUPS] + [(NZ, NY, ROWS, count)]
    return pl.pallas_call(
        side_kernel,
        in_specs=[HBM] * 3,
        out_specs=[HBM] * len(shapes) + [VMEM],
        out_shape=[pltpu.HBM(s, BF16) for s in shapes] + [jax.ShapeDtypeStruct((FF // D * NZ * NY, 128), F32)],
        scratch_shapes=[pltpu.VMEM(s, BF16) for s in shapes]
        + [pltpu.VMEM((count, D), BF16)] * 3
        + [pltpu.VMEM((D, count), BF16), pltpu.SemaphoreType.DMA((3 + len(shapes),))],
        compiler_params=vmem_limit(24),
    )(tokens, grad_out, next_tokens)


def finish_kernel(first_hbm, up, down, second_hbm, near, past, far, slots_in, first, second, slots, *scratch):
    own, other, sems = scratch
    copies = [
        pltpu.make_async_copy(first_hbm.at[lax.axis_index("z")], own, sems.at[0]),
        pltpu.make_async_copy(second_hbm.at[lax.axis_index("y")], other, sems.at[1]),
    ]
    for copy in copies:
        copy.start()
    for copy in copies:
        copy.wait()
    first[...] = own[...] + up[...].astype(F32) + down[...].astype(F32)
    sent = near[...].astype(F32) + past[...].astype(F32) + far[...].astype(F32)
    second[...] = other[...] + sent
    squares = jnp.sum(first[...] * first[...], axis=(0, 1), keepdims=True)
    squares += jnp.sum(second[...] * second[...], axis=(0, 1), keepdims=True)
    lane = lax.broadcasted_iota(jnp.int32, slots.shape, 1)
    slots[...] = jnp.where(lane < ROWS, slots_in[...], squares)


def finish(first, up, down, second, sends, slots):
    shapes = first.shape[1:], second.shape[1:], slots.shape
    return pl.pallas_call(
        finish_kernel,
        in_specs=[HBM, VMEM, VMEM, HBM] + [VMEM] * 4,
        out_specs=[VMEM] * 3,
        out_shape=[jax.ShapeDtypeStruct(s, F32) for s in shapes],
        scratch_shapes=[pltpu.VMEM(s, F32) for s in shapes[:2]] + [pltpu.SemaphoreType.DMA((2,))],
        compiler_params=vmem_limit(12),
    )(in_hbm(first), up, down, in_hbm(second), *sends, slots)


def update_kernel(slots, first, second, master_hbm, momentum_hbm, *refs):
    new_master, new_momentum, one, two, checks, master, momentum, sems = refs
    copies = [
        pltpu.make_async_copy(master_hbm, master, sems.at[0]),
        pltpu.make_async_copy(momentum_hbm, momentum, sems.at[1]),
    ]
    for copy in copies:
        copy.start()
    lane = lax.broadcasted_iota(jnp.int32, slots.shape, 1)
    row = lax.broadcasted_iota(jnp.int32, slots.shape, 0)
    place = lax.axis_index("x") * NC + lax.axis_index("c")
    values = slots[...]
    squares = jnp.sum(jnp.where(lane == ROWS, values, 0.0), axis=(0, 1), keepdims=True)
    clip_factor = jnp.minimum(1.0, 1.0 / jnp.sqrt(squares / (D * FF) + 1e-06))
    row_sum = jnp.sum(jnp.where(row % (NX * NC) == place, values, 0.0), axis=0, keepdims=True)
    checks[...] = (clip_factor * row_sum / float(D) ** 0.5)[:, :ROWS]
    for copy in copies:
        copy.wait()
    for grad, start in ((first, 0), (second, HALF)):
        at = pl.ds(start, grad.shape[1])
        fresh = 0.9 * momentum[:, at] + clip_factor * grad[...]
        new_momentum[:, at] = fresh
        new_master[:, at] = master[:, at] - 0.01 * fresh
    one[...] = new_master[:, :WIDE].astype(BF16)
    two[...] = new_master[:, WIDE:].astype(BF16)


def update(slots, first, second, master, momentum):
    shapes = [(master.shape, F32)] * 2 + [((ROWS, WIDE), BF16), ((ROWS, D - WIDE), BF16), ((1, ROWS), F32)]
    return pl.pallas_call(
        update_kernel,
        in_specs=[VMEM] * 3 + [HBM] * 2,
        out_specs=[VMEM] * 5,
        out_shape=[jax.ShapeDtypeStruct(*s) for s in shapes],
        scratch_shapes=[pltpu.VMEM(master.shape, F32)] * 2 + [pltpu.SemaphoreType.DMA((2,))],
        compiler_params=vmem_limit(16),
    )(slots, first, second, in_hbm(master), in_hbm(momentum))


def stack_kernel(groups, *refs):
    refs = list(refs)
    outs = refs[len(refs) - len(groups) :]
    for group, out in zip(groups, outs):
        at = 0
        for start, stop in group:
            out[at : at + stop - start, :] = refs.pop(0)[start:stop, :]
            at += stop - start


def stack(*groups):
    ranges = [[(start, stop) for _, start, stop in group] for group in groups]
    blocks = [block for group in groups for block, _, _ in group]
    rows = [sum(stop - start for start, stop in group) for group in ranges]
    return pl.pallas_call(
        functools.partial(stack_kernel, ranges),
        in_specs=[VMEM] * len(blocks),
        out_specs=[VMEM] * len(groups),
        out_shape=[
            jax.ShapeDtypeStruct((count, group[0][0].shape[1]), BF16) for count, group in zip(rows, groups)
        ],
        compiler_params=vmem_limit(16),
    )(*blocks)


def whole(*blocks):
    return [(block, 0, block.shape[0]) for block in blocks]


def chunk_of(chunks, axis):
    size = SIZES[axis]
    me = lax.axis_index(axis)
    return lambda k: lax.dynamic_index_in_dim(chunks, (me + k) % size, 0, keepdims=False).astype(F32)


def scatter_rounds(chunks, axis, up, down, ready, come):
    up, down = lax.optimization_barrier((up, down))
    for k in range(SIZES[axis] // 2 - 1, 0, -1):
        up, down = ready(k, *ring_add(chunks, axis, k, up, down))
        up, down = come(k, shift(up, axis, 1), shift(down, axis, -1))
    return up, down


def jump(value):
    return lax.ppermute(value, "z", [(i, (i + 2 - i % 2 * 4) % NZ) for i in range(NZ)])


def short_ring(chunk, far, up, down):
    far, even = far.astype(F32), lax.axis_index("z") % 2 == 0
    up = chunk(2) + up.astype(F32) + jnp.where(even, far, 0.0)
    down = chunk(-2) + down.astype(F32) + jnp.where(even, 0.0, far)
    up, down = shift(up.astype(BF16), "z", 1), shift(down.astype(BF16), "z", -1)
    up, down = lax.optimization_barrier((up, down))
    up, down = chunk(1) + up.astype(F32), chunk(-1) + down.astype(F32)
    up, down = shift(up.astype(BF16), "z", 1), shift(down.astype(BF16), "z", -1)
    return lax.optimization_barrier((up, down))


def product(features, *blocks):
    return lax.dot_general(
        features.reshape(-1, features.shape[-1]), jnp.concatenate(blocks),
        (((0,), (0,)), ((), ())), preferred_element_type=F32,
    )


def together(k, *values):
    return lax.optimization_barrier(values)


def local(tokens, grad_out, next_tokens, master, momentum):
    far_tokens = in_hbm(tokens)
    far_grad = in_hbm(grad_out)
    up1, down1, up2, down2, turned = far_chunks(far_tokens, far_grad)
    up2, down2 = shift(up2, "z", 1), shift(down2, "z", -1)
    up1, down1 = shift(up1, "y", 1), shift(down1, "y", -1)
    by_y, by_z = all_chunks(turned, far_grad)

    by_y = in_hbm(by_y.reshape(NY, YROWS, HALF))
    by_z = in_hbm(by_z.reshape(NZ, ZROWS, D - HALF))

    aside, held = [], []

    def ready_first(k, up, down):
        return up, down

    def ready_second(k, up, down):
        if k == 2:
            up, down, *late = together(k, up, down, tokens, grad_out, next_tokens)
            aside.extend(side_work(*map(in_hbm, late)))
        elif k == 1:
            held[:] = together(k, *held, up, down)[:3]
        return up, down

    def come_second(k, up, down):
        if k == 2:
            up, down, *aside[:] = together(k, up, down, *aside)
            return up, down
        return together(k, up, down)

    first = scatter_rounds(by_y, "y", up1, down1, ready_first, together)
    first, held[:] = ring_total(by_y, "y", *first, "z", (4, 3, -3))
    second = scatter_rounds(by_z, "z", up2, down2, ready_second, come_second)
    second, sends = ring_total(by_z, "z", *second, "y", (1, -1, 2))
    held = [jump(held[0]), shift(held[1], "z", 1), shift(held[2], "z", -1)]
    *held, _ = together(0, *held, sends[0])
    up, down = short_ring(chunk_of(first, "z"), *held)
    sends = together(0, *(shift(send, "y", k) for send, k in zip(sends, (1, -1, 2))))
    *by_y, by_z, slots = aside

    first, second, slots = finish(first, up, down, second, sends, slots)
    slots = lax.all_to_all(slots, ("z", "y", "x", "c"), split_axis=0, concat_axis=0, tiled=True)
    new_master, new_momentum, one, two, row_checks = update(slots, first, second, master, momentum)

    up1, down1, *twos = together(
        1, shift(one, "z", 1), shift(one, "z", -1), shift(two, "y", 1), shift(two, "y", -1), shift(two, "y", 2)
    )
    groups = [stack(whole(one, up1, down1))[0]]
    up3, down3 = shift(groups[0], "y", 1), shift(groups[0], "y", -1)
    (two,) = stack(whole(two, *twos))
    up1, down1, two = together(2, shift(up1, "z", 1), shift(down1, "z", -1), two)
    ones = [up1, down1]

    up1 = shift(up1, "z", 1)
    up2, down2 = shift(two, "z", 1), shift(two, "z", -1)
    up3, down3 = together(1, up3, down3)
    sides = [(up3, down3)]
    group, up3, down3 = stack(
        whole(*ones), [*whole(*ones), (up3, 0, CUTS[0])], [*whole(*ones), (down3, CUTS[0], 3 * ROWS)]
    )
    groups.append(group)
    up3, down3 = shift(up3, "y", 1), shift(down3, "y", -1)
    up2, down2, down1 = together(1, up2, down2, down1)
    arrived = [(up2, down2)]
    ones = [up1, shift(down1, "z", -1), shift(up1, "z", 1)]
    up2, down2 = together(2, shift(up2, "z", 1), shift(down2, "z", -1))
    arrived.append((up2, down2))
    up3, down3 = together(2, up3, down3)
    sides.append((up3, down3))
    group, up3, down3 = stack(
        whole(*ones), [*whole(*ones), (up3, 0, CUTS[1])], [*whole(*ones), (down3, CUTS[1], 2 * ROWS)]
    )
    groups.append(group)
    up3, down3 = shift(up3, "y", 1), shift(down3, "y", -1)
    up2, down2 = together(3, shift(up2, "z", 1), shift(down2, "z", -1))
    arrived.append((up2, down2))
    up3, down3 = together(3, up3, down3)
    sides.append((up3, down3))
    ends2 = stack([(up2, 0, ZROWS // 2)], [(down2, ZROWS // 2, ZROWS)])
    far2 = shift(ends2[0], "z", 1), shift(ends2[1], "z", -1)
    ends3 = stack([(up3, 0, CUTS[2])], [(down3, CUTS[2], 3 * ROWS)])
    far3 = shift(ends3[0], "y", 1), shift(ends3[1], "y", -1)

    out_two = product(by_z[0], two)
    for k, blocks in enumerate(arrived):
        out_two += product(by_z[2 * k + 1 : 2 * k + 3], *blocks)
    out_two += product(by_z[NZ - 1], *far2)
    out_one = 0.0
    for i, (features, group) in enumerate(zip(by_y, groups)):
        out_one += product(features[0], group)
        count = group.shape[0]
        up3, down3 = sides[i]
        pair = [(up3, 0, count), (down3, 0, count)]
        if i == 0:
            (pair,) = stack(pair)
        else:
            pair, far = stack(pair, [(up3, count, up3.shape[0]), (down3, count, down3.shape[0])])
            out_one += product(by_y[i - 1][3], far)
        out_one += product(features[1:3], pair)
    out_one += product(by_y[-1][3], *far3)
    forward = jnp.concatenate([out_one, out_two], axis=1).astype(BF16)
    return new_master, new_momentum, forward, row_checks


def solution(mesh):
    split = Mesh(mesh.devices.reshape(NZ, NY, NX, NC), ("z", "y", "x", "c"))
    dp, mp = ("z", "y"), ("x", "c")
    in_specs = (P(dp, None), P(dp, mp), P(dp, None), P(dp, mp), P(dp, mp))
    out_specs = (P(dp, mp), P(dp, mp), P(dp, mp), P(mp, dp))
    return jax.shard_map(local, mesh=split, in_specs=in_specs, out_specs=out_specs, check_vma=False)
```

```python
import functools

import jax
import jax.numpy as jnp
from jax import lax
from jax.experimental import pallas as pl
from jax.experimental.pallas import tpu as pltpu
from jax.sharding import Mesh, PartitionSpec as P

D = 2304
FF = 18432
NZ, NY, NX, NC = 8, 4, 4, 2
SIZES = {"z": NZ, "y": NY, "x": NX, "c": NC}
ROWS = D // (NZ * NY)
YROWS, ZROWS = NZ * ROWS, NY * ROWS
HALF = 1152
WIDE = 1280
NEAR = 5
CUT = 192
F32, BF16 = jnp.float32, jnp.bfloat16
HBM = pl.BlockSpec(memory_space=pltpu.HBM)
VMEM = pl.BlockSpec(memory_space=pltpu.VMEM)


def vmem_limit(mib):
    return pltpu.CompilerParams(vmem_limit_bytes=mib * 1024 * 1024)


def in_hbm(value):
    return pltpu.with_memory_space_constraint(value, pltpu.HBM)


def shift(value, axis, by):
    size = SIZES[axis]
    return lax.ppermute(value, axis, [(i, (i + by) % size) for i in range(size)])


def far_kernel(tokens_hbm, grad_hbm, up_y, down_y, up_z, down_z, turned, tokens, grad, sems):
    first = pltpu.make_async_copy(tokens_hbm, tokens, sems.at[0])
    second = pltpu.make_async_copy(grad_hbm, grad, sems.at[1])
    first.start()
    second.start()
    first.wait()
    turned[...] = tokens[...].T
    second.wait()
    z = (lax.axis_index("z") + NZ // 2) % NZ
    y = (lax.axis_index("y") + NY // 2) % NY
    rows = turned[pl.ds(pl.multiple_of(z * ZROWS, ZROWS), ZROWS), :]
    part = jnp.dot(rows, grad[:, HALF:], preferred_element_type=F32).astype(BF16)
    up_z[...] = part[: ZROWS // 2]
    down_z[...] = part[ZROWS // 2 :]
    for j in range(NY):

        @pl.when(y == j)
        def _():
            starts = [i * ZROWS + j * ROWS for i in range(NZ)]
            rows = jnp.concatenate([turned[s : s + ROWS, :] for s in starts])
            part = jnp.dot(rows, grad[:, :HALF], preferred_element_type=F32).astype(BF16)
            up_y[...] = part[: YROWS // 2]
            down_y[...] = part[YROWS // 2 :]


def far_chunks(tokens, grad_out):
    count = tokens.shape[0]
    shapes = [(YROWS // 2, HALF)] * 2 + [(ZROWS // 2, D - HALF)] * 2 + [(D, count)]
    return pl.pallas_call(
        far_kernel,
        in_specs=[HBM, HBM],
        out_specs=[VMEM] * 5,
        out_shape=[jax.ShapeDtypeStruct(s, BF16) for s in shapes],
        scratch_shapes=[
            pltpu.VMEM(tokens.shape, BF16),
            pltpu.VMEM(grad_out.shape, BF16),
            pltpu.SemaphoreType.DMA((2,)),
        ],
        compiler_params=vmem_limit(24),
    )(tokens, grad_out)


def grad_kernel(turned, grad_hbm, by_y_hbm, by_z_hbm, grad, by_y, by_z, sem, sems):
    whole = pltpu.make_async_copy(grad_hbm, grad, sem)
    whole.start()
    whole.wait()
    step = 2 * ZROWS
    writes = []
    for i in range(NZ // 2):
        part = jnp.dot(turned[i * step : (i + 1) * step, :], grad[...], preferred_element_type=F32)
        part = part.astype(BF16).reshape(2, NY, ROWS, D)
        for k in range(2):
            for j in range(NY):
                by_y[j, 2 * i + k] = part[k, j, :, :HALF]
                by_z[2 * i + k, j] = part[k, j, :, HALF:]
        pair = pl.ds(2 * i, 2)
        writes.append(pltpu.make_async_copy(by_z.at[pair], by_z_hbm.at[pair], sems.at[0, i]))
        writes[-1].start()
        writes.append(pltpu.make_async_copy(by_y.at[:, pair], by_y_hbm.at[:, pair], sems.at[1, i]))
        writes[-1].start()
    for write in writes:
        write.wait()


def all_chunks(turned, grad_out):
    shapes = (NY, NZ, ROWS, HALF), (NZ, NY, ROWS, D - HALF)
    return pl.pallas_call(
        grad_kernel,
        in_specs=[VMEM, HBM],
        out_specs=[HBM, HBM],
        out_shape=[pltpu.HBM(s, BF16) for s in shapes],
        scratch_shapes=[pltpu.VMEM(s, BF16) for s in (grad_out.shape, *shapes)]
        + [pltpu.SemaphoreType.DMA, pltpu.SemaphoreType.DMA((2, NZ // 2))],
        compiler_params=vmem_limit(32),
    )(turned, grad_out)


def add_kernel(axis, k, chunks, up, down, up_out, down_out, above, below, sems):
    size, me = SIZES[axis], lax.axis_index(axis)
    first = pltpu.make_async_copy(chunks.at[(me + k) % size], above, sems.at[0])
    second = pltpu.make_async_copy(chunks.at[(me - k + size) % size], below, sems.at[1])
    first.start()
    second.start()
    rows, half = above.shape[0], up.shape[0]
    first.wait()
    up_out[:half] = above[:half] + up[...]
    if half < rows:
        up_out[half:] = above[half:]
    second.wait()
    rest = rows - down.shape[0]
    if rest:
        down_out[:rest] = below[:rest]
    down_out[rest:] = below[rest:] + down[...]


def ring_add(chunks, axis, k, up, down):
    shape = chunks.shape[1:]
    return pl.pallas_call(
        functools.partial(add_kernel, axis, k),
        in_specs=[HBM, VMEM, VMEM],
        out_specs=[VMEM, VMEM],
        out_shape=[jax.ShapeDtypeStruct(shape, BF16)] * 2,
        scratch_shapes=[pltpu.VMEM(shape, BF16)] * 2 + [pltpu.SemaphoreType.DMA((2,))],
        compiler_params=vmem_limit(16),
    )(chunks, up, down)


def total_kernel(axis, other, places, chunks, up, down, out, *refs):
    sends, (own, total, sem) = refs[: len(places)], refs[len(places) :]
    copy = pltpu.make_async_copy(chunks.at[lax.axis_index(axis)], own, sem)
    copy.start()
    copy.wait()
    total[...] = own[...].astype(F32) + up[...].astype(F32) + down[...].astype(F32)
    copy = pltpu.make_async_copy(total, out, sem)
    copy.start()
    for send, k in zip(sends, places):
        start = (lax.axis_index(other) + k + SIZES[other]) % SIZES[other] * ROWS
        send[...] = total[pl.ds(pl.multiple_of(start, ROWS), ROWS), :].astype(BF16)
    copy.wait()


def ring_total(chunks, axis, up, down, other, places):
    shape = chunks.shape[1:]
    total, *sends = pl.pallas_call(
        functools.partial(total_kernel, axis, other, places),
        in_specs=[HBM, VMEM, VMEM],
        out_specs=[HBM] + [VMEM] * len(places),
        out_shape=[pltpu.HBM(shape, F32)] + [jax.ShapeDtypeStruct((ROWS, shape[1]), BF16)] * len(places),
        scratch_shapes=[pltpu.VMEM(shape, BF16), pltpu.VMEM(shape, F32), pltpu.SemaphoreType.DMA],
        compiler_params=vmem_limit(16),
    )(chunks, up, down)
    return total.reshape(SIZES[other], ROWS, shape[1]), sends


def offsets(size):
    order = [0]
    for k in range(1, size // 2):
        order += [-k, k]
    return order + [size // 2]


def side_kernel(tokens_hbm, grad_hbm, next_hbm, near_hbm, rest_hbm, by_z_hbm, slots, *scratch):
    near, rest, by_z, tokens, grad, late, turned, sems = scratch
    pairs = (next_hbm, late), (grad_hbm, grad), (tokens_hbm, tokens)
    copies = [pltpu.make_async_copy(a, b, sems.at[i]) for i, (a, b) in enumerate(pairs)]
    for copy in copies:
        copy.start()
    copies[0].wait()
    turned[...] = late[...].T
    z, y = lax.axis_index("z"), lax.axis_index("y")
    for j in range(NY):

        @pl.when(y == j)
        def _():
            for i, far in enumerate(offsets(NZ)):
                start = pl.multiple_of((z + far + NZ) % NZ * ZROWS, ZROWS)
                block = turned[pl.ds(start, ZROWS), :]
                for k, off in enumerate(offsets(NY)):
                    at = (j + off) % NY * ROWS
                    by_z[i, k] = block[at : at + ROWS]
                    if i < NEAR:
                        near[k, i] = block[at : at + ROWS]
                    else:
                        rest[k, i - NEAR] = block[at : at + ROWS]

    pairs = (near, near_hbm), (rest, rest_hbm), (by_z, by_z_hbm)
    writes = [pltpu.make_async_copy(a, b, sems.at[i + 3]) for i, (a, b) in enumerate(pairs)]
    for write in writes:
        write.start()
    copies[1].wait()
    copies[2].wait()
    total = jnp.zeros((1, D), F32)
    for i in range(0, tokens.shape[0], 64):
        sums = jnp.sum(grad[i : i + 64, :].astype(F32), axis=1, keepdims=True)
        total += jnp.sum(tokens[i : i + 64, :].astype(F32) * sums, axis=0, keepdims=True)
    slots[...] = jnp.zeros_like(slots)
    for i in range(NZ * NY):
        row = jnp.broadcast_to(total[:, i * ROWS : (i + 1) * ROWS], (NX * NC, ROWS))
        slots[i * NX * NC : (i + 1) * NX * NC, :ROWS] = row
    for write in writes:
        write.wait()


def side_work(tokens, grad_out, next_tokens):
    count = tokens.shape[0]
    shapes = (NY, NEAR, ROWS, count), (NY, NZ - NEAR, ROWS, count), (NZ, NY, ROWS, count)
    return pl.pallas_call(
        side_kernel,
        in_specs=[HBM] * 3,
        out_specs=[HBM] * 3 + [VMEM],
        out_shape=[pltpu.HBM(s, BF16) for s in shapes] + [jax.ShapeDtypeStruct((FF // D * NZ * NY, 128), F32)],
        scratch_shapes=[pltpu.VMEM(s, BF16) for s in shapes]
        + [pltpu.VMEM((count, D), BF16)] * 3
        + [pltpu.VMEM((D, count), BF16), pltpu.SemaphoreType.DMA((6,))],
        compiler_params=vmem_limit(24),
    )(tokens, grad_out, next_tokens)


def finish_kernel(first_hbm, up, down, second_hbm, near, past, far, slots_in, first, second, slots, *scratch):
    own, other, sems = scratch
    copies = [
        pltpu.make_async_copy(first_hbm.at[lax.axis_index("z")], own, sems.at[0]),
        pltpu.make_async_copy(second_hbm.at[lax.axis_index("y")], other, sems.at[1]),
    ]
    for copy in copies:
        copy.start()
    for copy in copies:
        copy.wait()
    first[...] = own[...] + up[...].astype(F32) + down[...].astype(F32)
    sent = near[...].astype(F32) + past[...].astype(F32) + far[...].astype(F32)
    second[...] = other[...] + sent
    squares = jnp.sum(first[...] * first[...], axis=(0, 1), keepdims=True)
    squares += jnp.sum(second[...] * second[...], axis=(0, 1), keepdims=True)
    lane = lax.broadcasted_iota(jnp.int32, slots.shape, 1)
    slots[...] = jnp.where(lane < ROWS, slots_in[...], squares)


def finish(first, up, down, second, sends, slots):
    shapes = first.shape[1:], second.shape[1:], slots.shape
    return pl.pallas_call(
        finish_kernel,
        in_specs=[HBM, VMEM, VMEM, HBM] + [VMEM] * 4,
        out_specs=[VMEM] * 3,
        out_shape=[jax.ShapeDtypeStruct(s, F32) for s in shapes],
        scratch_shapes=[pltpu.VMEM(s, F32) for s in shapes[:2]] + [pltpu.SemaphoreType.DMA((2,))],
        compiler_params=vmem_limit(12),
    )(in_hbm(first), up, down, in_hbm(second), *sends, slots)


def update_kernel(slots, first, second, master_hbm, momentum_hbm, *refs):
    new_master, new_momentum, one, two, checks, master, momentum, sems = refs
    copies = [
        pltpu.make_async_copy(master_hbm, master, sems.at[0]),
        pltpu.make_async_copy(momentum_hbm, momentum, sems.at[1]),
    ]
    for copy in copies:
        copy.start()
    lane = lax.broadcasted_iota(jnp.int32, slots.shape, 1)
    row = lax.broadcasted_iota(jnp.int32, slots.shape, 0)
    place = lax.axis_index("x") * NC + lax.axis_index("c")
    values = slots[...]
    squares = jnp.sum(jnp.where(lane == ROWS, values, 0.0), axis=(0, 1), keepdims=True)
    clip_factor = jnp.minimum(1.0, 1.0 / jnp.sqrt(squares / (D * FF) + 1e-06))
    row_sum = jnp.sum(jnp.where(row % (NX * NC) == place, values, 0.0), axis=0, keepdims=True)
    checks[...] = (clip_factor * row_sum / float(D) ** 0.5)[:, :ROWS]
    for copy in copies:
        copy.wait()
    for grad, start in ((first, 0), (second, HALF)):
        at = pl.ds(start, grad.shape[1])
        fresh = 0.9 * momentum[:, at] + clip_factor * grad[...]
        new_momentum[:, at] = fresh
        new_master[:, at] = master[:, at] - 0.01 * fresh
    one[...] = new_master[:, :WIDE].astype(BF16)
    two[...] = new_master[:, WIDE:].astype(BF16)


def update(slots, first, second, master, momentum):
    shapes = [(master.shape, F32)] * 2 + [((ROWS, WIDE), BF16), ((ROWS, D - WIDE), BF16), ((1, ROWS), F32)]
    return pl.pallas_call(
        update_kernel,
        in_specs=[VMEM] * 3 + [HBM] * 2,
        out_specs=[VMEM] * 5,
        out_shape=[jax.ShapeDtypeStruct(*s) for s in shapes],
        scratch_shapes=[pltpu.VMEM(master.shape, F32)] * 2 + [pltpu.SemaphoreType.DMA((2,))],
        compiler_params=vmem_limit(16),
    )(slots, first, second, in_hbm(master), in_hbm(momentum))


def stack_kernel(groups, *refs):
    refs = list(refs)
    outs = refs[len(refs) - len(groups) :]
    for group, out in zip(groups, outs):
        at = 0
        for start, stop in group:
            out[at : at + stop - start, :] = refs.pop(0)[start:stop, :]
            at += stop - start


def stack(*groups):
    ranges = [[(start, stop) for _, start, stop in group] for group in groups]
    blocks = [block for group in groups for block, _, _ in group]
    rows = [sum(stop - start for start, stop in group) for group in ranges]
    return pl.pallas_call(
        functools.partial(stack_kernel, ranges),
        in_specs=[VMEM] * len(blocks),
        out_specs=[VMEM] * len(groups),
        out_shape=[
            jax.ShapeDtypeStruct((count, group[0][0].shape[1]), BF16) for count, group in zip(rows, groups)
        ],
        compiler_params=vmem_limit(16),
    )(*blocks)


def whole(*blocks):
    return [(block, 0, block.shape[0]) for block in blocks]


def chunk_of(chunks, axis):
    size = SIZES[axis]
    me = lax.axis_index(axis)
    return lambda k: lax.dynamic_index_in_dim(chunks, (me + k) % size, 0, keepdims=False).astype(F32)


def scatter_rounds(chunks, axis, up, down, ready, come):
    up, down = lax.optimization_barrier((up, down))
    for k in range(SIZES[axis] // 2 - 1, 0, -1):
        up, down = ready(k, *ring_add(chunks, axis, k, up, down))
        up, down = come(k, shift(up, axis, 1), shift(down, axis, -1))
    return up, down


def jump(value):
    return lax.ppermute(value, "z", [(i, (i + 2 - i % 2 * 4) % NZ) for i in range(NZ)])


def short_ring(chunk, far, up, down):
    far, even = far.astype(F32), lax.axis_index("z") % 2 == 0
    up = chunk(2) + up.astype(F32) + jnp.where(even, far, 0.0)
    down = chunk(-2) + down.astype(F32) + jnp.where(even, 0.0, far)
    up, down = shift(up.astype(BF16), "z", 1), shift(down.astype(BF16), "z", -1)
    up, down = lax.optimization_barrier((up, down))
    up, down = chunk(1) + up.astype(F32), chunk(-1) + down.astype(F32)
    up, down = shift(up.astype(BF16), "z", 1), shift(down.astype(BF16), "z", -1)
    return lax.optimization_barrier((up, down))


def product(features, *blocks):
    return lax.dot_general(
        features.reshape(-1, features.shape[-1]), jnp.concatenate(blocks),
        (((0,), (0,)), ((), ())), preferred_element_type=F32,
    )


def together(k, *values):
    return lax.optimization_barrier(values)


def local(tokens, grad_out, next_tokens, master, momentum):
    far_tokens = in_hbm(tokens)
    far_grad = in_hbm(grad_out)
    up1, down1, up2, down2, turned = far_chunks(far_tokens, far_grad)
    up2, down2 = shift(up2, "z", 1), shift(down2, "z", -1)
    up1, down1 = shift(up1, "y", 1), shift(down1, "y", -1)
    by_y, by_z = all_chunks(turned, far_grad)

    by_y = in_hbm(by_y.reshape(NY, YROWS, HALF))
    by_z = in_hbm(by_z.reshape(NZ, ZROWS, D - HALF))

    aside, held = [], []

    def ready_first(k, up, down):
        return up, down

    def ready_second(k, up, down):
        if k == 2:
            up, down, *late = together(k, up, down, tokens, grad_out, next_tokens)
            aside.extend(side_work(*map(in_hbm, late)))
        elif k == 1:
            held[:] = together(k, *held, up, down)[:3]
        return up, down

    def come_second(k, up, down):
        if k == 2:
            up, down, *aside[:] = together(k, up, down, *aside)
            return up, down
        return together(k, up, down)

    first = scatter_rounds(by_y, "y", up1, down1, ready_first, together)
    first, held[:] = ring_total(by_y, "y", *first, "z", (4, 3, -3))
    second = scatter_rounds(by_z, "z", up2, down2, ready_second, come_second)
    second, sends = ring_total(by_z, "z", *second, "y", (1, -1, 2))
    held = [jump(held[0]), shift(held[1], "z", 1), shift(held[2], "z", -1)]
    *held, _ = together(0, *held, sends[0])
    up, down = short_ring(chunk_of(first, "z"), *held)
    sends = together(0, *(shift(send, "y", k) for send, k in zip(sends, (1, -1, 2))))
    near, rest, by_z, slots = aside

    first, second, slots = finish(first, up, down, second, sends, slots)
    slots = lax.all_to_all(slots, ("z", "y", "x", "c"), split_axis=0, concat_axis=0, tiled=True)
    new_master, new_momentum, one, two, row_checks = update(slots, first, second, master, momentum)

    *ones, up1, down1, near2, past2, far2 = together(
        1,
        *(shift(one, "z", k) for k in (1, -1, 2, -2)),
        *(shift(two, "y", k) for k in (1, -1, 2)),
    )
    ones = [one, *ones]
    (two,) = stack(whole(two, near2, past2, far2))
    (one_near,) = stack(whole(*ones, up1, down1))

    up1 = shift(up1, "z", 1)
    up3, down3 = shift(one_near, "y", 1), shift(one_near, "y", -1)
    up2, down2 = shift(two, "z", 1), shift(two, "z", -1)
    up2, down2, down1 = together(1, up2, down2, down1)
    arrived = [(up2, down2)]
    ones = [up1, shift(down1, "z", -1), shift(up1, "z", 1)]
    up2, down2 = together(2, shift(up2, "z", 1), shift(down2, "z", -1))
    arrived.append((up2, down2))
    up3, down3 = together(1, up3, down3)
    count = NEAR * ROWS
    one_rest, up4, down4 = stack(
        whole(*ones), [*whole(*ones), (up3, 0, CUT)], [*whole(*ones), (down3, CUT, count)]
    )
    up4, down4 = shift(up4, "y", 1), shift(down4, "y", -1)
    up2, down2 = shift(up2, "z", 1), shift(down2, "z", -1)
    up2, down2, up4, down4 = together(3, up2, down2, up4, down4)
    arrived.append((up2, down2))
    count = (NZ - NEAR) * ROWS
    cut = count // 16 * 8
    ends2 = stack([(up2, 0, ZROWS // 2)], [(down2, ZROWS // 2, ZROWS)])
    up4, down4, *ends2 = together(4, up4, down4, *ends2)
    ends4 = stack([(up4, 0, cut)], [(down4, cut, count)])
    far2 = shift(ends2[0], "z", 1), shift(ends2[1], "z", -1)
    far4 = shift(ends4[0], "y", 1), shift(ends4[1], "y", -1)
    sides4, far3 = stack(
        [(up4, 0, count), (down4, 0, count)],
        [(up4, count, up4.shape[0]), (down4, count, down4.shape[0])],
    )
    out_two = product(by_z[0], two)
    for k, blocks in enumerate(arrived):
        out_two += product(by_z[2 * k + 1 : 2 * k + 3], *blocks)
    out_two += product(by_z[NZ - 1], *far2)
    out_one = product(near[0], one_near) + product(rest[0], one_rest)
    out_one += product(near[1:3], up3, down3)
    out_one += product(near[3], far3)
    out_one += product(rest[1:3], sides4)
    out_one += product(rest[3], *far4)
    forward = jnp.concatenate([out_one, out_two], axis=1).astype(BF16)
    return new_master, new_momentum, forward, row_checks


def solution(mesh):
    split = Mesh(mesh.devices.reshape(NZ, NY, NX, NC), ("z", "y", "x", "c"))
    dp, mp = ("z", "y"), ("x", "c")
    in_specs = (P(dp, None), P(dp, mp), P(dp, None), P(dp, mp), P(dp, mp))
    out_specs = (P(dp, mp), P(dp, mp), P(dp, mp), P(mp, dp))
    return jax.shard_map(local, mesh=split, in_specs=in_specs, out_specs=out_specs, check_vma=False)
```

```python
import functools

import jax
import jax.numpy as jnp
from jax import lax
from jax.experimental import pallas as pl
from jax.experimental.pallas import tpu as pltpu
from jax.sharding import Mesh, PartitionSpec as P

D = 2304
FF = 18432
NZ, NY, NX, NC = 8, 4, 4, 2
SIZES = {"z": NZ, "y": NY, "x": NX, "c": NC}
ROWS = D // (NZ * NY)
YROWS, ZROWS = NZ * ROWS, NY * ROWS
HALF = 1152
WIDE = 1152
NEAR = 5
CUT = 192
F32, BF16 = jnp.float32, jnp.bfloat16
HBM = pl.BlockSpec(memory_space=pltpu.HBM)
VMEM = pl.BlockSpec(memory_space=pltpu.VMEM)


def vmem_limit(mib):
    return pltpu.CompilerParams(vmem_limit_bytes=mib * 1024 * 1024)


def in_hbm(value):
    return pltpu.with_memory_space_constraint(value, pltpu.HBM)


def shift(value, axis, by):
    size = SIZES[axis]
    return lax.ppermute(value, axis, [(i, (i + by) % size) for i in range(size)])


def far_kernel(tokens_hbm, grad_hbm, up_y, down_y, up_z, down_z, turned, tokens, grad, sems):
    first = pltpu.make_async_copy(tokens_hbm, tokens, sems.at[0])
    second = pltpu.make_async_copy(grad_hbm, grad, sems.at[1])
    first.start()
    second.start()
    first.wait()
    turned[...] = tokens[...].T
    second.wait()
    z = (lax.axis_index("z") + NZ // 2) % NZ
    y = (lax.axis_index("y") + NY // 2) % NY
    rows = turned[pl.ds(pl.multiple_of(z * ZROWS, ZROWS), ZROWS), :]
    part = jnp.dot(rows, grad[:, HALF:], preferred_element_type=F32).astype(BF16)
    up_z[...] = part[: ZROWS // 2]
    down_z[...] = part[ZROWS // 2 :]
    for j in range(NY):

        @pl.when(y == j)
        def _():
            starts = [i * ZROWS + j * ROWS for i in range(NZ)]
            rows = jnp.concatenate([turned[s : s + ROWS, :] for s in starts])
            part = jnp.dot(rows, grad[:, :HALF], preferred_element_type=F32).astype(BF16)
            up_y[...] = part[: YROWS // 2]
            down_y[...] = part[YROWS // 2 :]


def far_chunks(tokens, grad_out):
    count = tokens.shape[0]
    shapes = [(YROWS // 2, HALF)] * 2 + [(ZROWS // 2, D - HALF)] * 2 + [(D, count)]
    return pl.pallas_call(
        far_kernel,
        in_specs=[HBM, HBM],
        out_specs=[VMEM] * 5,
        out_shape=[jax.ShapeDtypeStruct(s, BF16) for s in shapes],
        scratch_shapes=[
            pltpu.VMEM(tokens.shape, BF16),
            pltpu.VMEM(grad_out.shape, BF16),
            pltpu.SemaphoreType.DMA((2,)),
        ],
        compiler_params=vmem_limit(24),
    )(tokens, grad_out)


def grad_kernel(start, turned, grad_hbm, out_hbm, grad, out, sem, sems):
    columns = pl.ds(start, grad.shape[1])
    whole = pltpu.make_async_copy(grad_hbm.at[:, columns], grad, sem)
    whole.start()
    whole.wait()
    step = 2 * ZROWS
    writes = []
    for i in range(NZ // 2):
        part = jnp.dot(turned[i * step : (i + 1) * step, :], grad[...], preferred_element_type=F32)
        part = part.astype(BF16).reshape(2, NY, ROWS, grad.shape[1])
        if start:
            pair = (pl.ds(2 * i, 2),)
            out[2 * i : 2 * i + 2] = part
        else:
            pair = (slice(None), pl.ds(2 * i, 2))
            for k in range(2):
                for j in range(NY):
                    out[j, 2 * i + k] = part[k, j]
        writes.append(pltpu.make_async_copy(out.at[pair], out_hbm.at[pair], sems.at[i]))
        writes[-1].start()
    for write in writes:
        write.wait()


def all_chunks(turned, grad_out, shape, start):
    return pl.pallas_call(
        functools.partial(grad_kernel, start),
        in_specs=[VMEM, HBM],
        out_specs=HBM,
        out_shape=pltpu.HBM(shape, BF16),
        scratch_shapes=[
            pltpu.VMEM((grad_out.shape[0], shape[-1]), BF16),
            pltpu.VMEM(shape, BF16),
            pltpu.SemaphoreType.DMA,
            pltpu.SemaphoreType.DMA((NZ // 2,)),
        ],
        compiler_params=vmem_limit(24),
    )(turned, grad_out)


def add_kernel(axis, k, chunks, up, down, up_out, down_out, above, below, sems):
    size, me = SIZES[axis], lax.axis_index(axis)
    first = pltpu.make_async_copy(chunks.at[(me + k) % size], above, sems.at[0])
    second = pltpu.make_async_copy(chunks.at[(me - k + size) % size], below, sems.at[1])
    first.start()
    second.start()
    rows, half = above.shape[0], up.shape[0]
    first.wait()
    up_out[:half] = above[:half] + up[...]
    if half < rows:
        up_out[half:] = above[half:]
    second.wait()
    rest = rows - down.shape[0]
    if rest:
        down_out[:rest] = below[:rest]
    down_out[rest:] = below[rest:] + down[...]


def ring_add(chunks, axis, k, up, down):
    shape = chunks.shape[1:]
    return pl.pallas_call(
        functools.partial(add_kernel, axis, k),
        in_specs=[HBM, VMEM, VMEM],
        out_specs=[VMEM, VMEM],
        out_shape=[jax.ShapeDtypeStruct(shape, BF16)] * 2,
        scratch_shapes=[pltpu.VMEM(shape, BF16)] * 2 + [pltpu.SemaphoreType.DMA((2,))],
        compiler_params=vmem_limit(16),
    )(chunks, up, down)


def total_kernel(axis, other, places, chunks, up, down, out, *refs):
    sends, (own, total, sem) = refs[: len(places)], refs[len(places) :]
    copy = pltpu.make_async_copy(chunks.at[lax.axis_index(axis)], own, sem)
    copy.start()
    copy.wait()
    total[...] = own[...].astype(F32) + up[...].astype(F32) + down[...].astype(F32)
    copy = pltpu.make_async_copy(total, out, sem)
    copy.start()
    for send, k in zip(sends, places):
        start = (lax.axis_index(other) + k + SIZES[other]) % SIZES[other] * ROWS
        send[...] = total[pl.ds(pl.multiple_of(start, ROWS), ROWS), :].astype(BF16)
    copy.wait()


def ring_total(chunks, axis, up, down, other, places):
    shape = chunks.shape[1:]
    total, *sends = pl.pallas_call(
        functools.partial(total_kernel, axis, other, places),
        in_specs=[HBM, VMEM, VMEM],
        out_specs=[HBM] + [VMEM] * len(places),
        out_shape=[pltpu.HBM(shape, F32)] + [jax.ShapeDtypeStruct((ROWS, shape[1]), BF16)] * len(places),
        scratch_shapes=[pltpu.VMEM(shape, BF16), pltpu.VMEM(shape, F32), pltpu.SemaphoreType.DMA],
        compiler_params=vmem_limit(16),
    )(chunks, up, down)
    return total.reshape(SIZES[other], ROWS, shape[1]), sends


def offsets(size):
    order = [0]
    for k in range(1, size // 2):
        order += [-k, k]
    return order + [size // 2]


def side_kernel(tokens_hbm, grad_hbm, next_hbm, near_hbm, rest_hbm, by_z_hbm, slots, *scratch):
    near, rest, by_z, tokens, grad, late, turned, sems = scratch
    pairs = (next_hbm, late), (grad_hbm, grad), (tokens_hbm, tokens)
    copies = [pltpu.make_async_copy(a, b, sems.at[i]) for i, (a, b) in enumerate(pairs)]
    for copy in copies:
        copy.start()
    copies[0].wait()
    turned[...] = late[...].T
    z, y = lax.axis_index("z"), lax.axis_index("y")
    for j in range(NY):

        @pl.when(y == j)
        def _():
            for i, far in enumerate(offsets(NZ)):
                start = pl.multiple_of((z + far + NZ) % NZ * ZROWS, ZROWS)
                block = turned[pl.ds(start, ZROWS), :]
                for k, off in enumerate(offsets(NY)):
                    at = (j + off) % NY * ROWS
                    by_z[i, k] = block[at : at + ROWS]
                    if i < NEAR:
                        near[k, i] = block[at : at + ROWS]
                    else:
                        rest[k, i - NEAR] = block[at : at + ROWS]

    pairs = (near, near_hbm), (rest, rest_hbm), (by_z, by_z_hbm)
    writes = [pltpu.make_async_copy(a, b, sems.at[i + 3]) for i, (a, b) in enumerate(pairs)]
    for write in writes:
        write.start()
    copies[1].wait()
    copies[2].wait()
    total = jnp.zeros((1, D), F32)
    for i in range(0, tokens.shape[0], 64):
        sums = jnp.sum(grad[i : i + 64, :].astype(F32), axis=1, keepdims=True)
        total += jnp.sum(tokens[i : i + 64, :].astype(F32) * sums, axis=0, keepdims=True)
    slots[...] = jnp.zeros_like(slots)
    for i in range(NZ * NY):
        row = jnp.broadcast_to(total[:, i * ROWS : (i + 1) * ROWS], (NX * NC, ROWS))
        slots[i * NX * NC : (i + 1) * NX * NC, :ROWS] = row
    for write in writes:
        write.wait()


def side_work(tokens, grad_out, next_tokens):
    count = tokens.shape[0]
    shapes = (NY, NEAR, ROWS, count), (NY, NZ - NEAR, ROWS, count), (NZ, NY, ROWS, count)
    return pl.pallas_call(
        side_kernel,
        in_specs=[HBM] * 3,
        out_specs=[HBM] * 3 + [VMEM],
        out_shape=[pltpu.HBM(s, BF16) for s in shapes] + [jax.ShapeDtypeStruct((FF // D * NZ * NY, 128), F32)],
        scratch_shapes=[pltpu.VMEM(s, BF16) for s in shapes]
        + [pltpu.VMEM((count, D), BF16)] * 3
        + [pltpu.VMEM((D, count), BF16), pltpu.SemaphoreType.DMA((6,))],
        compiler_params=vmem_limit(24),
    )(tokens, grad_out, next_tokens)


def finish_kernel(first_hbm, up, down, second_hbm, near, past, far, slots_in, first, second, slots, *scratch):
    own, other, sems = scratch
    copies = [
        pltpu.make_async_copy(first_hbm.at[lax.axis_index("z")], own, sems.at[0]),
        pltpu.make_async_copy(second_hbm.at[lax.axis_index("y")], other, sems.at[1]),
    ]
    for copy in copies:
        copy.start()
    for copy in copies:
        copy.wait()
    first[...] = own[...] + up[...].astype(F32) + down[...].astype(F32)
    sent = near[...].astype(F32) + past[...].astype(F32) + far[...].astype(F32)
    second[...] = other[...] + sent
    squares = jnp.sum(first[...] * first[...], axis=(0, 1), keepdims=True)
    squares += jnp.sum(second[...] * second[...], axis=(0, 1), keepdims=True)
    lane = lax.broadcasted_iota(jnp.int32, slots.shape, 1)
    slots[...] = jnp.where(lane < ROWS, slots_in[...], squares)


def finish(first, up, down, second, sends, slots):
    shapes = first.shape[1:], second.shape[1:], slots.shape
    return pl.pallas_call(
        finish_kernel,
        in_specs=[HBM, VMEM, VMEM, HBM] + [VMEM] * 4,
        out_specs=[VMEM] * 3,
        out_shape=[jax.ShapeDtypeStruct(s, F32) for s in shapes],
        scratch_shapes=[pltpu.VMEM(s, F32) for s in shapes[:2]] + [pltpu.SemaphoreType.DMA((2,))],
        compiler_params=vmem_limit(12),
    )(in_hbm(first), up, down, in_hbm(second), *sends, slots)


def update_kernel(slots, first, second, master_hbm, momentum_hbm, *refs):
    new_master, new_momentum, one, two, checks, master, momentum, sems = refs
    copies = [
        pltpu.make_async_copy(master_hbm, master, sems.at[0]),
        pltpu.make_async_copy(momentum_hbm, momentum, sems.at[1]),
    ]
    for copy in copies:
        copy.start()
    lane = lax.broadcasted_iota(jnp.int32, slots.shape, 1)
    row = lax.broadcasted_iota(jnp.int32, slots.shape, 0)
    place = lax.axis_index("x") * NC + lax.axis_index("c")
    values = slots[...]
    squares = jnp.sum(jnp.where(lane == ROWS, values, 0.0), axis=(0, 1), keepdims=True)
    clip_factor = jnp.minimum(1.0, 1.0 / jnp.sqrt(squares / (D * FF) + 1e-06))
    row_sum = jnp.sum(jnp.where(row % (NX * NC) == place, values, 0.0), axis=0, keepdims=True)
    checks[...] = (clip_factor * row_sum / float(D) ** 0.5)[:, :ROWS]
    for copy in copies:
        copy.wait()
    for grad, start in ((first, 0), (second, HALF)):
        at = pl.ds(start, grad.shape[1])
        fresh = 0.9 * momentum[:, at] + clip_factor * grad[...]
        new_momentum[:, at] = fresh
        new_master[:, at] = master[:, at] - 0.01 * fresh
    one[...] = new_master[:, :WIDE].astype(BF16)
    two[...] = new_master[:, WIDE:].astype(BF16)


def update(slots, first, second, master, momentum):
    shapes = [(master.shape, F32)] * 2 + [((ROWS, WIDE), BF16), ((ROWS, D - WIDE), BF16), ((1, ROWS), F32)]
    return pl.pallas_call(
        update_kernel,
        in_specs=[VMEM] * 3 + [HBM] * 2,
        out_specs=[VMEM] * 5,
        out_shape=[jax.ShapeDtypeStruct(*s) for s in shapes],
        scratch_shapes=[pltpu.VMEM(master.shape, F32)] * 2 + [pltpu.SemaphoreType.DMA((2,))],
        compiler_params=vmem_limit(16),
    )(slots, first, second, in_hbm(master), in_hbm(momentum))


def stack_kernel(groups, *refs):
    refs = list(refs)
    outs = refs[len(refs) - len(groups) :]
    for group, out in zip(groups, outs):
        at = 0
        for start, stop in group:
            out[at : at + stop - start, :] = refs.pop(0)[start:stop, :]
            at += stop - start


def stack(*groups):
    ranges = [[(start, stop) for _, start, stop in group] for group in groups]
    blocks = [block for group in groups for block, _, _ in group]
    rows = [sum(stop - start for start, stop in group) for group in ranges]
    return pl.pallas_call(
        functools.partial(stack_kernel, ranges),
        in_specs=[VMEM] * len(blocks),
        out_specs=[VMEM] * len(groups),
        out_shape=[
            jax.ShapeDtypeStruct((count, group[0][0].shape[1]), BF16) for count, group in zip(rows, groups)
        ],
        compiler_params=vmem_limit(16),
    )(*blocks)


def whole(*blocks):
    return [(block, 0, block.shape[0]) for block in blocks]


def scatter_rounds(chunks, axis, up, down, ready, come):
    up, down = lax.optimization_barrier((up, down))
    for k in range(SIZES[axis] // 2 - 1, 0, -1):
        up, down = ready(k, *ring_add(chunks, axis, k, up, down))
        up, down = come(k, shift(up, axis, 1), shift(down, axis, -1))
    return up, down


def jump(value):
    return lax.ppermute(value, "z", [(i, (i + 2 - i % 2 * 4) % NZ) for i in range(NZ)])


def short_kernel(k, chunks, *refs):
    *sent, up_out, down_out, above, below, sems = refs
    me = lax.axis_index("z")
    copies = [
        pltpu.make_async_copy(chunks.at[(me + k) % NZ], above, sems.at[0]),
        pltpu.make_async_copy(chunks.at[(me - k + NZ) % NZ], below, sems.at[1]),
    ]
    for copy in copies:
        copy.start()
    for copy in copies:
        copy.wait()
    sent = [ref[...].astype(F32) for ref in sent]
    up, down = above[...] + sent[0], below[...] + sent[1]
    if len(sent) == 3:
        even = (me % 2 == 0).astype(F32)
        up, down = up + sent[2] * even, down + sent[2] * (1.0 - even)
    up_out[...] = up.astype(BF16)
    down_out[...] = down.astype(BF16)


def short_add(chunks, k, *sent):
    shape = chunks.shape[1:]
    return pl.pallas_call(
        functools.partial(short_kernel, k),
        in_specs=[HBM] + [VMEM] * len(sent),
        out_specs=[VMEM] * 2,
        out_shape=[jax.ShapeDtypeStruct(shape, BF16)] * 2,
        scratch_shapes=[pltpu.VMEM(shape, F32)] * 2 + [pltpu.SemaphoreType.DMA((2,))],
        compiler_params=vmem_limit(8),
    )(in_hbm(chunks), *sent)


def short_ring(chunks, far, up, down):
    sent = up, down, far
    for k in (2, 1):
        up, down = short_add(chunks, k, *sent)
        sent = lax.optimization_barrier((shift(up, "z", 1), shift(down, "z", -1)))
    return sent


def product(features, *blocks):
    return lax.dot_general(
        features.reshape(-1, features.shape[-1]), jnp.concatenate(blocks),
        (((0,), (0,)), ((), ())), preferred_element_type=F32,
    )


def last_kernel(one_hbm, two, features, up, down, out, one, last, sems):
    copy = pltpu.make_async_copy(one_hbm, one, sems.at[0])
    copy.start()
    copy.wait()
    copy = pltpu.make_async_copy(one, out.at[:, pl.ds(0, WIDE)], sems.at[1])
    copy.start()
    half = up.shape[0]
    dims = (((0,), (0,)), ((), ()))
    part = lax.dot_general(features[:half], up[...], dims, preferred_element_type=F32)
    part += lax.dot_general(features[half:], down[...], dims, preferred_element_type=F32)
    last[...] = (two[...] + part).astype(BF16)
    end = pltpu.make_async_copy(last, out.at[:, pl.ds(WIDE, D - WIDE)], sems.at[0])
    end.start()
    copy.wait()
    end.wait()


def last_product(one, two, features, up, down):
    count = one.shape[0]
    return pl.pallas_call(
        last_kernel,
        in_specs=[HBM] + [VMEM] * 4,
        out_specs=HBM,
        out_shape=pltpu.HBM((count, D), BF16),
        scratch_shapes=[
            pltpu.VMEM((count, WIDE), BF16),
            pltpu.VMEM((count, D - WIDE), BF16),
            pltpu.SemaphoreType.DMA((2,)),
        ],
        compiler_params=vmem_limit(16),
    )(one, two, features.reshape(-1, count), up, down)


def together(k, *values):
    return lax.optimization_barrier(values)


def local(tokens, grad_out, next_tokens, master, momentum):
    far_tokens = in_hbm(tokens)
    far_grad = in_hbm(grad_out)
    up1, down1, up2, down2, turned = far_chunks(far_tokens, far_grad)
    up2, down2 = shift(up2, "z", 1), shift(down2, "z", -1)
    up1, down1 = shift(up1, "y", 1), shift(down1, "y", -1)
    by_z = all_chunks(turned, far_grad, (NZ, NY, ROWS, D - HALF), HALF)
    by_y = all_chunks(turned, far_grad, (NY, NZ, ROWS, HALF), 0)

    by_y = in_hbm(by_y.reshape(NY, YROWS, HALF))
    by_z = in_hbm(by_z.reshape(NZ, ZROWS, D - HALF))

    aside, held = [], []

    def ready_first(k, up, down):
        return up, down

    def ready_second(k, up, down):
        if k == 2:
            up, down, *late = together(k, up, down, tokens, grad_out, next_tokens)
            aside.extend(side_work(*map(in_hbm, late)))
        elif k == 1:
            held[:] = together(k, *held, up, down)[:3]
        return up, down

    def come_second(k, up, down):
        if k == 2:
            up, down, *aside[:] = together(k, up, down, *aside)
            return up, down
        return together(k, up, down)

    first = scatter_rounds(by_y, "y", up1, down1, ready_first, together)
    first, held[:] = ring_total(by_y, "y", *first, "z", (4, 3, -3))
    second = scatter_rounds(by_z, "z", up2, down2, ready_second, come_second)
    second, sends = ring_total(by_z, "z", *second, "y", (1, -1, 2))
    held = [jump(held[0]), shift(held[1], "z", 1), shift(held[2], "z", -1)]
    *held, _ = together(0, *held, sends[0])
    up, down = short_ring(first, *held)
    sends = together(0, *(shift(send, "y", k) for send, k in zip(sends, (1, -1, 2))))
    near, rest, by_z, slots = aside

    first, second, slots = finish(first, up, down, second, sends, slots)
    slots = lax.all_to_all(slots, ("z", "y", "x", "c"), split_axis=0, concat_axis=0, tiled=True)
    new_master, new_momentum, one, two, row_checks = update(slots, first, second, master, momentum)

    up1, down1, *twos = together(
        1, shift(one, "z", 1), shift(one, "z", -1), shift(two, "y", 1), shift(two, "y", -1), shift(two, "y", 2)
    )
    ones = [one, up1, down1]
    (two,) = stack(whole(two, *twos))
    up1, down1, two = together(2, shift(up1, "z", 1), shift(down1, "z", -1), two)
    (one_near,) = stack(whole(*ones, up1, down1))

    up1 = shift(up1, "z", 1)
    up3, down3 = shift(one_near, "y", 1), shift(one_near, "y", -1)
    up2, down2 = shift(two, "z", 1), shift(two, "z", -1)
    up2, down2, down1 = together(1, up2, down2, down1)
    arrived = [(up2, down2)]
    ones = [up1, shift(down1, "z", -1), shift(up1, "z", 1)]
    up2, down2 = together(2, shift(up2, "z", 1), shift(down2, "z", -1))
    arrived.append((up2, down2))
    up3, down3 = together(1, up3, down3)
    count = NEAR * ROWS
    one_rest, up4, down4 = stack(
        whole(*ones), [*whole(*ones), (up3, 0, CUT)], [*whole(*ones), (down3, CUT, count)]
    )
    up4, down4 = shift(up4, "y", 1), shift(down4, "y", -1)
    up2, down2 = shift(up2, "z", 1), shift(down2, "z", -1)
    up2, down2, up4, down4 = together(3, up2, down2, up4, down4)
    arrived.append((up2, down2))
    count = (NZ - NEAR) * ROWS
    cut = count // 16 * 8
    ends2 = stack([(up2, 0, ZROWS // 2)], [(down2, ZROWS // 2, ZROWS)])
    up4, down4, *ends2 = together(4, up4, down4, *ends2)
    ends4 = stack([(up4, 0, cut)], [(down4, cut, count)])
    far2 = shift(ends2[0], "z", 1), shift(ends2[1], "z", -1)
    far4 = shift(ends4[0], "y", 1), shift(ends4[1], "y", -1)
    sides4, far3 = stack(
        [(up4, 0, count), (down4, 0, count)],
        [(up4, count, up4.shape[0]), (down4, count, down4.shape[0])],
    )
    out_two = product(by_z[0], two)
    for k, blocks in enumerate(arrived):
        out_two += product(by_z[2 * k + 1 : 2 * k + 3], *blocks)
    out_one = product(near[0], one_near) + product(rest[0], one_rest)
    out_one += product(near[1:3], up3, down3)
    out_one += product(near[3], far3)
    out_one += product(rest[1:3], sides4)
    out_one += product(rest[3], *far4)
    forward = last_product(out_one.astype(BF16), out_two, by_z[NZ - 1], *far2)
    return new_master, new_momentum, forward, row_checks


def solution(mesh):
    split = Mesh(mesh.devices.reshape(NZ, NY, NX, NC), ("z", "y", "x", "c"))
    dp, mp = ("z", "y"), ("x", "c")
    in_specs = (P(dp, None), P(dp, mp), P(dp, None), P(dp, mp), P(dp, mp))
    out_specs = (P(dp, mp), P(dp, mp), P(dp, mp), P(mp, dp))
    return jax.shard_map(local, mesh=split, in_specs=in_specs, out_specs=out_specs, check_vma=False)
```

```python
import functools

import jax
import jax.numpy as jnp
from jax import lax
from jax.experimental import pallas as pl
from jax.experimental.pallas import tpu as pltpu
from jax.sharding import Mesh, PartitionSpec as P

D = 2304
FF = 18432
NZ, NY, NX, NC = 8, 4, 4, 2
SIZES = {"z": NZ, "y": NY, "x": NX, "c": NC}
ROWS = D // (NZ * NY)
YROWS, ZROWS = NZ * ROWS, NY * ROWS
HALF = 1152
WIDE = 1152
NEAR = 5
CUT = 192
F32, BF16 = jnp.float32, jnp.bfloat16
HBM = pl.BlockSpec(memory_space=pltpu.HBM)
VMEM = pl.BlockSpec(memory_space=pltpu.VMEM)


def vmem_limit(mib):
    return pltpu.CompilerParams(vmem_limit_bytes=mib * 1024 * 1024)


def in_hbm(value):
    return pltpu.with_memory_space_constraint(value, pltpu.HBM)


def shift(value, axis, by):
    size = SIZES[axis]
    return lax.ppermute(value, axis, [(i, (i + by) % size) for i in range(size)])


def far_kernel(tokens_hbm, grad_hbm, up_y, down_y, up_z, down_z, turned, tokens, grad, sems):
    first = pltpu.make_async_copy(tokens_hbm, tokens, sems.at[0])
    second = pltpu.make_async_copy(grad_hbm, grad, sems.at[1])
    first.start()
    second.start()
    first.wait()
    turned[...] = tokens[...].T
    second.wait()
    z = (lax.axis_index("z") + NZ // 2) % NZ
    y = (lax.axis_index("y") + NY // 2) % NY
    rows = turned[pl.ds(pl.multiple_of(z * ZROWS, ZROWS), ZROWS), :]
    part = jnp.dot(rows, grad[:, HALF:], preferred_element_type=F32).astype(BF16)
    up_z[...] = part[: ZROWS // 2]
    down_z[...] = part[ZROWS // 2 :]
    for j in range(NY):

        @pl.when(y == j)
        def _():
            starts = [i * ZROWS + j * ROWS for i in range(NZ)]
            rows = jnp.concatenate([turned[s : s + ROWS, :] for s in starts])
            part = jnp.dot(rows, grad[:, :HALF], preferred_element_type=F32).astype(BF16)
            up_y[...] = part[: YROWS // 2]
            down_y[...] = part[YROWS // 2 :]


def far_chunks(tokens, grad_out):
    count = tokens.shape[0]
    shapes = [(YROWS // 2, HALF)] * 2 + [(ZROWS // 2, D - HALF)] * 2 + [(D, count)]
    return pl.pallas_call(
        far_kernel,
        in_specs=[HBM, HBM],
        out_specs=[VMEM] * 5,
        out_shape=[jax.ShapeDtypeStruct(s, BF16) for s in shapes],
        scratch_shapes=[
            pltpu.VMEM(tokens.shape, BF16),
            pltpu.VMEM(grad_out.shape, BF16),
            pltpu.SemaphoreType.DMA((2,)),
        ],
        compiler_params=vmem_limit(24),
    )(tokens, grad_out)


def grad_kernel(start, turned, grad_hbm, out_hbm, grad, out, sem, sems):
    columns = pl.ds(start, grad.shape[1])
    whole = pltpu.make_async_copy(grad_hbm.at[:, columns], grad, sem)
    whole.start()
    whole.wait()
    step = 2 * ZROWS
    writes = []
    for i in range(NZ // 2):
        part = jnp.dot(turned[i * step : (i + 1) * step, :], grad[...], preferred_element_type=F32)
        part = part.astype(BF16).reshape(2, NY, ROWS, grad.shape[1])
        if start:
            pair = (pl.ds(2 * i, 2),)
            out[2 * i : 2 * i + 2] = part
        else:
            pair = (slice(None), pl.ds(2 * i, 2))
            for k in range(2):
                for j in range(NY):
                    out[j, 2 * i + k] = part[k, j]
        writes.append(pltpu.make_async_copy(out.at[pair], out_hbm.at[pair], sems.at[i]))
        writes[-1].start()
    for write in writes:
        write.wait()


def all_chunks(turned, grad_out, shape, start):
    return pl.pallas_call(
        functools.partial(grad_kernel, start),
        in_specs=[VMEM, HBM],
        out_specs=HBM,
        out_shape=pltpu.HBM(shape, BF16),
        scratch_shapes=[
            pltpu.VMEM((grad_out.shape[0], shape[-1]), BF16),
            pltpu.VMEM(shape, BF16),
            pltpu.SemaphoreType.DMA,
            pltpu.SemaphoreType.DMA((NZ // 2,)),
        ],
        compiler_params=vmem_limit(24),
    )(turned, grad_out)


def add_kernel(axis, k, chunks, up, down, up_out, down_out, above, below, sems):
    size, me = SIZES[axis], lax.axis_index(axis)
    first = pltpu.make_async_copy(chunks.at[(me + k) % size], above, sems.at[0])
    second = pltpu.make_async_copy(chunks.at[(me - k + size) % size], below, sems.at[1])
    first.start()
    second.start()
    rows, half = above.shape[0], up.shape[0]
    first.wait()
    up_out[:half] = above[:half] + up[...]
    if half < rows:
        up_out[half:] = above[half:]
    second.wait()
    rest = rows - down.shape[0]
    if rest:
        down_out[:rest] = below[:rest]
    down_out[rest:] = below[rest:] + down[...]


def ring_add(chunks, axis, k, up, down):
    shape = chunks.shape[1:]
    return pl.pallas_call(
        functools.partial(add_kernel, axis, k),
        in_specs=[HBM, VMEM, VMEM],
        out_specs=[VMEM, VMEM],
        out_shape=[jax.ShapeDtypeStruct(shape, BF16)] * 2,
        scratch_shapes=[pltpu.VMEM(shape, BF16)] * 2 + [pltpu.SemaphoreType.DMA((2,))],
        compiler_params=vmem_limit(16),
    )(chunks, up, down)


def total_kernel(axis, other, places, chunks, up, down, out, *refs):
    sends, (own, total, sem) = refs[: len(places)], refs[len(places) :]
    copy = pltpu.make_async_copy(chunks.at[lax.axis_index(axis)], own, sem)
    copy.start()
    copy.wait()
    total[...] = own[...].astype(F32) + up[...].astype(F32) + down[...].astype(F32)
    copy = pltpu.make_async_copy(total, out, sem)
    copy.start()
    for send, k in zip(sends, places):
        start = (lax.axis_index(other) + k + SIZES[other]) % SIZES[other] * ROWS
        send[...] = total[pl.ds(pl.multiple_of(start, ROWS), ROWS), :].astype(BF16)
    copy.wait()


def ring_total(chunks, axis, up, down, other, places):
    shape = chunks.shape[1:]
    total, *sends = pl.pallas_call(
        functools.partial(total_kernel, axis, other, places),
        in_specs=[HBM, VMEM, VMEM],
        out_specs=[HBM] + [VMEM] * len(places),
        out_shape=[pltpu.HBM(shape, F32)] + [jax.ShapeDtypeStruct((ROWS, shape[1]), BF16)] * len(places),
        scratch_shapes=[pltpu.VMEM(shape, BF16), pltpu.VMEM(shape, F32), pltpu.SemaphoreType.DMA],
        compiler_params=vmem_limit(16),
    )(chunks, up, down)
    return total.reshape(SIZES[other], ROWS, shape[1]), sends


def offsets(size):
    order = [0]
    for k in range(1, size // 2):
        order += [-k, k]
    return order + [size // 2]


def side_kernel(tokens_hbm, grad_hbm, next_hbm, near_hbm, rest_hbm, by_z_hbm, slots, *scratch):
    near, rest, by_z, tokens, grad, late, turned, sems = scratch
    pairs = (next_hbm, late), (grad_hbm, grad), (tokens_hbm, tokens)
    copies = [pltpu.make_async_copy(a, b, sems.at[i]) for i, (a, b) in enumerate(pairs)]
    for copy in copies:
        copy.start()
    copies[0].wait()
    turned[...] = late[...].T
    z, y = lax.axis_index("z"), lax.axis_index("y")
    for j in range(NY):

        @pl.when(y == j)
        def _():
            for i, far in enumerate(offsets(NZ)):
                start = pl.multiple_of((z + far + NZ) % NZ * ZROWS, ZROWS)
                block = turned[pl.ds(start, ZROWS), :]
                for k, off in enumerate(offsets(NY)):
                    at = (j + off) % NY * ROWS
                    by_z[i, k] = block[at : at + ROWS]
                    if i < NEAR:
                        near[k, i] = block[at : at + ROWS]
                    else:
                        rest[k, i - NEAR] = block[at : at + ROWS]

    pairs = (near, near_hbm), (rest, rest_hbm), (by_z, by_z_hbm)
    writes = [pltpu.make_async_copy(a, b, sems.at[i + 3]) for i, (a, b) in enumerate(pairs)]
    for write in writes:
        write.start()
    copies[1].wait()
    copies[2].wait()
    total = jnp.zeros((1, D), F32)
    for i in range(0, tokens.shape[0], 64):
        sums = jnp.sum(grad[i : i + 64, :].astype(F32), axis=1, keepdims=True)
        total += jnp.sum(tokens[i : i + 64, :].astype(F32) * sums, axis=0, keepdims=True)
    slots[...] = jnp.zeros_like(slots)
    for i in range(NZ * NY):
        row = jnp.broadcast_to(total[:, i * ROWS : (i + 1) * ROWS], (NX * NC, ROWS))
        slots[i * NX * NC : (i + 1) * NX * NC, :ROWS] = row
    for write in writes:
        write.wait()


def side_work(tokens, grad_out, next_tokens):
    count = tokens.shape[0]
    shapes = (NY, NEAR, ROWS, count), (NY, NZ - NEAR, ROWS, count), (NZ, NY, ROWS, count)
    return pl.pallas_call(
        side_kernel,
        in_specs=[HBM] * 3,
        out_specs=[HBM] * 3 + [VMEM],
        out_shape=[pltpu.HBM(s, BF16) for s in shapes] + [jax.ShapeDtypeStruct((FF // D * NZ * NY, 128), F32)],
        scratch_shapes=[pltpu.VMEM(s, BF16) for s in shapes]
        + [pltpu.VMEM((count, D), BF16)] * 3
        + [pltpu.VMEM((D, count), BF16), pltpu.SemaphoreType.DMA((6,))],
        compiler_params=vmem_limit(24),
    )(tokens, grad_out, next_tokens)


def finish_kernel(first_hbm, up, down, second_hbm, near, past, far, slots_in, first, second, slots, *scratch):
    own, other, sems = scratch
    copies = [
        pltpu.make_async_copy(first_hbm.at[lax.axis_index("z")], own, sems.at[0]),
        pltpu.make_async_copy(second_hbm.at[lax.axis_index("y")], other, sems.at[1]),
    ]
    for copy in copies:
        copy.start()
    for copy in copies:
        copy.wait()
    first[...] = own[...] + up[...].astype(F32) + down[...].astype(F32)
    sent = near[...].astype(F32) + past[...].astype(F32) + far[...].astype(F32)
    second[...] = other[...] + sent
    squares = jnp.sum(first[...] * first[...], axis=(0, 1), keepdims=True)
    squares += jnp.sum(second[...] * second[...], axis=(0, 1), keepdims=True)
    lane = lax.broadcasted_iota(jnp.int32, slots.shape, 1)
    slots[...] = jnp.where(lane < ROWS, slots_in[...], squares)


def finish(first, up, down, second, sends, slots):
    shapes = first.shape[1:], second.shape[1:], slots.shape
    return pl.pallas_call(
        finish_kernel,
        in_specs=[HBM, VMEM, VMEM, HBM] + [VMEM] * 4,
        out_specs=[VMEM] * 3,
        out_shape=[jax.ShapeDtypeStruct(s, F32) for s in shapes],
        scratch_shapes=[pltpu.VMEM(s, F32) for s in shapes[:2]] + [pltpu.SemaphoreType.DMA((2,))],
        compiler_params=vmem_limit(12),
    )(in_hbm(first), up, down, in_hbm(second), *sends, slots)


def update_kernel(slots, first, second, master_hbm, momentum_hbm, *refs):
    new_master, new_momentum, one, two, checks, master, momentum, sems = refs
    copies = [
        pltpu.make_async_copy(master_hbm, master, sems.at[0]),
        pltpu.make_async_copy(momentum_hbm, momentum, sems.at[1]),
    ]
    for copy in copies:
        copy.start()
    lane = lax.broadcasted_iota(jnp.int32, slots.shape, 1)
    row = lax.broadcasted_iota(jnp.int32, slots.shape, 0)
    place = lax.axis_index("x") * NC + lax.axis_index("c")
    values = slots[...]
    squares = jnp.sum(jnp.where(lane == ROWS, values, 0.0), axis=(0, 1), keepdims=True)
    clip_factor = jnp.minimum(1.0, 1.0 / jnp.sqrt(squares / (D * FF) + 1e-06))
    row_sum = jnp.sum(jnp.where(row % (NX * NC) == place, values, 0.0), axis=0, keepdims=True)
    checks[...] = (clip_factor * row_sum / float(D) ** 0.5)[:, :ROWS]
    for copy in copies:
        copy.wait()
    for grad, start in ((first, 0), (second, HALF)):
        at = pl.ds(start, grad.shape[1])
        fresh = 0.9 * momentum[:, at] + clip_factor * grad[...]
        new_momentum[:, at] = fresh
        new_master[:, at] = master[:, at] - 0.01 * fresh
    one[...] = new_master[:, :WIDE].astype(BF16)
    two[...] = new_master[:, WIDE:].astype(BF16)


def update(slots, first, second, master, momentum):
    shapes = [(master.shape, F32)] * 2 + [((ROWS, WIDE), BF16), ((ROWS, D - WIDE), BF16), ((1, ROWS), F32)]
    return pl.pallas_call(
        update_kernel,
        in_specs=[VMEM] * 3 + [HBM] * 2,
        out_specs=[VMEM] * 5,
        out_shape=[jax.ShapeDtypeStruct(*s) for s in shapes],
        scratch_shapes=[pltpu.VMEM(master.shape, F32)] * 2 + [pltpu.SemaphoreType.DMA((2,))],
        compiler_params=vmem_limit(16),
    )(slots, first, second, in_hbm(master), in_hbm(momentum))


def stack_kernel(groups, *refs):
    refs = list(refs)
    outs = refs[len(refs) - len(groups) :]
    for group, out in zip(groups, outs):
        at = 0
        for start, stop in group:
            out[at : at + stop - start, :] = refs.pop(0)[start:stop, :]
            at += stop - start


def stack(*groups):
    ranges = [[(start, stop) for _, start, stop in group] for group in groups]
    blocks = [block for group in groups for block, _, _ in group]
    rows = [sum(stop - start for start, stop in group) for group in ranges]
    return pl.pallas_call(
        functools.partial(stack_kernel, ranges),
        in_specs=[VMEM] * len(blocks),
        out_specs=[VMEM] * len(groups),
        out_shape=[
            jax.ShapeDtypeStruct((count, group[0][0].shape[1]), BF16) for count, group in zip(rows, groups)
        ],
        compiler_params=vmem_limit(16),
    )(*blocks)


def whole(*blocks):
    return [(block, 0, block.shape[0]) for block in blocks]


def scatter_rounds(chunks, axis, up, down, ready, come):
    up, down = lax.optimization_barrier((up, down))
    for k in range(SIZES[axis] // 2 - 1, 0, -1):
        up, down = ready(k, *ring_add(chunks, axis, k, up, down))
        up, down = come(k, shift(up, axis, 1), shift(down, axis, -1))
    return up, down


def jump(value):
    return lax.ppermute(value, "z", [(i, (i + 2 - i % 2 * 4) % NZ) for i in range(NZ)])


def short_kernel(k, chunks, *refs):
    *sent, up_out, down_out, above, below, sems = refs
    me = lax.axis_index("z")
    copies = [
        pltpu.make_async_copy(chunks.at[(me + k) % NZ], above, sems.at[0]),
        pltpu.make_async_copy(chunks.at[(me - k + NZ) % NZ], below, sems.at[1]),
    ]
    for copy in copies:
        copy.start()
    for copy in copies:
        copy.wait()
    sent = [ref[...].astype(F32) for ref in sent]
    up, down = above[...] + sent[0], below[...] + sent[1]
    if len(sent) == 3:
        even = (me % 2 == 0).astype(F32)
        up, down = up + sent[2] * even, down + sent[2] * (1.0 - even)
    up_out[...] = up.astype(BF16)
    down_out[...] = down.astype(BF16)


def short_add(chunks, k, *sent):
    shape = chunks.shape[1:]
    return pl.pallas_call(
        functools.partial(short_kernel, k),
        in_specs=[HBM] + [VMEM] * len(sent),
        out_specs=[VMEM] * 2,
        out_shape=[jax.ShapeDtypeStruct(shape, BF16)] * 2,
        scratch_shapes=[pltpu.VMEM(shape, F32)] * 2 + [pltpu.SemaphoreType.DMA((2,))],
        compiler_params=vmem_limit(8),
    )(in_hbm(chunks), *sent)


def short_ring(chunks, far, up, down):
    sent = up, down, far
    for k in (2, 1):
        up, down = short_add(chunks, k, *sent)
        sent = lax.optimization_barrier((shift(up, "z", 1), shift(down, "z", -1)))
    return sent


def product(features, *blocks):
    return lax.dot_general(
        features.reshape(-1, features.shape[-1]), jnp.concatenate(blocks),
        (((0,), (0,)), ((), ())), preferred_element_type=F32,
    )


def last_kernel(one_hbm, two, features, up, down, out, one, last, sems):
    copy = pltpu.make_async_copy(one_hbm, one, sems.at[0])
    copy.start()
    copy.wait()
    copy = pltpu.make_async_copy(one, out.at[:, pl.ds(0, WIDE)], sems.at[1])
    copy.start()
    half = up.shape[0]
    dims = (((0,), (0,)), ((), ()))
    part = lax.dot_general(features[:half], up[...], dims, preferred_element_type=F32)
    part += lax.dot_general(features[half:], down[...], dims, preferred_element_type=F32)
    last[...] = (two[...] + part).astype(BF16)
    end = pltpu.make_async_copy(last, out.at[:, pl.ds(WIDE, D - WIDE)], sems.at[0])
    end.start()
    copy.wait()
    end.wait()


def last_product(one, two, features, up, down):
    count = one.shape[0]
    return pl.pallas_call(
        last_kernel,
        in_specs=[HBM] + [VMEM] * 4,
        out_specs=HBM,
        out_shape=pltpu.HBM((count, D), BF16),
        scratch_shapes=[
            pltpu.VMEM((count, WIDE), BF16),
            pltpu.VMEM((count, D - WIDE), BF16),
            pltpu.SemaphoreType.DMA((2,)),
        ],
        compiler_params=vmem_limit(16),
    )(one, two, features.reshape(-1, count), up, down)


def together(k, *values):
    return lax.optimization_barrier(values)


def local(tokens, grad_out, next_tokens, master, momentum):
    far_tokens = in_hbm(tokens)
    far_grad = in_hbm(grad_out)
    up1, down1, up2, down2, turned = far_chunks(far_tokens, far_grad)
    up2, down2 = shift(up2, "z", 1), shift(down2, "z", -1)
    up1, down1 = shift(up1, "y", 1), shift(down1, "y", -1)
    by_z = all_chunks(turned, far_grad, (NZ, NY, ROWS, D - HALF), HALF)
    by_y = all_chunks(turned, far_grad, (NY, NZ, ROWS, HALF), 0)

    by_y = in_hbm(by_y.reshape(NY, YROWS, HALF))
    by_z = in_hbm(by_z.reshape(NZ, ZROWS, D - HALF))

    aside, held = [], []

    def ready_first(k, up, down):
        return up, down

    def ready_second(k, up, down):
        if k == 2:
            up, down, *late = together(k, up, down, tokens, grad_out, next_tokens)
            aside.extend(side_work(*map(in_hbm, late)))
        elif k == 1:
            held[:] = together(k, *held, up, down)[:3]
        return up, down

    def come_second(k, up, down):
        if k == 2:
            up, down, *aside[:] = together(k, up, down, *aside)
            return up, down
        return together(k, up, down)

    first = scatter_rounds(by_y, "y", up1, down1, ready_first, together)
    first, held[:] = ring_total(by_y, "y", *first, "z", (4, 3, -3))
    second = scatter_rounds(by_z, "z", up2, down2, ready_second, come_second)
    second, sends = ring_total(by_z, "z", *second, "y", (1, -1, 2))
    held = [jump(held[0]), shift(held[1], "z", 1), shift(held[2], "z", -1)]
    *held, _ = together(0, *held, sends[0])
    up, down = short_ring(first, *held)
    sends = together(0, *(shift(send, "y", k) for send, k in zip(sends, (1, -1, 2))))
    near, rest, by_z, slots = aside

    first, second, slots = finish(first, up, down, second, sends, slots)
    slots = lax.all_to_all(slots, ("z", "y", "x", "c"), split_axis=0, concat_axis=0, tiled=True)
    new_master, new_momentum, one, two, row_checks = update(slots, first, second, master, momentum)

    up1, down1, *twos = together(
        1, shift(one, "z", 1), shift(one, "z", -1), shift(two, "y", 1), shift(two, "y", -1), shift(two, "y", 2)
    )
    ones = [one, up1, down1]
    (two,) = stack(whole(two, *twos))
    up1, down1, two = together(2, shift(up1, "z", 1), shift(down1, "z", -1), two)
    (one_near,) = stack(whole(*ones, up1, down1))

    up1 = shift(up1, "z", 1)
    up3, down3 = shift(one_near, "y", 1), shift(one_near, "y", -1)
    up2, down2 = shift(two, "z", 1), shift(two, "z", -1)
    up2, down2, down1 = together(1, up2, down2, down1)
    arrived = [(up2, down2)]
    ones = [up1, shift(down1, "z", -1), shift(up1, "z", 1)]
    up2, down2 = together(2, shift(up2, "z", 1), shift(down2, "z", -1))
    arrived.append((up2, down2))
    up3, down3 = together(1, up3, down3)
    count = NEAR * ROWS
    one_rest, up4, down4 = stack(
        whole(*ones), [*whole(*ones), (up3, 0, CUT)], [*whole(*ones), (down3, CUT, count)]
    )
    up4, down4 = shift(up4, "y", 1), shift(down4, "y", -1)
    up2, down2 = shift(up2, "z", 1), shift(down2, "z", -1)
    up4, down4 = together(3, up4, down4)
    up2, down2 = together(3, up2, down2)
    arrived.append((up2, down2))
    count = (NZ - NEAR) * ROWS
    cut = count // 16 * 8
    ends2 = stack([(up2, 0, ZROWS // 2)], [(down2, ZROWS // 2, ZROWS)])
    ends4 = stack([(up4, 0, cut)], [(down4, cut, count)])
    far2 = shift(ends2[0], "z", 1), shift(ends2[1], "z", -1)
    far4 = shift(ends4[0], "y", 1), shift(ends4[1], "y", -1)
    sides4, far3 = stack(
        [(up4, 0, count), (down4, 0, count)],
        [(up4, count, up4.shape[0]), (down4, count, down4.shape[0])],
    )
    out_two = product(by_z[0], two)
    for k, blocks in enumerate(arrived):
        out_two += product(by_z[2 * k + 1 : 2 * k + 3], *blocks)
    out_one = product(near[0], one_near) + product(rest[0], one_rest)
    out_one += product(near[1:3], up3, down3)
    out_one += product(near[3], far3)
    out_one += product(rest[1:3], sides4)
    out_one += product(rest[3], *far4)
    forward = last_product(out_one.astype(BF16), out_two, by_z[NZ - 1], *far2)
    return new_master, new_momentum, forward, row_checks


def solution(mesh):
    split = Mesh(mesh.devices.reshape(NZ, NY, NX, NC), ("z", "y", "x", "c"))
    dp, mp = ("z", "y"), ("x", "c")
    in_specs = (P(dp, None), P(dp, mp), P(dp, None), P(dp, mp), P(dp, mp))
    out_specs = (P(dp, mp), P(dp, mp), P(dp, mp), P(mp, dp))
    return jax.shard_map(local, mesh=split, in_specs=in_specs, out_specs=out_specs, check_vma=False)
```
